128 devices in a mesh: ns: 8 (over y, core), ew: 16 (over z, x).
Axes of the slice: x: 4, y: 4, z: 4, core: 2. Of those that a mesh axis runs over, the one named last changes fastest.
Arguments:
- fields: bfloat16 [64, 64, 2048], P(None, 'ns', 'ew'), may hold values from -6 to 6
- w_in: bfloat16 [64, 192], replicated, may hold values from -0.75 to 0.75
- conv_first: bfloat16 [3, 3, 192, 192], replicated, may hold values from -0.15625 to 0.15625
- conv_second: bfloat16 [3, 3, 192, 192], replicated, may hold values from -0.15625 to 0.15625
- w_out: bfloat16 [192, 6], replicated, may hold values from -0.4375 to 0.4375
- slot_cells: int32 [128, 4, 16384], P(('ns', 'ew')), may hold values from 0 to 1023
- slot_weights: float32 [128, 4, 16384], P(('ns', 'ew')), may hold values from 0 to 1
- slot_count: int32 [128, 128], P(('ns', 'ew')), may hold values from 0 to 128, as said below
- recv_obs: int32 [128, 16384], P(('ns', 'ew')), may hold values from 0 to 2047
- targets: float32 [6, 262144], P(None, ('ns', 'ew')), may hold values from -6 to 6
Outputs:
- station_pred: float32 [6, 262144], P(None, ('ns', 'ew'))
- loss: float32 [], replicated
- grad_first: float32 [3, 3, 192, 192], replicated
- grad_second: float32 [3, 3, 192, 192], replicated
- grad_in: float32 [64, 192], replicated
- grad_out: float32 [192, 6], replicated
- grad_fields: float32 [64, 64, 2048], P(None, 'ns', 'ew')
The draws below stay inside these ranges and needn't reach their ends.
Inputs may be any that keep to these rules, and one draw needn't show every extreme that they name: `slot_cells`: local cell numbers of a tile, row-major. `slot_count`: every row has a column equal to 128.
All inputs are finite; a program needn't handle non-finite values.
Results may differ from the reference program's by a relative error of at most 0.008.
Values may be sent and summed in bfloat16 or wider, within the bound.
No kernel may reach another device: no remote copies, remote signals or barrier semaphores. Data moves between devices by JAX's collectives and lax.ppermute only.
A program may use at most 64 MiB of HBM per device.

```python
import jax
import jax.numpy as jnp
from jax import lax

C = 192
FIELDS = 64
VARS = 6
TH = 8
TW = 128
CAP = 128
OBS_DEV = 2048
NSG = 64
EWG = 2048
SLOTS = 16384
OBS = 262144
N_NS = 8
N_EW = 16
DEVICES = 128


def draw_slot_count(key, part):
    peer_count = DEVICES
    key_dense, key_base, key_full = jax.random.split(jax.random.fold_in(key, 7), 3)
    density = jax.random.randint(key_dense, (peer_count, 1), 1, 5)
    base = jax.random.randint(key_base, (peer_count, peer_count), 0, CAP + 1)
    counts = jnp.minimum(CAP, base * density // 2)
    column = jax.random.randint(key_full, (peer_count, 1), 0, peer_count)
    counts = jnp.where(jnp.arange(peer_count)[None, :] == column, CAP, counts)
    return counts.astype(jnp.int32)


def touch_ends(values, key, smallest, largest):
    extent = values.shape
    spot = [jax.random.randint(jax.random.fold_in(key, axis), (), 0, extent[axis]) for axis in range(len(extent))]
    values = values.at[tuple(spot)].set(smallest)
    longest = extent.index(max(extent))
    spot[longest] = (spot[longest] + 1) % extent[longest]
    return values.at[tuple(spot)].set(largest)


def block_levels(own_key, extent, cuts, low, high):
    def one(position, shards_of):
        steps = jax.random.uniform(jax.random.fold_in(jax.random.fold_in(own_key, 6), position), (shards_of,), jnp.float32, low / len(cuts), high / len(cuts))
        return jnp.repeat(jnp.exp(steps), extent[position] // shards_of).reshape((-1,) + (1,) * (len(extent) - position - 1))

    factor_of = one(*cuts[0])
    for cut in cuts[1:]:
        factor_of = factor_of * one(*cut)
    return factor_of


def gaussian(rng, shape, scale, bound, shards=(), dtype=jnp.bfloat16):
    level = block_levels(rng, shape, shards, -0.22, 0.18) if shards else 1.0
    result = jax.random.normal(rng, shape, jnp.float32) * scale * level
    return jnp.minimum(jnp.maximum(result, -bound), bound).astype(dtype)


def setup_inputs(seed: int = 0) -> dict:
    seeds = jax.random.split(jax.random.key(seed), 11)
    fields = gaussian(seeds[0], (FIELDS, NSG, EWG), 1.0, 6.0, ((1, 8), (2, 16)))
    w_in = gaussian(seeds[1], (FIELDS, C), FIELDS ** -0.5, 0.75)
    conv_first = gaussian(seeds[2], (3, 3, C, C), (9 * C) ** -0.5, 0.15625)
    conv_second = gaussian(seeds[3], (3, 3, C, C), (9 * C) ** -0.5, 0.15625)
    w_out = gaussian(seeds[4], (C, VARS), C ** -0.5, 0.4375)
    slot_cells = touch_ends(jax.random.randint(seeds[5], (DEVICES, 4, SLOTS), 0, TH * TW), jax.random.fold_in(seeds[5], 1), 0, (TH * TW) - 1).astype(jnp.int32)
    slot_weights = jnp.clip(1.0 * jax.random.uniform(seeds[6], (DEVICES, 4, SLOTS), jnp.float32) ** block_levels(seeds[6], (DEVICES, 4, SLOTS), ((0, 128),), -0.2, 0.2), 0.0, 1.0)
    slot_count = draw_slot_count(jax.random.fold_in(seeds[10], 71), 0)
    recv_obs = touch_ends(jax.random.randint(seeds[8], (DEVICES, SLOTS), 0, OBS_DEV), jax.random.fold_in(seeds[8], 1), 0, OBS_DEV - 1).astype(jnp.int32)
    targets = gaussian(seeds[9], (VARS, OBS), 1.0, 6.0, ((1, 128),), jnp.float32)
    return dict(fields=fields, w_in=w_in, conv_first=conv_first, conv_second=conv_second, w_out=w_out, slot_cells=slot_cells, slot_weights=slot_weights, slot_count=slot_count, recv_obs=recv_obs, targets=targets)


def pad_cells(grid):
    return jnp.pad(grid, ((0, 0), (1, 1), (1, 1)))

def conv_full(grid, kernel):
    height, breadth = (grid.shape[1], grid.shape[2])
    padded = pad_cells(grid).astype(jnp.float32)
    kernel_f = kernel.astype(jnp.float32)
    total = jnp.zeros((kernel.shape[3], height, breadth), jnp.float32)
    for row_off in range(3):
        for col_off in range(3):
            window = padded[:, row_off:row_off + height, col_off:col_off + breadth]
            total = total + jnp.einsum('co,chw->ohw', kernel_f[row_off, col_off], window)
    return total

def conv_back(grad, kernel):
    height, breadth = (grad.shape[1], grad.shape[2])
    padded = pad_cells(grad).astype(jnp.float32)
    kernel_f = kernel.astype(jnp.float32)
    total = jnp.zeros((kernel.shape[2], height, breadth), jnp.float32)
    for row_off in range(3):
        for col_off in range(3):
            window = padded[:, 2 - row_off:2 - row_off + height, 2 - col_off:2 - col_off + breadth]
            total = total + jnp.einsum('co,ohw->chw', kernel_f[row_off, col_off], window)
    return total

def kernel_grad(grid, grad):
    height, breadth = (grid.shape[1], grid.shape[2])
    padded = pad_cells(grid).astype(jnp.float32)
    grad_f = grad.astype(jnp.float32)
    taps = []
    for row_off in range(3):
        line = []
        for col_off in range(3):
            window = padded[:, row_off:row_off + height, col_off:col_off + breadth]
            line.append(jnp.einsum('chw,ohw->co', window, grad_f))
        taps.append(jnp.stack(line))
    return jnp.stack(taps)

def to_tiles(grid):
    var_count = grid.shape[0]
    return grid.reshape(var_count, N_NS, TH, N_EW, TW).transpose(0, 1, 3, 2, 4).reshape(var_count, N_NS * N_EW, TH * TW)

def from_tiles(tiled):
    var_count = tiled.shape[0]
    return tiled.reshape(var_count, N_NS, N_EW, TH, TW).transpose(0, 1, 3, 2, 4).reshape(var_count, N_NS * TH, N_EW * TW)

def reference(fields, w_in, conv_first, conv_second, w_out, slot_cells, slot_weights, slot_count, recv_obs, targets):
    peer_count = N_NS * N_EW
    hp = lax.Precision.HIGHEST
    fields_f = fields.astype(jnp.float32)
    h0 = jnp.einsum('fc,fhw->chw', w_in.astype(jnp.float32), fields_f)
    h0b = h0.astype(jnp.bfloat16)
    z1 = conv_full(h0b, conv_first)
    a1b = jax.nn.gelu(z1).astype(jnp.bfloat16)
    h2b = (h0 + conv_full(a1b, conv_second)).astype(jnp.bfloat16)
    field = jnp.einsum('cv,chw->vhw', w_out.astype(jnp.float32), h2b.astype(jnp.float32))
    tiled = to_tiles(field)
    picked = jax.vmap(lambda grid, cells: grid[:, cells], in_axes=(1, 0), out_axes=1)(tiled, slot_cells)
    partial_value = lax.optimization_barrier(jnp.sum(picked * slot_weights[None], axis=2))
    live = (jnp.arange(CAP)[None, None, :] < slot_count[:, :, None]).reshape(peer_count, SLOTS)
    partial_value = jnp.where(live[None], partial_value, 0.0)
    received = partial_value.reshape(VARS, peer_count, peer_count, CAP).transpose(0, 2, 1, 3).reshape(VARS, peer_count, SLOTS)

    def collect(values, index):
        return jnp.zeros((VARS, OBS_DEV), jnp.float32).at[:, index].add(values)
    predicted = jax.vmap(collect, in_axes=(1, 0), out_axes=1)(received, recv_obs)
    station_pred = predicted.reshape(VARS, OBS)
    resid = station_pred - targets
    scale = 1.0 / (VARS * OBS_DEV)
    loss = 0.5 * jnp.sum(resid * resid) * scale
    grad_obs = (resid * scale).reshape(VARS, peer_count, OBS_DEV)
    grad_recv = jax.vmap(lambda values, index: values[:, index], in_axes=(1, 0), out_axes=1)(grad_obs, recv_obs)
    grad_slot = grad_recv.reshape(VARS, peer_count, peer_count, CAP).transpose(0, 2, 1, 3).reshape(VARS, peer_count, SLOTS)
    grad_slot = jnp.where(live[None], grad_slot, 0.0)

    def spread(values, cells, weights):
        terms = (weights[None] * values[:, None, :]).reshape(VARS, -1)
        return jnp.zeros((VARS, TH * TW), jnp.float32).at[:, cells.reshape(-1)].add(terms)
    grad_tiles = jax.vmap(spread, in_axes=(1, 0, 0), out_axes=1)(grad_slot, slot_cells, slot_weights)
    grad_field = from_tiles(grad_tiles)
    grad_out = jnp.einsum('chw,vhw->cv', h2b.astype(jnp.float32), grad_field, precision=hp)
    grad_h2 = jnp.einsum('cv,vhw->chw', w_out.astype(jnp.float32), grad_field, precision=hp)
    grad_h2b = grad_h2.astype(jnp.bfloat16)
    grad_second = kernel_grad(a1b, grad_h2b)
    grad_a1 = conv_back(grad_h2b, conv_second)
    _, gelu_back = jax.vjp(jax.nn.gelu, z1)
    grad_z1b = gelu_back(grad_a1)[0].astype(jnp.bfloat16)
    grad_first = kernel_grad(h0b, grad_z1b)
    grad_h0b = (grad_h2 + conv_back(grad_z1b, conv_first)).astype(jnp.bfloat16)
    grad_in = jnp.einsum('fhw,chw->fc', fields_f, grad_h0b.astype(jnp.float32))
    grad_fields = jnp.einsum('fc,chw->fhw', w_in.astype(jnp.float32), grad_h0b.astype(jnp.float32))
    return (station_pred, loss, grad_first, grad_second, grad_in, grad_out, grad_fields)
```

```python
import functools

import jax
import jax.numpy as jnp
from jax import lax
from jax.experimental import pallas as pl
from jax.experimental.pallas import tpu as pltpu
from jax.sharding import PartitionSpec as P

BF = jnp.bfloat16
F32 = jnp.float32
CAP = 128
TH, TW = 8, 128
ROW = 144
N12, N10, N8 = 12 * ROW, 10 * ROW, 8 * ROW
CP = 256
AXES = ("ns", "ew")
PIECE = 48
NT = (((1,), (1,)), ((), ()))
TN = (((0,), (0,)), ((), ()))
PARAMS = pltpu.CompilerParams(vmem_limit_bytes=60 * 1024 * 1024)


def dot(x, y, dims=(((1,), (0,)), ((), ()))):
    return lax.dot_general(x, y, dims, preferred_element_type=F32)


def taps(cat, weight, first, count, order):
    total = None
    for a in range(3):
        start = (a if order > 0 else 2 - a) * ROW + first
        term = dot(cat[start : start + count, :], weight[a])
        total = term if total is None else total + term
    return total


def pick(table_row, index):
    return jnp.take_along_axis(
        jnp.broadcast_to(table_row, (8, 128)), index, axis=1, mode="promise_in_bounds"
    )


def forward_kernel(
    flags, ft, win, w1, w2, wo, cells, wts, cnt, out, xcat, acat, gp, h2b_out, hs, as_, fs, pf
):
    zero8 = jnp.zeros((8, CP), F32)
    hs[0:8, :] = zero8
    hs[N12 + 8 : N12 + 16, :] = zero8
    as_[0:8, :] = zero8
    as_[N10 + 8 : N10 + 16, :] = zero8
    hs[8 : N12 + 8, :] = dot(ft[...], win[...])
    for b in range(3):
        xcat[:, b * CP : (b + 1) * CP] = hs[7 + b : 7 + b + N12, :].astype(BF)
    col = lax.broadcasted_iota(jnp.int32, (ROW, CP), 0)
    col_mask = jnp.where(col == 1, flags[2], jnp.where(col == 130, flags[3], 1.0))
    root = 0.7978845608028654
    for part in range(5):
        z2 = taps(xcat, w1, part * 2 * ROW, 2 * ROW, 1)
        for q in range(2):
            r = part * 2 + q
            z = z2[q * ROW : (q + 1) * ROW]
            mask = col_mask
            if r == 0:
                mask = col_mask * flags[0]
            if r == 9:
                mask = col_mask * flags[1]
            zz = z * z
            t = jnp.tanh(root * z * (1.0 + 0.044715 * zz))
            half = 0.5 * (1.0 + t)
            slope = half + 0.5 * z * (1.0 - t * t) * (root * (1.0 + 3 * 0.044715 * zz))
            as_[8 + r * ROW : 8 + (r + 1) * ROW, :] = z * half * mask
            gp[r * ROW : (r + 1) * ROW, :] = slope * mask
    for b in range(3):
        acat[:, b * CP : (b + 1) * CP] = as_[7 + b : 7 + b + N10, :].astype(BF)
    for part in range(4):
        at = part * 2 * ROW
        h2 = hs[8 + 2 * ROW + at : 8 + 4 * ROW + at, :] + taps(acat, w2, at, 2 * ROW, 1)
        h2b_out[at : at + 2 * ROW, :] = h2.astype(BF)
    field = dot(wo[...], h2b_out[...], NT)
    for r in range(8):
        fs[r * 8 : (r + 1) * 8, :] = field[0:8, r * ROW + 2 : r * ROW + 2 + TW]
    pf[...] = jnp.zeros_like(pf)
    lane = lax.broadcasted_iota(jnp.int32, (8, 128), 1)

    def owners(ob, carry):
        rows = pl.ds(pl.multiple_of(ob * 8, 8), 8)
        live = lane < cnt[rows, 0:1]
        index = [cells[k, rows, :] for k in range(4)]
        low = [i & 127 for i in index]
        high = [i >> 7 for i in index]
        weight = [jnp.where(live, wts[k, rows, :], 0.0) for k in range(4)]
        for v in range(6):
            got = [jnp.zeros((8, 128), F32)] * 4
            for r in range(8):
                row = fs[r * 8 + v : r * 8 + v + 1, :]
                got = [
                    jnp.where(high[k] == r, pick(row, low[k]), got[k]) for k in range(4)
                ]
            value = sum(weight[k] * got[k] for k in range(4))
            pf[pl.ds(ob * 64 + v, 8, stride=8), :] = value
        return carry

    lax.fori_loop(0, 16, owners, 0)
    out[...] = pf[...].astype(BF)


def one_hot_rows(low_row, iotas):
    spread = jnp.broadcast_to(low_row, (16, 128)).astype(BF)
    one, zero = jnp.ones((16, 128), BF), jnp.zeros((16, 128), BF)
    return [jnp.where(spread == i, one, zero) for i in iotas]


def low_iotas():
    base = lax.broadcasted_iota(jnp.int32, (16, 128), 0)
    return [(base + 16 * m).astype(F32).astype(BF) for m in range(8)]


def owner_kernel(recv, obs, target, pred, loss, out, left, right, rs, gf):
    iotas = low_iotas()

    def collect(tb, carry):
        block = recv[pl.ds(pl.multiple_of(tb * 64, 64), 64), :].astype(F32)
        index = obs[pl.ds(pl.multiple_of(tb * 8, 8), 8), :]
        low = (index & 127).astype(F32)
        high = index >> 7
        for i in range(8):
            at = pl.ds(pl.multiple_of(tb * 1024 + i * 128, 128), 128)
            mine = jnp.broadcast_to(high[i : i + 1], (8, 128))
            value = block[i * 8 : i * 8 + 8]
            for h in range(8):
                two = [jnp.where(mine == 2 * h + e, value, 0.0) for e in range(2)]
                left[h * 16 : h * 16 + 16, at] = jnp.concatenate(two, 0).astype(BF)
            for m, hot in enumerate(one_hot_rows(low[i : i + 1], iotas)):
                right[m * 16 : m * 16 + 16, at] = hot
        return carry

    lax.fori_loop(0, 16, collect, 0)
    total = dot(left[...], right[...], NT)
    scale = 1.0 / (6 * 2048)
    squares = jnp.zeros((6, 128), F32)
    for h in range(16):
        at = slice(h * 128, h * 128 + 128)
        mine = total[h * 8 : h * 8 + 6]
        pred[:, at] = mine
        resid = mine - target[:, at]
        squares = squares + resid * resid
        rs[h * 8 : h * 8 + 6, :] = resid * scale
    loss[...] = jnp.full((16, 128), jnp.sum(squares) * (0.5 * scale), F32)
    gf[...] = jnp.zeros_like(gf)

    def choose(tb, carry):
        index = obs[pl.ds(pl.multiple_of(tb * 8, 8), 8), :]
        low, high = index & 127, index >> 7
        got = [jnp.zeros((8, 128), F32)] * 6
        for h in range(16):
            here = high == h
            got = [
                jnp.where(here, pick(rs[h * 8 + v : h * 8 + v + 1, :], low), got[v])
                for v in range(6)
            ]
        for v in range(6):
            gf[pl.ds(tb * 64 + v, 8, stride=8), :] = got[v]
        return carry

    lax.fori_loop(0, 16, choose, 0)
    out[...] = gf[...].astype(BF)


def spread_kernel(grad, cells, wts, cnt, out, left, right):
    iotas = low_iotas()
    out[...] = jnp.zeros_like(out)
    lane = lax.broadcasted_iota(jnp.int32, (8, 128), 1)

    def owners(ob, carry):
        rows = pl.ds(pl.multiple_of(ob * 8, 8), 8)
        live = lane < cnt[rows, 0:1]
        block = grad[pl.ds(pl.multiple_of(ob * 64, 64), 64), :].astype(F32)
        for k in range(4):
            index = cells[k, rows, :]
            low = (index & 127).astype(F32)
            high = index >> 7
            weight = jnp.where(live, wts[k, rows, :], 0.0)
            for i in range(8):
                at = slice((k * 8 + i) * 128, (k * 8 + i) * 128 + 128)
                mine = jnp.broadcast_to(high[i : i + 1], (8, 128))
                value = block[i * 8 : i * 8 + 8] * jnp.broadcast_to(weight[i : i + 1], (8, 128))
                for h in range(4):
                    two = [jnp.where(mine == 2 * h + e, value, 0.0) for e in range(2)]
                    left[h * 16 : h * 16 + 16, at] = jnp.concatenate(two, 0).astype(BF)
                for m, hot in enumerate(one_hot_rows(low[i : i + 1], iotas)):
                    right[m * 16 : m * 16 + 16, at] = hot
        out[...] += dot(left[...], right[...], NT)
        return carry

    lax.fori_loop(0, 16, owners, 0)


def backward_kernel(
    gfn, ft, xcat, acat, gp, h2b, w2t, w1t, win, wo, loss, pay, gfields, gs, g2cat, zs, gzcat, own
):
    zero8 = jnp.zeros((8, CP), F32)
    gs[0:8, :] = zero8
    gs[N12 + 8 : N12 + 16, :] = zero8
    zs[0:8, :] = zero8
    zs[N10 + 8 : N10 + 16, :] = zero8
    x = gfn[...]
    x_hi = x.astype(BF)
    x_lo = (x - x_hi.astype(F32)).astype(BF)
    gs[8 : N12 + 8, :] = dot(x_hi, wo[...]) + dot(x_lo, wo[...])
    for b in range(3):
        g2cat[:, b * CP : (b + 1) * CP] = gs[9 - b : 9 - b + N12, :].astype(BF)
    for part in range(5):
        at = part * 2 * ROW
        g = taps(g2cat, w2t, at, 2 * ROW, -1)
        zs[8 + at : 8 + at + 2 * ROW, :] = g * gp[at : at + 2 * ROW, :]
    for b in range(3):
        gzcat[:, b * CP : (b + 1) * CP] = zs[9 - b : 9 - b + N10, :].astype(BF)
    col = lax.broadcasted_iota(jnp.int32, (ROW, CP), 0)
    keep = jnp.where((col >= 2) & (col < 2 + TW), 1.0, 0.0)
    keep2 = jnp.concatenate([keep, keep], 0)
    for part in range(4):
        at = part * 2 * ROW
        g = gs[8 + 2 * ROW + at : 8 + 4 * ROW + at, :] + taps(gzcat, w1t, at, 2 * ROW, -1)
        own[at : at + 2 * ROW, :] = (g * keep2).astype(BF)
    g_in = dot(ft[2 * ROW : 10 * ROW, :], own[...], TN)
    g_fields = dot(win[...], own[...], NT)
    for r in range(8):
        gfields[pl.ds(r, 64, stride=8), :] = g_fields[:, r * ROW + 2 : r * ROW + 2 + TW]
    small = keep[:, 0:8]
    x_own = x[2 * ROW : 10 * ROW] * jnp.concatenate([small] * 8, 0)
    o_hi = x_own.astype(BF)
    o_lo = (x_own - o_hi.astype(F32)).astype(BF)
    g_out = dot(o_hi, h2b[...], TN) + dot(o_lo, h2b[...], TN)

    for part in range(4):
        at = part * 2 * ROW
        own[at : at + 2 * ROW, :] = (gs[8 + 2 * ROW + at : 8 + 4 * ROW + at, :] * keep2).astype(BF)
    second_t = own[...].T[0:192]
    for part in range(4):
        at = part * 2 * ROW
        own[at : at + 2 * ROW, :] = (zs[8 + ROW + at : 8 + 3 * ROW + at, :] * keep2).astype(BF)
    first_t = own[...].T[0:192]
    for a in range(3):
        y2 = dot(second_t, acat[a * ROW : a * ROW + N8, :])
        y1 = dot(first_t, xcat[(1 + a) * ROW : (1 + a) * ROW + N8, :])
        for b in range(3):
            at = (a * 3 + b) * 192
            pay[at : at + 192, :] = y2[:, b * CP : b * CP + 128].astype(BF)
            pay[1728 + at : 1728 + at + 192, :] = y1[:, b * CP : b * CP + 128].astype(BF)
            rest2 = y2[:, b * CP + 128 : b * CP + 256]
            rest1 = y1[:, b * CP + 128 : b * CP + 256]
            pay[3456 + at : 3456 + at + 192, :] = (rest2 + pltpu.roll(rest1, 64, 1)).astype(BF)
    pay[5184:5248, :] = g_in[:, 0:128].astype(BF)
    pay[5248:5312, :] = g_in[:, 128:256].astype(BF)
    pay[5312:5328, :] = jnp.concatenate([g_out[:, 0:128], g_out[:, 128:256]], 0).astype(BF)
    pay[5328:5344, :] = loss[...].astype(BF)
    pay[5344:, :] = jnp.zeros((128 * PIECE - 5344, 128), BF)


def neighbours(array, axis, dim, width):
    count, length = lax.axis_size(axis), array.shape[dim]
    up = [(i, i + 1) for i in range(count - 1)]
    down = [(j, i) for i, j in up]
    last = lax.slice_in_dim(array, length - width, length, axis=dim)
    first = lax.slice_in_dim(array, 0, width, axis=dim)
    before = lax.ppermute(last, axis, up)
    after = lax.ppermute(first, axis, down)
    return jnp.concatenate([before, array, after], axis=dim)


def exchange(rows):
    return lax.all_to_all(rows, AXES, split_axis=0, concat_axis=0, tiled=True)


def call(kernel, out_shapes, scratch, *operands, smem=0):
    specs = [pl.BlockSpec(memory_space=pltpu.SMEM)] * smem + [
        pl.BlockSpec(memory_space=pltpu.VMEM)
    ] * (len(operands) - smem)
    return pl.pallas_call(
        kernel,
        out_shape=[jax.ShapeDtypeStruct(s, d) for s, d in out_shapes],
        in_specs=specs,
        out_specs=[pl.BlockSpec(memory_space=pltpu.VMEM)] * len(out_shapes),
        scratch_shapes=[pltpu.VMEM(s, d) for s, d in scratch],
        compiler_params=PARAMS,
    )(*operands)


def stacked(kernel):
    padded = jnp.pad(kernel, ((0, 0), (0, 0), (0, CP - 192), (0, CP - 192)))
    return padded.reshape(3, 3 * CP, CP)


def on_device(
    fields,
    w_in,
    conv_first,
    conv_second,
    w_out,
    slot_cells,
    slot_weights,
    slot_count,
    recv_obs,
    targets,
):
    ns, ew = lax.axis_index("ns"), lax.axis_index("ew")
    flags = jnp.stack(
        [ns > 0, ns < lax.axis_size("ns") - 1, ew > 0, ew < lax.axis_size("ew") - 1]
    ).astype(F32)
    cells = slot_cells.reshape(4, 128, CAP)
    wts = slot_weights.reshape(4, 128, CAP)
    cnt = slot_count.reshape(128, 1)
    obs = recv_obs.reshape(128, CAP)
    win = jnp.pad(w_in, ((0, 0), (0, CP - 192)))
    wo = jnp.pad(w_out.T, ((0, 2), (0, CP - 192)))
    wo16 = jnp.pad(wo, ((0, 8), (0, 0)))

    grid = fields.transpose(1, 2, 0)
    grid = neighbours(grid, "ns", 0, 2)
    grid = neighbours(grid, "ew", 1, 2)
    ft = jnp.pad(grid, ((0, 0), (0, ROW - TW - 4), (0, 0))).reshape(N12, 64)
    sent, xcat, acat, gp, h2b = call(
        forward_kernel,
        [((1024, 128), BF), ((N12, 3 * CP), BF), ((N10, 3 * CP), BF), ((N10, CP), F32), ((N8, CP), BF)],
        [((N12 + 16, CP), F32), ((N10 + 16, CP), F32), ((64, 128), F32), ((1024, 128), F32)],
        flags, ft, win, stacked(conv_first), stacked(conv_second), wo16, cells, wts, cnt,
        smem=1,
    )
    received = exchange(sent)
    pred, loss, back = call(
        owner_kernel,
        [((6, 2048), F32), ((16, 128), F32), ((1024, 128), BF)],
        [((128, 16384), BF), ((128, 16384), BF), ((128, 128), F32), ((1024, 128), F32)],
        received, obs, targets,
    )
    grads = exchange(back)
    (g_field,) = call(
        spread_kernel,
        [((64, 128), F32)],
        [((64, 4096), BF), ((128, 4096), BF)],
        grads, cells, wts, cnt,
    )
    g_field = neighbours(g_field.reshape(8, 8, 128), "ns", 0, 2)
    g_field = neighbours(g_field, "ew", 2, 2).transpose(0, 2, 1)
    gfn = jnp.pad(g_field, ((0, 0), (0, ROW - TW - 4), (0, 0))).reshape(N12, 8)
    swap = (0, 1, 3, 2)
    pay, g_fields = call(
        backward_kernel,
        [((128 * PIECE, 128), BF), ((512, 128), F32)],
        [
            ((N12 + 16, CP), F32), ((N12, 3 * CP), BF), ((N10 + 16, CP), F32),
            ((N10, 3 * CP), BF), ((N8, CP), BF),
        ],
        gfn, ft, xcat, acat, gp, h2b,
        stacked(conv_second.transpose(swap)), stacked(conv_first.transpose(swap)), win, wo, loss,
    )
    share = jnp.sum(exchange(pay.reshape(128, PIECE, 128)).astype(F32), axis=0).astype(BF)
    whole = exchange(jnp.broadcast_to(share[None], (128, PIECE, 128)))
    whole = whole.reshape(128 * PIECE, 128).astype(F32)
    rest = whole[3456:5184].reshape(3, 3, 192, 128)
    second = whole[0:1728].reshape(3, 3, 192, 128)
    first = whole[1728:3456].reshape(3, 3, 192, 128)
    grad_second = jnp.concatenate([second, rest[..., :64]], -1).transpose(swap)
    grad_first = jnp.concatenate([first, rest[..., 64:]], -1).transpose(swap)
    grad_in = jnp.concatenate([whole[5184:5248], whole[5248:5312, :64]], 1)
    grad_out = jnp.concatenate([whole[5312:5318], whole[5320:5326, :64]], 1).T
    return (
        pred,
        whole[5328, 0],
        grad_first,
        grad_second,
        grad_in,
        grad_out,
        g_fields.reshape(64, TH, TW),
    )


def solution(mesh):
    in_specs = (
        P(None, "ns", "ew"),
        P(),
        P(),
        P(),
        P(),
        P(("ns", "ew"), None, None),
        P(("ns", "ew"), None, None),
        P(("ns", "ew"), None),
        P(("ns", "ew"), None),
        P(None, ("ns", "ew")),
    )
    out_specs = (P(None, ("ns", "ew")), P(), P(), P(), P(), P(), P(None, "ns", "ew"))
    return jax.shard_map(
        on_device, mesh=mesh, in_specs=in_specs, out_specs=out_specs, check_vma=False
    )
```

```python
import jax
import jax.numpy as jnp
from jax import lax
from jax.experimental import pallas as pl
from jax.experimental.pallas import tpu as pltpu
from jax.sharding import PartitionSpec as P

BF = jnp.bfloat16
F32 = jnp.float32
I32 = jnp.int32
CAP = 128
TH, TW = 8, 128
C = 192
ROW = 144
N12, N10, N8 = 12 * ROW, 10 * ROW, 8 * ROW
CP = 256
AXES = ("ns", "ew")
PIECE = 48
HALF = 64 * PIECE
REST = 1728
EXTRA = 2592
NT = (((1,), (1,)), ((), ()))
TN = (((0,), (0,)), ((), ()))


def dot(x, y, dims=(((1,), (0,)), ((), ()))):
    return lax.dot_general(x, y, dims, preferred_element_type=F32)


def taps(cat, weight, first, count, order):
    total = None
    for a in range(3):
        start = (a if order > 0 else 2 - a) * ROW + first
        rows = cat[start : start + count, :]
        term = dot(rows, weight[a]) if order > 0 else dot(rows, weight[a], NT)
        total = term if total is None else total + term
    return total


def stack_weights(out, kernel, order):
    out[...] = jnp.zeros_like(out)
    for a in range(3):
        for b in range(3):
            if order > 0:
                out[a, b * CP : b * CP + C, 0:C] = kernel[a, b]
            else:
                out[a, 0:C, b * CP : b * CP + C] = kernel[a, b]


def pick(table, row, index):
    return jnp.take_along_axis(
        jnp.broadcast_to(table[row : row + 1, :], (8, 128)),
        index,
        axis=1,
        mode="promise_in_bounds",
    )


def pack_pair(x, y):
    return x * 65536 + (y + 32768)


def unpack_pair(word):
    return (word >> 16).astype(F32), ((word & 65535) - 32768).astype(F32)


def forward_kernel(
    flags, ft, small, c1, c2, cells, wts, cnt, out, a1_out, gp, h2b, hs, xcat, as_, acat, w1, w2,
    fq, pf,
):
    zero8 = jnp.zeros((8, CP), F32)
    hs[0:8, :] = zero8
    hs[N12 + 8 : N12 + 16, :] = zero8
    as_[0:8, :] = zero8
    as_[N10 + 8 : N10 + 16, :] = zero8
    stack_weights(w1, c1, 1)
    stack_weights(w2, c2, 1)
    hs[8 : N12 + 8, :] = dot(ft[...], small[0:64, :])
    for b in range(3):
        xcat[:, b * CP : (b + 1) * CP] = hs[7 + b : 7 + b + N12, :].astype(BF)
    col = lax.broadcasted_iota(I32, (ROW, CP), 0)
    col_mask = jnp.where(col == 1, flags[2], jnp.where(col == 130, flags[3], 1.0))
    root = 0.7978845608028654
    for part in range(5):
        z2 = taps(xcat, w1, part * 2 * ROW, 2 * ROW, 1)
        for q in range(2):
            r = part * 2 + q
            z = z2[q * ROW : (q + 1) * ROW]
            mask = col_mask
            if r == 0:
                mask = col_mask * flags[0]
            if r == 9:
                mask = col_mask * flags[1]
            zz = z * z
            t = jnp.tanh(root * z * (1.0 + 0.044715 * zz))
            half = 0.5 * (1.0 + t)
            slope = half + 0.5 * z * (1.0 - t * t) * (root * (1.0 + 3 * 0.044715 * zz))
            a1 = z * half * mask
            as_[8 + r * ROW : 8 + (r + 1) * ROW, :] = a1
            a1_out[r * ROW : (r + 1) * ROW, :] = a1.astype(BF)
            gp[r * ROW : (r + 1) * ROW, :] = (slope * mask).astype(BF)
    for b in range(3):
        acat[:, b * CP : (b + 1) * CP] = as_[7 + b : 7 + b + N10, :].astype(BF)
    for part in range(4):
        at = part * 2 * ROW
        h2 = hs[8 + 2 * ROW + at : 8 + 4 * ROW + at, :] + taps(acat, w2, at, 2 * ROW, 1)
        h2b[at : at + 2 * ROW, :] = h2.astype(BF)
    field = dot(small[64:80, :], h2b[...], NT)
    tiles = [field[0:8, r * ROW + 2 : r * ROW + 2 + TW] for r in range(8)]
    top = tiles[0]
    for r in range(1, 8):
        top = jnp.maximum(jnp.abs(top), jnp.abs(tiles[r]))
    largest = jnp.maximum(jnp.max(jnp.abs(top)), 1e-30)
    up = 32000.0 / largest
    down = largest * (1.0 / 32000.0)
    for r in range(8):
        whole = jnp.round(tiles[r] * up).astype(I32)
        fq[r * 8 : r * 8 + 3, :] = pack_pair(whole[0:3], whole[3:6])
    pf[...] = jnp.zeros_like(pf)
    lane = lax.broadcasted_iota(I32, (8, 128), 1)

    def owners(ob, carry):
        rows = pl.ds(pl.multiple_of(ob * 8, 8), 8)
        live = lane < cnt[rows, 0:1]
        sums = [jnp.zeros((8, 128), F32)] * 6
        for k in range(4):
            index = cells[k, rows, :]
            low, high = index & 127, index >> 7
            weight = jnp.where(live, wts[k, rows, :] * down, 0.0)
            got = [jnp.zeros((8, 128), I32)] * 3
            for r in range(8):
                here = high == r
                got = [jnp.where(here, pick(fq, r * 8 + v, low), got[v]) for v in range(3)]
            for v in range(3):
                x, y = unpack_pair(got[v])
                sums[v] = sums[v] + weight * x
                sums[v + 3] = sums[v + 3] + weight * y
        for v in range(6):
            pf[pl.ds(ob * 64 + v, 8, stride=8), :] = sums[v]
        return carry

    lax.fori_loop(0, 16, owners, 0)
    out[...] = pf[...].astype(BF)


def turn_kernel(a1, ft, small, a1t, h0t, wide, thin, pa, pt):
    wide[...] = a1[...].astype(F32)
    thin[...] = ft[...].astype(F32)
    ones = lax.broadcasted_iota(I32, (CP, CP), 0) == lax.broadcasted_iota(I32, (CP, CP), 1)
    same = jnp.where(ones, 1.0, 0.0).astype(BF)
    win_t = dot(same[0:C, :], small[0:64, :], NT).astype(BF)
    for b in range(3):
        for r in range(10):
            at = slice(r * 128, r * 128 + 128)
            pa[at, :] = wide[r * ROW + 1 + b : r * ROW + 129 + b, :].astype(BF)
            pt[at, :] = thin[(r + 1) * ROW + 1 + b : (r + 1) * ROW + 129 + b, :].astype(BF)
        a1t[b * C : (b + 1) * C, :] = dot(same[0:C, :], pa[...], NT).astype(BF)
        h0t[b * C : (b + 1) * C, :] = dot(win_t, pt[...], NT).astype(BF)


def spread_row(row):
    return jnp.broadcast_to(row, (16, 128)).astype(BF)


def iotas(count):
    base = lax.broadcasted_iota(I32, (16, 128), 0)
    return [(base + 16 * m).astype(F32).astype(BF) for m in range(count)]


def owner_kernel(recv, obs, target, pred, loss, out, left, right, total, rq, gf):
    steps = iotas(8)
    none = jnp.zeros((16, 128), BF)
    one = jnp.ones((16, 128), BF)

    def collect(tb, carry):
        block = recv[pl.ds(pl.multiple_of(tb * 64, 64), 64), :].astype(F32)
        index = obs[pl.ds(pl.multiple_of(tb * 8, 8), 8), :]
        low = (index & 127).astype(F32)
        high = (index >> 7).astype(F32)
        for i in range(8):
            at = pl.ds(pl.multiple_of(tb * 1024 + i * 128, 128), 128)
            here = spread_row(high[i : i + 1]) == steps[0]
            for v in range(6):
                value = spread_row(block[i * 8 + v : i * 8 + v + 1])
                left[v * 16 : v * 16 + 16, at] = jnp.where(here, value, none)
            mine = spread_row(low[i : i + 1])
            for m in range(8):
                right[m * 16 : m * 16 + 16, at] = jnp.where(mine == steps[m], one, none)
        return carry

    lax.fori_loop(0, 16, collect, 0)
    total[...] = dot(left[...], right[...], NT)
    scale = 1.0 / (6 * 2048)
    squares = jnp.zeros((6, 128), F32)
    resids = []
    for h in range(16):
        at = slice(h * 128, h * 128 + 128)
        mine = total[pl.ds(h, 6, stride=16), :]
        pred[:, at] = mine
        resid = mine - target[:, at]
        squares = squares + resid * resid
        resids.append(resid * scale)
    loss[...] = jnp.full((16, 128), jnp.sum(squares) * (0.5 * scale), F32)
    top = jnp.abs(resids[0])
    for h in range(1, 16):
        top = jnp.maximum(top, jnp.abs(resids[h]))
    largest = jnp.maximum(jnp.max(top), 1e-30)
    up = 32000.0 / largest
    down = largest * (1.0 / 32000.0)
    for h in range(16):
        whole = jnp.round(resids[h] * up).astype(I32)
        rq[h * 8 : h * 8 + 3, :] = pack_pair(whole[0:3], whole[3:6])
    gf[...] = jnp.zeros_like(gf)

    def choose(tb, carry):
        index = obs[pl.ds(pl.multiple_of(tb * 8, 8), 8), :]
        low, high = index & 127, index >> 7
        got = [jnp.zeros((8, 128), I32)] * 3
        for h in range(16):
            here = high == h
            got = [jnp.where(here, pick(rq, h * 8 + v, low), got[v]) for v in range(3)]
        for v in range(3):
            x, y = unpack_pair(got[v])
            gf[pl.ds(tb * 64 + v, 8, stride=8), :] = x * down
            gf[pl.ds(tb * 64 + v + 3, 8, stride=8), :] = y * down
        return carry

    lax.fori_loop(0, 16, choose, 0)
    out[...] = gf[...].astype(BF)


def spread_kernel(grad, cells, wts, cnt, out, left, right, total):
    steps = iotas(4)
    none = jnp.zeros((16, 128), BF)
    total[...] = jnp.zeros_like(total)
    lane = lax.broadcasted_iota(I32, (8, 128), 1)

    def owners(ob, carry):
        rows = pl.ds(pl.multiple_of(ob * 8, 8), 8)
        live = lane < cnt[rows, 0:1]
        block = grad[pl.ds(pl.multiple_of(ob * 64, 64), 64), :].astype(F32)
        index = [cells[k, rows, :] for k in range(4)]
        low = [(i & 63).astype(F32) for i in index]
        high = [(i >> 6).astype(F32) for i in index]
        weight = [jnp.where(live, wts[k, rows, :], 0.0) for k in range(4)]
        for i in range(8):
            values = [spread_row(block[i * 8 + v : i * 8 + v + 1]) for v in range(6)]
            for k in range(4):
                at = slice((i * 4 + k) * 128, (i * 4 + k) * 128 + 128)
                here = spread_row(high[k][i : i + 1]) == steps[0]
                for v in range(6):
                    left[v * 16 : v * 16 + 16, at] = jnp.where(here, values[v], none)
                mine = spread_row(low[k][i : i + 1])
                amount = spread_row(weight[k][i : i + 1])
                for m in range(4):
                    right[m * 16 : m * 16 + 16, at] = jnp.where(mine == steps[m], amount, none)
        total[...] += dot(left[...], right[...], NT)
        return carry

    lax.fori_loop(0, 16, owners, 0)
    out[...] = jnp.zeros_like(out)
    for r in range(8):
        even = total[pl.ds(2 * r, 6, stride=16), :]
        odd = total[pl.ds(2 * r + 1, 6, stride=16), :]
        out[r * 8 : r * 8 + 6, :] = jnp.concatenate([even, odd], 1)


def backward_kernel(
    core, gfn, ft, a1t, h0t, gp, h2b, c2, c1, small, loss, pay, gfields, gs, g2cat, zs, gzcat, own,
    w2, w1, gc,
):
    zero8 = jnp.zeros((8, CP), F32)
    gs[0:8, :] = zero8
    gs[N12 + 8 : N12 + 16, :] = zero8
    zs[0:8, :] = zero8
    zs[N10 + 8 : N10 + 16, :] = zero8
    stack_weights(w2, c2, -1)
    stack_weights(w1, c1, -1)
    wo = small[64:72, :]
    base_s = pl.multiple_of(core[0] * HALF, 16)
    base_f = pl.multiple_of((1 - core[0]) * HALF, 16)

    def put(base, at, value):
        pay[pl.ds(pl.multiple_of(base + at, 16), value.shape[0]), :] = value.astype(BF)

    def put_taps(base, turned):
        for a in range(3):
            y = dot(turned[:, a * 128 : a * 128 + 1024], gc[...])
            for b in range(3):
                tap = a * 3 + b
                mine = y[b * C : (b + 1) * C]
                put(base, tap * C, mine[:, 0:128])
                rest = mine[:, 128:256]
                put(base, REST + tap * 96, rest[0:96] + pltpu.roll(rest[96:192], 64, 1))

    x = gfn[...]
    x_hi = x.astype(BF)
    x_lo = (x - x_hi.astype(F32)).astype(BF)
    gs[8 : N12 + 8, :] = dot(x_hi, wo) + dot(x_lo, wo)
    for b in range(3):
        g2cat[:, b * CP : (b + 1) * CP] = gs[9 - b : 9 - b + N12, :].astype(BF)
    for r in range(8):
        at = 8 + (r + 2) * ROW + 2
        gc[r * 128 : r * 128 + 128, :] = gs[at : at + 128, :].astype(BF)
    put_taps(base_s, a1t)
    for part in range(5):
        at = part * 2 * ROW
        g = taps(g2cat, w2, at, 2 * ROW, -1)
        zs[8 + at : 8 + at + 2 * ROW, :] = g * gp[at : at + 2 * ROW, :].astype(F32)
    for b in range(3):
        gzcat[:, b * CP : (b + 1) * CP] = zs[9 - b : 9 - b + N10, :].astype(BF)
    for r in range(8):
        at = 8 + (r + 1) * ROW + 2
        gc[r * 128 : r * 128 + 128, :] = zs[at : at + 128, :].astype(BF)
    put_taps(base_f, h0t)
    col = lax.broadcasted_iota(I32, (ROW, CP), 0)
    keep = jnp.where((col >= 2) & (col < 2 + TW), 1.0, 0.0)
    keep2 = jnp.concatenate([keep, keep], 0)
    for part in range(4):
        at = part * 2 * ROW
        g = gs[8 + 2 * ROW + at : 8 + 4 * ROW + at, :] + taps(gzcat, w1, at, 2 * ROW, -1)
        own[at : at + 2 * ROW, :] = (g * keep2).astype(BF)
    g_in = dot(ft[2 * ROW : 10 * ROW, :], own[...], TN)
    g_fields = dot(small[0:64, :], own[...], NT)
    for r in range(8):
        gfields[pl.ds(r, 64, stride=8), :] = g_fields[:, r * ROW + 2 : r * ROW + 2 + TW]
    x_own = x[2 * ROW : 10 * ROW] * jnp.concatenate([keep[:, 0:8]] * 8, 0)
    o_hi = x_own.astype(BF)
    o_lo = (x_own - o_hi.astype(F32)).astype(BF)
    g_out = dot(o_hi, h2b[...], TN) + dot(o_lo, h2b[...], TN)
    put(base_s, EXTRA, g_in[:, 0:128])
    rest = g_in[:, 128:256]
    put(base_s, EXTRA + 64, rest[0:32] + pltpu.roll(rest[32:64], 64, 1))
    put(base_s, EXTRA + 96, jnp.zeros((HALF - EXTRA - 96, 128), F32))
    put(base_f, EXTRA, jnp.concatenate([g_out[:, 0:128], g_out[:, 128:256]], 0))
    put(base_f, EXTRA + 16, loss[...])
    put(base_f, EXTRA + 32, jnp.zeros((HALF - EXTRA - 32, 128), F32))


def unpack_kernel(core, mine, other, second, first, g_in, g_out, loss):
    def unpack(source, kernel):
        for tap in range(9):
            a, b = tap // 3, tap % 3
            kernel[a, b, :, 0:128] = source[tap * C : (tap + 1) * C, :].astype(F32)
            rest = source[REST + tap * 96 : REST + tap * 96 + 96, :].astype(F32)
            kernel[a, b, 0:96, 128:C] = rest[:, 0:64]
            kernel[a, b, 96:C, 128:C] = pltpu.roll(rest, 64, 1)[:, 0:64]

    def both(s, f):
        unpack(s, second)
        unpack(f, first)
        g_in[:, 0:128] = s[EXTRA : EXTRA + 64, :].astype(F32)
        rest = s[EXTRA + 64 : EXTRA + 96, :].astype(F32)
        g_in[0:32, 128:C] = rest[:, 0:64]
        g_in[32:64, 128:C] = pltpu.roll(rest, 64, 1)[:, 0:64]
        extra = f[EXTRA : EXTRA + 32, :].astype(F32)
        g_out[:, 0:128] = extra[0:8]
        g_out[:, 128:256] = extra[8:16]
        loss[...] = extra[16:24]

    @pl.when(core[0] == 0)
    def _():
        both(mine, other)

    @pl.when(core[0] == 1)
    def _():
        both(other, mine)


def neighbours(array, axis, dim, width):
    count, length = lax.axis_size(axis), array.shape[dim]
    up = [(i, i + 1) for i in range(count - 1)]
    down = [(j, i) for i, j in up]
    last = lax.slice_in_dim(array, length - width, length, axis=dim)
    first = lax.slice_in_dim(array, 0, width, axis=dim)
    before = lax.ppermute(last, axis, up)
    after = lax.ppermute(first, axis, down)
    return jnp.concatenate([before, array, after], axis=dim)


def exchange(rows, groups=None):
    return lax.all_to_all(
        rows, AXES, split_axis=0, concat_axis=0, tiled=True, axis_index_groups=groups
    )


def call(kernel, out_shapes, scratch, *operands, smem=0, vmem=60, flops=0):
    specs = [pl.BlockSpec(memory_space=pltpu.SMEM)] * smem + [
        pl.BlockSpec(memory_space=pltpu.VMEM)
    ] * (len(operands) - smem)
    return pl.pallas_call(
        kernel,
        out_shape=[jax.ShapeDtypeStruct(s, d) for s, d in out_shapes],
        in_specs=specs,
        out_specs=[pl.BlockSpec(memory_space=pltpu.VMEM)] * len(out_shapes),
        scratch_shapes=[pltpu.VMEM(s, d) for s, d in scratch],
        compiler_params=pltpu.CompilerParams(vmem_limit_bytes=vmem * 1024 * 1024),
        cost_estimate=pl.CostEstimate(flops=flops, bytes_accessed=4_000_000, transcendentals=0),
    )(*operands)


def on_device(
    fields,
    w_in,
    conv_first,
    conv_second,
    w_out,
    slot_cells,
    slot_weights,
    slot_count,
    recv_obs,
    targets,
):
    ns, ew = lax.axis_index("ns"), lax.axis_index("ew")
    n_ns, n_ew = lax.axis_size("ns"), lax.axis_size("ew")
    flags = jnp.stack([ns > 0, ns < n_ns - 1, ew > 0, ew < n_ew - 1]).astype(F32)
    core = (ns % 2).astype(I32).reshape(1)
    cells = slot_cells.reshape(4, 128, CAP)
    wts = slot_weights.reshape(4, 128, CAP)
    cnt = slot_count.reshape(128, 1)
    obs = recv_obs.reshape(128, CAP)
    small = jnp.concatenate([w_in, jnp.pad(w_out.T, ((0, 10), (0, 0)))], 0)
    small = jnp.pad(small, ((0, 0), (0, CP - C)))

    grid = fields.transpose(1, 2, 0)
    grid = neighbours(grid, "ns", 0, 2)
    grid = neighbours(grid, "ew", 1, 2)
    ft = jnp.pad(grid, ((0, 0), (0, ROW - TW - 4), (0, 0))).reshape(N12, 64)
    sent, a1, gp, h2b = call(
        forward_kernel,
        [((1024, 128), BF), ((N10, CP), BF), ((N10, CP), BF), ((N8, CP), BF)],
        [
            ((N12 + 16, CP), F32), ((N12, 3 * CP), BF), ((N10 + 16, CP), F32),
            ((N10, 3 * CP), BF), ((3, 3 * CP, CP), BF), ((3, 3 * CP, CP), BF),
            ((64, 128), I32), ((1024, 128), F32),
        ],
        flags, ft, small, conv_first, conv_second, cells, wts, cnt,
        smem=1, vmem=40, flops=2 * 10**9,
    )
    received = exchange(sent)
    a1t, h0t = call(
        turn_kernel,
        [((3 * C, 1280), BF), ((3 * C, 1280), BF)],
        [((N10, CP), F32), ((N12, 64), F32), ((1280, CP), BF), ((1280, 64), BF)],
        a1, ft, small,
        vmem=32, flops=10**9,
    )
    pred, loss, back = call(
        owner_kernel,
        [((6, 2048), F32), ((16, 128), F32), ((1024, 128), BF)],
        [
            ((96, 16384), BF), ((128, 16384), BF), ((96, 128), F32), ((128, 128), I32),
            ((1024, 128), F32),
        ],
        received, obs, targets,
        vmem=32, flops=10**9,
    )
    grads = exchange(back)
    (g_field,) = call(
        spread_kernel,
        [((64, 128), F32)],
        [((96, 4096), BF), ((64, 4096), BF), ((96, 64), F32)],
        grads, cells, wts, cnt,
        vmem=32, flops=10**9,
    )
    g_field = neighbours(g_field.reshape(8, 8, 128), "ns", 0, 2)
    g_field = neighbours(g_field, "ew", 2, 2).transpose(0, 2, 1)
    gfn = jnp.pad(g_field, ((0, 0), (0, ROW - TW - 4), (0, 0))).reshape(N12, 8)
    pay, g_fields = call(
        backward_kernel,
        [((2 * HALF, 128), BF), ((512, 128), F32)],
        [
            ((N12 + 16, CP), F32), ((N12, 3 * CP), BF), ((N10 + 16, CP), F32),
            ((N10, 3 * CP), BF), ((N8, CP), BF), ((3, CP, 3 * CP), BF), ((3, CP, 3 * CP), BF),
            ((1024, CP), BF),
        ],
        core, gfn, ft, a1t, h0t, gp, h2b, conv_second, conv_first, small, loss,
        smem=1, vmem=40, flops=2 * 10**9,
    )
    pairs = [(n, n + 1 - 2 * (n % 2)) for n in range(n_ns)]
    groups = [[n * n_ew + e for n in range(c, n_ns, 2) for e in range(n_ew)] for c in range(2)]
    theirs = lax.ppermute(pay[HALF:], "ns", pairs)
    summed = (pay[:HALF].astype(F32) + theirs.astype(F32)).astype(BF).reshape(64, PIECE, 128)
    share = jnp.sum(exchange(summed, groups).astype(F32), axis=0).astype(BF)
    mine = exchange(jnp.broadcast_to(share[None], (64, PIECE, 128)), groups).reshape(HALF, 128)
    other = lax.ppermute(mine, "ns", pairs)
    grad_second, grad_first, grad_in, g_out, total = call(
        unpack_kernel,
        [((3, 3, C, C), F32), ((3, 3, C, C), F32), ((64, C), F32), ((8, CP), F32), ((8, 128), F32)],
        [],
        core, mine, other,
        smem=1, vmem=32,
    )
    return (
        pred,
        total[0, 0],
        grad_first,
        grad_second,
        grad_in,
        g_out[:6, :C].T,
        g_fields.reshape(64, TH, TW),
    )


def solution(mesh):
    in_specs = (
        P(None, "ns", "ew"),
        P(),
        P(),
        P(),
        P(),
        P(("ns", "ew"), None, None),
        P(("ns", "ew"), None, None),
        P(("ns", "ew"), None),
        P(("ns", "ew"), None),
        P(None, ("ns", "ew")),
    )
    out_specs = (P(None, ("ns", "ew")), P(), P(), P(), P(), P(), P(None, "ns", "ew"))
    return jax.shard_map(
        on_device, mesh=mesh, in_specs=in_specs, out_specs=out_specs, check_vma=False
    )
```

```python
import jax
import jax.numpy as jnp
from jax import lax
from jax.experimental import pallas as pl
from jax.experimental.pallas import tpu as pltpu
from jax.sharding import PartitionSpec as P

BF = jnp.bfloat16
F32 = jnp.float32
I32 = jnp.int32
CAP = 128
TH, TW = 8, 128
C = 192
ROW = 144
N12, N10, N8 = 12 * ROW, 10 * ROW, 8 * ROW
CP = 256
AXES = ("ns", "ew")
PIECE = 48
HALF = 64 * PIECE
REST = 1728
EXTRA = 2592
NT = (((1,), (1,)), ((), ()))
TN = (((0,), (0,)), ((), ()))


def dot(x, y, dims=(((1,), (0,)), ((), ()))):
    return lax.dot_general(x, y, dims, preferred_element_type=F32)


def taps(cat, weight, first, count, order):
    total = None
    for a in range(3):
        start = (a if order > 0 else 2 - a) * ROW + first
        rows = cat[start : start + count, :]
        term = dot(rows, weight[a]) if order > 0 else dot(rows, weight[a], NT)
        total = term if total is None else total + term
    return total


def stack_weights(out, kernel, order):
    out[...] = jnp.zeros_like(out)
    for a in range(3):
        for b in range(3):
            if order > 0:
                out[a, b * CP : b * CP + C, 0:C] = kernel[a, b]
            else:
                out[a, 0:C, b * CP : b * CP + C] = kernel[a, b]


def pick(table, row, index):
    return jnp.take_along_axis(
        jnp.broadcast_to(table[row : row + 1, :], (8, 128)),
        index,
        axis=1,
        mode="promise_in_bounds",
    )


def pack_pair(x, y):
    return x * 65536 + (y + 32768)


def unpack_pair(word):
    return (word >> 16).astype(F32), ((word & 65535) - 32768).astype(F32)


def fields_kernel(f8, north, south, ftm, fm, wl, wr, s8, sn, ss, sw, se):
    s8[...] = f8[...].astype(F32)
    sn[...] = north[...].astype(F32)
    ss[...] = south[...].astype(F32)
    sw[...] = jnp.zeros_like(sw)
    se[...] = jnp.zeros_like(se)
    for r in range(12):
        if r < 2:
            block = sn[pl.ds(r, 64, stride=2), :]
        elif r < 10:
            block = s8[pl.ds(r - 2, 64, stride=8), :]
            fm[:, (r - 2) * 128 : (r - 1) * 128] = block.astype(BF)
        else:
            block = ss[pl.ds(r - 10, 64, stride=2), :]
        turned = block.T
        ftm[r * 128 : r * 128 + 128, :] = turned.astype(BF)
        sw[2 * r : 2 * r + 2, :] = turned[0:2]
        se[2 * r : 2 * r + 2, :] = turned[126:128]
    wl[...] = sw[...].astype(BF)
    wr[...] = se[...].astype(BF)


def turn_field_kernel(gf, north, south, et, wl, wr):
    turned = jnp.concatenate([north[...], gf[...], south[...]], 0).T
    et[...] = turned
    wl[...] = turned[0:2]
    wr[...] = turned[126:128]


def forward_kernel(
    flags, ftm, wl, wr, small, c1, c2, cells, wts, cnt, out, a1_out, gp, h2c, hs, xcat, as_, acat,
    w1, w2, fq, pf,
):
    zero8 = jnp.zeros((8, CP), F32)
    hs[0:8, :] = zero8
    hs[N12 + 8 : N12 + 16, :] = zero8
    as_[0:8, :] = zero8
    as_[N10 + 8 : N10 + 16, :] = zero8
    stack_weights(w1, c1, 1)
    stack_weights(w2, c2, 1)
    main = dot(ftm[...], small[0:64, :])
    west, east = dot(wl[...], small[0:64, :]), dot(wr[...], small[0:64, :])
    for r in range(12):
        at = 8 + r * ROW
        hs[at + 128 : at + ROW, :] = jnp.zeros((ROW - 128, CP), F32)
        hs[at : at + 2, :] = west[2 * r : 2 * r + 2]
        hs[at + 2 : at + 130, :] = main[r * 128 : r * 128 + 128]
        hs[at + 130 : at + 132, :] = east[2 * r : 2 * r + 2]
    for b in range(3):
        xcat[:, b * CP : (b + 1) * CP] = hs[7 + b : 7 + b + N12, :].astype(BF)
    col = lax.broadcasted_iota(I32, (ROW, CP), 0)
    col_mask = jnp.where(col == 1, flags[2], jnp.where(col == 130, flags[3], 1.0))
    root = 0.7978845608028654
    for part in range(5):
        z2 = taps(xcat, w1, part * 2 * ROW, 2 * ROW, 1)
        for q in range(2):
            r = part * 2 + q
            z = z2[q * ROW : (q + 1) * ROW]
            mask = col_mask
            if r == 0:
                mask = col_mask * flags[0]
            if r == 9:
                mask = col_mask * flags[1]
            zz = z * z
            t = jnp.tanh(root * z * (1.0 + 0.044715 * zz))
            half = 0.5 * (1.0 + t)
            slope = half + 0.5 * z * (1.0 - t * t) * (root * (1.0 + 3 * 0.044715 * zz))
            a1 = z * half * mask
            as_[8 + r * ROW : 8 + (r + 1) * ROW, :] = a1
            a1_out[r * ROW : (r + 1) * ROW, :] = a1.astype(BF)
            gp[r * ROW : (r + 1) * ROW, :] = (slope * mask).astype(BF)
    for b in range(3):
        acat[:, b * CP : (b + 1) * CP] = as_[7 + b : 7 + b + N10, :].astype(BF)
    for part in range(4):
        at = part * 2 * ROW
        h2 = hs[8 + 2 * ROW + at : 8 + 4 * ROW + at, :] + taps(acat, w2, at, 2 * ROW, 1)
        as_[at : at + 2 * ROW, :] = h2
    for r in range(8):
        h2c[r * 128 : r * 128 + 128, :] = as_[r * ROW + 2 : r * ROW + 130, :].astype(BF)
    field = dot(small[64:80, :], h2c[...], NT)
    tiles = [field[0:8, r * 128 : r * 128 + 128] for r in range(8)]
    top = tiles[0]
    for r in range(1, 8):
        top = jnp.maximum(jnp.abs(top), jnp.abs(tiles[r]))
    largest = jnp.maximum(jnp.max(jnp.abs(top)), 1e-30)
    up = 32000.0 / largest
    down = largest * (1.0 / 32000.0)
    for r in range(8):
        whole = jnp.round(tiles[r] * up).astype(I32)
        fq[r * 8 : r * 8 + 3, :] = pack_pair(whole[0:3], whole[3:6])
    pf[...] = jnp.zeros_like(pf)
    lane = lax.broadcasted_iota(I32, (8, 128), 1)

    def owners(ob, carry):
        rows = pl.ds(pl.multiple_of(ob * 8, 8), 8)
        live = lane < cnt[rows, 0:1]
        sums = [jnp.zeros((8, 128), F32)] * 6
        for k in range(4):
            index = cells[k, rows, :]
            low, high = index & 127, index >> 7
            weight = jnp.where(live, wts[k, rows, :] * down, 0.0)
            got = [jnp.zeros((8, 128), I32)] * 3
            for r in range(8):
                here = high == r
                got = [jnp.where(here, pick(fq, r * 8 + v, low), got[v]) for v in range(3)]
            for v in range(3):
                x, y = unpack_pair(got[v])
                sums[v] = sums[v] + weight * x
                sums[v + 3] = sums[v + 3] + weight * y
        for v in range(6):
            pf[pl.ds(ob * 64 + v, 8, stride=8), :] = sums[v]
        return carry

    lax.fori_loop(0, 16, owners, 0)
    out[...] = pf[...].astype(BF)


def turn_kernel(a1, ftm, wl, wr, small, a1t, h0t, wide, thin, pa, pt):
    wide[...] = a1[...].astype(F32)
    west, east = wl[...].astype(F32), wr[...].astype(F32)
    for r in range(12):
        at = r * ROW
        thin[at : at + 2, :] = west[2 * r : 2 * r + 2]
        thin[at + 2 : at + 130, :] = ftm[r * 128 : r * 128 + 128, :].astype(F32)
        thin[at + 130 : at + 132, :] = east[2 * r : 2 * r + 2]
    ones = lax.broadcasted_iota(I32, (CP, CP), 0) == lax.broadcasted_iota(I32, (CP, CP), 1)
    same = jnp.where(ones, 1.0, 0.0).astype(BF)
    win_t = dot(same[0:C, :], small[0:64, :], NT).astype(BF)
    for b in range(3):
        for r in range(10):
            at = slice(r * 128, r * 128 + 128)
            pa[at, :] = wide[r * ROW + 1 + b : r * ROW + 129 + b, :].astype(BF)
            pt[at, :] = thin[(r + 1) * ROW + 1 + b : (r + 1) * ROW + 129 + b, :].astype(BF)
        a1t[b * C : (b + 1) * C, :] = dot(same[0:C, :], pa[...], NT).astype(BF)
        h0t[b * C : (b + 1) * C, :] = dot(win_t, pt[...], NT).astype(BF)


def spread_row(row):
    return jnp.broadcast_to(row, (16, 128)).astype(BF)


def iotas(count):
    base = lax.broadcasted_iota(I32, (16, 128), 0)
    return [(base + 16 * m).astype(F32).astype(BF) for m in range(count)]


def owner_kernel(recv, obs, target, pred, loss, out, left, right, total, rq, gf):
    steps = iotas(8)
    none = jnp.zeros((16, 128), BF)
    one = jnp.ones((16, 128), BF)

    def collect(tb, carry):
        block = recv[pl.ds(pl.multiple_of(tb * 64, 64), 64), :].astype(F32)
        index = obs[pl.ds(pl.multiple_of(tb * 8, 8), 8), :]
        low = (index & 127).astype(F32)
        high = (index >> 7).astype(F32)
        for i in range(8):
            at = pl.ds(pl.multiple_of(tb * 1024 + i * 128, 128), 128)
            here = spread_row(high[i : i + 1]) == steps[0]
            for v in range(6):
                value = spread_row(block[i * 8 + v : i * 8 + v + 1])
                left[v * 16 : v * 16 + 16, at] = jnp.where(here, value, none)
            mine = spread_row(low[i : i + 1])
            for m in range(8):
                right[m * 16 : m * 16 + 16, at] = jnp.where(mine == steps[m], one, none)
        return carry

    lax.fori_loop(0, 16, collect, 0)
    total[...] = dot(left[...], right[...], NT)
    scale = 1.0 / (6 * 2048)
    squares = jnp.zeros((6, 128), F32)
    resids = []
    for h in range(16):
        at = slice(h * 128, h * 128 + 128)
        mine = total[pl.ds(h, 6, stride=16), :]
        pred[:, at] = mine
        resid = mine - target[:, at]
        squares = squares + resid * resid
        resids.append(resid * scale)
    loss[...] = jnp.full((16, 128), jnp.sum(squares) * (0.5 * scale), F32)
    top = jnp.abs(resids[0])
    for h in range(1, 16):
        top = jnp.maximum(top, jnp.abs(resids[h]))
    largest = jnp.maximum(jnp.max(top), 1e-30)
    up = 32000.0 / largest
    down = largest * (1.0 / 32000.0)
    for h in range(16):
        whole = jnp.round(resids[h] * up).astype(I32)
        rq[h * 8 : h * 8 + 3, :] = pack_pair(whole[0:3], whole[3:6])
    gf[...] = jnp.zeros_like(gf)

    def choose(tb, carry):
        index = obs[pl.ds(pl.multiple_of(tb * 8, 8), 8), :]
        low, high = index & 127, index >> 7
        got = [jnp.zeros((8, 128), I32)] * 3
        for h in range(16):
            here = high == h
            got = [jnp.where(here, pick(rq, h * 8 + v, low), got[v]) for v in range(3)]
        for v in range(3):
            x, y = unpack_pair(got[v])
            gf[pl.ds(tb * 64 + v, 8, stride=8), :] = x * down
            gf[pl.ds(tb * 64 + v + 3, 8, stride=8), :] = y * down
        return carry

    lax.fori_loop(0, 16, choose, 0)
    out[...] = gf[...].astype(BF)


def spread_kernel(grad, cells, wts, cnt, out, left, right, total):
    steps = iotas(4)
    none = jnp.zeros((16, 128), BF)
    total[...] = jnp.zeros_like(total)
    lane = lax.broadcasted_iota(I32, (8, 128), 1)

    def owners(ob, carry):
        rows = pl.ds(pl.multiple_of(ob * 8, 8), 8)
        live = lane < cnt[rows, 0:1]
        block = grad[pl.ds(pl.multiple_of(ob * 64, 64), 64), :].astype(F32)
        index = [cells[k, rows, :] for k in range(4)]
        low = [(i & 63).astype(F32) for i in index]
        high = [(i >> 6).astype(F32) for i in index]
        weight = [jnp.where(live, wts[k, rows, :], 0.0) for k in range(4)]
        for i in range(8):
            values = [spread_row(block[i * 8 + v : i * 8 + v + 1]) for v in range(6)]
            for k in range(4):
                at = slice((i * 4 + k) * 128, (i * 4 + k) * 128 + 128)
                here = spread_row(high[k][i : i + 1]) == steps[0]
                for v in range(6):
                    left[v * 16 : v * 16 + 16, at] = jnp.where(here, values[v], none)
                mine = spread_row(low[k][i : i + 1])
                amount = spread_row(weight[k][i : i + 1])
                for m in range(4):
                    right[m * 16 : m * 16 + 16, at] = jnp.where(mine == steps[m], amount, none)
        total[...] += dot(left[...], right[...], NT)
        return carry

    lax.fori_loop(0, 16, owners, 0)
    out[...] = jnp.zeros_like(out)
    for r in range(8):
        even = total[pl.ds(2 * r, 6, stride=16), :]
        odd = total[pl.ds(2 * r + 1, 6, stride=16), :]
        out[r * 8 : r * 8 + 6, :] = jnp.concatenate([even, odd], 1)


def backward_kernel(
    core, gf, et, gl, gr, fm, a1t, h0t, gp, h2c, c2, c1, small, loss, pay, gfields, es, bw, gs,
    g2cat, zs, gzcat, w2, w1, gc,
):
    zero8 = jnp.zeros((8, CP), F32)
    gs[0:8, :] = zero8
    gs[N12 + 8 : N12 + 16, :] = zero8
    zs[0:8, :] = zero8
    zs[N10 + 8 : N10 + 16, :] = zero8
    stack_weights(w2, c2, -1)
    stack_weights(w1, c1, -1)
    base_s = pl.multiple_of(core[0] * HALF, 16)
    base_f = pl.multiple_of((1 - core[0]) * HALF, 16)

    def put(base, at, value):
        pay[pl.ds(pl.multiple_of(base + at, 16), value.shape[0]), :] = value.astype(BF)

    def put_taps(base, turned):
        for a in range(3):
            y = dot(turned[:, a * 128 : a * 128 + 1024], gc[...])
            for b in range(3):
                tap = a * 3 + b
                mine = y[b * C : (b + 1) * C]
                put(base, tap * C, mine[:, 0:128])
                rest = mine[:, 128:256]
                put(base, REST + tap * 96, rest[0:96] + pltpu.roll(rest[96:192], 64, 1))

    es[...] = jnp.zeros_like(es)
    es[2:130, 0:96] = et[...]
    es[0:2, 0:96] = gl[...]
    es[130:132, 0:96] = gr[...]
    bw[...] = jnp.zeros_like(bw)
    for r in range(12):
        at, block = (r // 2) * 16, small[64 + 16 * (r % 2) : 80 + 16 * (r % 2), :]
        bw[at : at + 16, r * CP : (r + 1) * CP] = block
        bw[128 + at : 144 + at, r * CP : (r + 1) * CP] = block
    x = es[...]
    x_hi = x.astype(BF)
    x_lo = (x - x_hi.astype(F32)).astype(BF)
    both = jnp.concatenate([x_hi, x_lo], 1)
    for r in range(12):
        gs[8 + r * ROW : 8 + (r + 1) * ROW, :] = dot(both, bw[:, r * CP : (r + 1) * CP])
    for b in range(3):
        g2cat[:, b * CP : (b + 1) * CP] = gs[9 - b : 9 - b + N12, :].astype(BF)
    for r in range(8):
        at = 8 + (r + 2) * ROW + 2
        gc[r * 128 : r * 128 + 128, :] = gs[at : at + 128, :].astype(BF)
    put_taps(base_s, a1t)
    for part in range(5):
        at = part * 2 * ROW
        g = taps(g2cat, w2, at, 2 * ROW, -1)
        zs[8 + at : 8 + at + 2 * ROW, :] = g * gp[at : at + 2 * ROW, :].astype(F32)
    for b in range(3):
        gzcat[:, b * CP : (b + 1) * CP] = zs[9 - b : 9 - b + N10, :].astype(BF)
    for r in range(8):
        at = 8 + (r + 1) * ROW + 2
        gc[r * 128 : r * 128 + 128, :] = zs[at : at + 128, :].astype(BF)
    put_taps(base_f, h0t)
    for part in range(4):
        at = 8 + 2 * ROW + part * 2 * ROW
        gs[at : at + 2 * ROW, :] = gs[at : at + 2 * ROW, :] + taps(
            gzcat, w1, part * 2 * ROW, 2 * ROW, -1
        )
    for r in range(8):
        at = 8 + (r + 2) * ROW + 2
        gc[r * 128 : r * 128 + 128, :] = gs[at : at + 128, :].astype(BF)
    g_in = dot(fm[...], gc[...])
    g_fields = dot(small[0:64, :], gc[...], NT)
    for r in range(8):
        gfields[pl.ds(r, 64, stride=8), :] = g_fields[:, r * 128 : r * 128 + 128]
    line = jnp.concatenate([gf[r * 8 : r * 8 + 8, :] for r in range(8)], 1)
    line_hi = line.astype(BF).astype(F32)
    line2 = jnp.concatenate([line_hi, line - line_hi], 0).astype(BF)
    g_out = dot(line2, h2c[...])
    g_out = g_out[0:8] + g_out[8:16]
    put(base_s, EXTRA, g_in[:, 0:128])
    rest = g_in[:, 128:256]
    put(base_s, EXTRA + 64, rest[0:32] + pltpu.roll(rest[32:64], 64, 1))
    put(base_s, EXTRA + 96, jnp.zeros((HALF - EXTRA - 96, 128), F32))
    put(base_f, EXTRA, jnp.concatenate([g_out[:, 0:128], g_out[:, 128:256]], 0))
    put(base_f, EXTRA + 16, loss[...])
    put(base_f, EXTRA + 32, jnp.zeros((HALF - EXTRA - 32, 128), F32))


def unpack_kernel(core, mine, other, second, first, g_in, g_out, loss):
    def unpack(source, kernel):
        for tap in range(9):
            a, b = tap // 3, tap % 3
            kernel[a, b, :, 0:128] = source[tap * C : (tap + 1) * C, :].astype(F32)
            rest = source[REST + tap * 96 : REST + tap * 96 + 96, :].astype(F32)
            kernel[a, b, 0:96, 128:C] = rest[:, 0:64]
            kernel[a, b, 96:C, 128:C] = pltpu.roll(rest, 64, 1)[:, 0:64]

    def both(s, f):
        unpack(s, second)
        unpack(f, first)
        g_in[:, 0:128] = s[EXTRA : EXTRA + 64, :].astype(F32)
        rest = s[EXTRA + 64 : EXTRA + 96, :].astype(F32)
        g_in[0:32, 128:C] = rest[:, 0:64]
        g_in[32:64, 128:C] = pltpu.roll(rest, 64, 1)[:, 0:64]
        extra = f[EXTRA : EXTRA + 32, :].astype(F32)
        g_out[:, 0:128] = extra[0:8]
        g_out[:, 128:256] = extra[8:16]
        loss[...] = extra[16:24]

    @pl.when(core[0] == 0)
    def _():
        both(mine, other)

    @pl.when(core[0] == 1)
    def _():
        both(other, mine)


def shift_pair(last, first, axis):
    count = lax.axis_size(axis)
    up = [(i, i + 1) for i in range(count - 1)]
    down = [(j, i) for i, j in up]
    return lax.ppermute(last, axis, up), lax.ppermute(first, axis, down)


def exchange(rows, groups=None):
    return lax.all_to_all(
        rows, AXES, split_axis=0, concat_axis=0, tiled=True, axis_index_groups=groups
    )


def call(kernel, out_shapes, scratch, *operands, smem=0, vmem=60, flops=0):
    specs = [pl.BlockSpec(memory_space=pltpu.SMEM)] * smem + [
        pl.BlockSpec(memory_space=pltpu.VMEM)
    ] * (len(operands) - smem)
    return pl.pallas_call(
        kernel,
        out_shape=[jax.ShapeDtypeStruct(s, d) for s, d in out_shapes],
        in_specs=specs,
        out_specs=[pl.BlockSpec(memory_space=pltpu.VMEM)] * len(out_shapes),
        scratch_shapes=[pltpu.VMEM(s, d) for s, d in scratch],
        compiler_params=pltpu.CompilerParams(vmem_limit_bytes=vmem * 1024 * 1024),
        cost_estimate=pl.CostEstimate(flops=flops, bytes_accessed=4_000_000, transcendentals=0),
    )(*operands)


def on_device(
    fields,
    w_in,
    conv_first,
    conv_second,
    w_out,
    slot_cells,
    slot_weights,
    slot_count,
    recv_obs,
    targets,
):
    ns, ew = lax.axis_index("ns"), lax.axis_index("ew")
    n_ns, n_ew = lax.axis_size("ns"), lax.axis_size("ew")
    flags = jnp.stack([ns > 0, ns < n_ns - 1, ew > 0, ew < n_ew - 1]).astype(F32)
    core = (ns % 2).astype(I32).reshape(1)
    cells = slot_cells.reshape(4, 128, CAP)
    wts = slot_weights.reshape(4, 128, CAP)
    cnt = slot_count.reshape(128, 1)
    obs = recv_obs.reshape(128, CAP)
    turned = w_out.T
    small = jnp.concatenate(
        [w_in, jnp.pad(turned, ((0, 10), (0, 0))), jnp.pad(turned, ((8, 2), (0, 0)))], 0
    )
    small = jnp.pad(small, ((0, 0), (0, CP - C)))

    north, south = shift_pair(
        fields[:, 6:8].reshape(128, 128), fields[:, 0:2].reshape(128, 128), "ns"
    )
    ftm, fm, first, last = call(
        fields_kernel,
        [((12 * 128, 64), BF), ((64, 1024), BF), ((32, 64), BF), ((32, 64), BF)],
        [((512, 128), F32), ((128, 128), F32), ((128, 128), F32), ((32, 64), F32), ((32, 64), F32)],
        fields.reshape(512, 128), north, south,
        vmem=8,
    )
    west, east = shift_pair(last, first, "ew")
    sent, a1, gp, h2c = call(
        forward_kernel,
        [((1024, 128), BF), ((N10, CP), BF), ((N10, CP), BF), ((1024, CP), BF)],
        [
            ((N12 + 16, CP), F32), ((N12, 3 * CP), BF), ((N10 + 16, CP), F32),
            ((N10, 3 * CP), BF), ((3, 3 * CP, CP), BF), ((3, 3 * CP, CP), BF),
            ((64, 128), I32), ((1024, 128), F32),
        ],
        flags, ftm, west, east, small, conv_first, conv_second, cells, wts, cnt,
        smem=1, vmem=28, flops=2 * 10**9,
    )
    received = exchange(sent)
    a1t, h0t = call(
        turn_kernel,
        [((3 * C, 1280), BF), ((3 * C, 1280), BF)],
        [((N10, CP), F32), ((N12, 64), F32), ((1280, CP), BF), ((1280, 64), BF)],
        a1, ftm, west, east, small,
        vmem=16, flops=10**9,
    )
    pred, loss, back = call(
        owner_kernel,
        [((6, 2048), F32), ((16, 128), F32), ((1024, 128), BF)],
        [
            ((96, 16384), BF), ((128, 16384), BF), ((96, 128), F32), ((128, 128), I32),
            ((1024, 128), F32),
        ],
        received, obs, targets,
        vmem=16, flops=10**9,
    )
    grads = exchange(back)
    (g_field,) = call(
        spread_kernel,
        [((64, 128), F32)],
        [((96, 4096), BF), ((64, 4096), BF), ((96, 64), F32)],
        grads, cells, wts, cnt,
        vmem=12, flops=10**9,
    )
    north, south = shift_pair(g_field[48:64], g_field[0:16], "ns")
    et, first, last = call(
        turn_field_kernel,
        [((128, 96), F32), ((2, 96), F32), ((2, 96), F32)],
        [],
        g_field, north, south,
        vmem=4,
    )
    g_west, g_east = shift_pair(last, first, "ew")
    pay, g_fields = call(
        backward_kernel,
        [((2 * HALF, 128), BF), ((512, 128), F32)],
        [
            ((ROW, 128), F32), ((CP, 12 * CP), BF), ((N12 + 16, CP), F32), ((N12, 3 * CP), BF),
            ((N10 + 16, CP), F32), ((N10, 3 * CP), BF), ((3, CP, 3 * CP), BF),
            ((3, CP, 3 * CP), BF), ((1024, CP), BF),
        ],
        core, g_field, et, g_west, g_east, fm, a1t, h0t, gp, h2c, conv_second, conv_first, small,
        loss,
        smem=1, vmem=28, flops=2 * 10**9,
    )
    pairs = [(n, n + 1 - 2 * (n % 2)) for n in range(n_ns)]
    groups = [[n * n_ew + e for n in range(c, n_ns, 2) for e in range(n_ew)] for c in range(2)]
    theirs = lax.ppermute(pay[HALF:], "ns", pairs)
    summed = (pay[:HALF].astype(F32) + theirs.astype(F32)).astype(BF).reshape(64, PIECE, 128)
    share = jnp.sum(exchange(summed, groups).astype(F32), axis=0).astype(BF)
    mine = exchange(jnp.broadcast_to(share[None], (64, PIECE, 128)), groups).reshape(HALF, 128)
    other = lax.ppermute(mine, "ns", pairs)
    grad_second, grad_first, grad_in, g_out, total = call(
        unpack_kernel,
        [((3, 3, C, C), F32), ((3, 3, C, C), F32), ((64, C), F32), ((8, CP), F32), ((8, 128), F32)],
        [],
        core, mine, other,
        smem=1, vmem=16,
    )
    return (
        pred,
        total[0, 0],
        grad_first,
        grad_second,
        grad_in,
        g_out[:6, :C].T,
        g_fields.reshape(64, TH, TW),
    )


def solution(mesh):
    in_specs = (
        P(None, "ns", "ew"),
        P(),
        P(),
        P(),
        P(),
        P(("ns", "ew"), None, None),
        P(("ns", "ew"), None, None),
        P(("ns", "ew"), None),
        P(("ns", "ew"), None),
        P(None, ("ns", "ew")),
    )
    out_specs = (P(None, ("ns", "ew")), P(), P(), P(), P(), P(), P(None, "ns", "ew"))
    return jax.shard_map(
        on_device, mesh=mesh, in_specs=in_specs, out_specs=out_specs, check_vma=False
    )
```

```python
import jax
import jax.numpy as jnp
from jax import lax
from jax.experimental import pallas as pl
from jax.experimental.pallas import tpu as pltpu
from jax.sharding import PartitionSpec as P

BF = jnp.bfloat16
F32 = jnp.float32
I32 = jnp.int32
CAP = 128
TH, TW = 8, 128
C = 192
ROW = 144
N12, N10, N8 = 12 * ROW, 10 * ROW, 8 * ROW
CP = 256
AXES = ("ns", "ew")
PIECE = 48
HALF = 64 * PIECE
REST = 1728
EXTRA = 2592
NT = (((1,), (1,)), ((), ()))
TN = (((0,), (0,)), ((), ()))


def dot(x, y, dims=(((1,), (0,)), ((), ()))):
    return lax.dot_general(x, y, dims, preferred_element_type=F32)


def taps(cat, weight, first, count, order):
    total = None
    for a in range(3):
        start = (a if order > 0 else 2 - a) * ROW + first
        rows = cat[start : start + count, :]
        term = dot(rows, weight[a]) if order > 0 else dot(rows, weight[a], NT)
        total = term if total is None else total + term
    return total


def stack_weights(out, kernel, order):
    out[...] = jnp.zeros_like(out)
    for a in range(3):
        for b in range(3):
            if order > 0:
                out[a, b * CP : b * CP + C, 0:C] = kernel[a, b]
            else:
                out[a, 0:C, b * CP : b * CP + C] = kernel[a, b]


def pick(table, row, index):
    return jnp.take_along_axis(
        jnp.broadcast_to(table[row : row + 1, :], (8, 128)),
        index,
        axis=1,
        mode="promise_in_bounds",
    )


def pack_pair(x, y):
    return x * 65536 + (y + 32768)


def unpack_pair(word):
    return (word >> 16).astype(F32), ((word & 65535) - 32768).astype(F32)


def ordered(odd, x, y):
    return jnp.where(odd > 0, x, y), jnp.where(odd > 0, y, x)


def fields_kernel(flags, f8, swap1, swap2, ftm, fm, out1, out2, s8, sn, ss, sw, se):
    s8[...] = f8[...].astype(F32)
    sn[...], ss[...] = ordered(flags[4], swap1[...].astype(F32), swap2[...].astype(F32))
    sw[...] = jnp.zeros_like(sw)
    se[...] = jnp.zeros_like(se)
    for r in range(12):
        if r < 2:
            block = sn[pl.ds(r, 64, stride=2), :]
        elif r < 10:
            block = s8[pl.ds(r - 2, 64, stride=8), :]
            fm[:, (r - 2) * 128 : (r - 1) * 128] = block.astype(BF)
        else:
            block = ss[pl.ds(r - 10, 64, stride=2), :]
        turned = block.T
        ftm[r * 128 : r * 128 + 128, :] = turned.astype(BF)
        sw[2 * r : 2 * r + 2, :] = turned[0:2]
        se[2 * r : 2 * r + 2, :] = turned[126:128]
    one, two = ordered(flags[5], sw[...], se[...])
    out1[...] = one.astype(BF)
    out2[...] = two.astype(BF)


def turn_field_kernel(flags, gf, swap1, swap2, et, out1, out2):
    north, south = ordered(flags[4], swap1[...], swap2[...])
    turned = jnp.concatenate([north, gf[...], south], 0).T
    et[...] = turned
    out1[...], out2[...] = ordered(flags[5], turned[0:2], turned[126:128])


def forward_kernel(
    flags, ftm, swap1, swap2, small, c1, c2, cells, wts, cnt, out, a1_out, gp, h2c, hs, xcat, as_, acat,
    w1, w2, fq, pf,
):
    zero8 = jnp.zeros((8, CP), F32)
    hs[0:8, :] = zero8
    hs[N12 + 8 : N12 + 16, :] = zero8
    as_[0:8, :] = zero8
    as_[N10 + 8 : N10 + 16, :] = zero8
    stack_weights(w1, c1, 1)
    stack_weights(w2, c2, 1)
    main = dot(ftm[...], small[0:64, :])
    west, east = ordered(
        flags[5], dot(swap1[...], small[0:64, :]), dot(swap2[...], small[0:64, :])
    )
    for r in range(12):
        at = 8 + r * ROW
        hs[at + 128 : at + ROW, :] = jnp.zeros((ROW - 128, CP), F32)
        hs[at : at + 2, :] = west[2 * r : 2 * r + 2]
        hs[at + 2 : at + 130, :] = main[r * 128 : r * 128 + 128]
        hs[at + 130 : at + 132, :] = east[2 * r : 2 * r + 2]
    for b in range(3):
        xcat[:, b * CP : (b + 1) * CP] = hs[7 + b : 7 + b + N12, :].astype(BF)
    col = lax.broadcasted_iota(I32, (ROW, CP), 0)
    col_mask = jnp.where(col == 1, flags[2], jnp.where(col == 130, flags[3], 1.0))
    root = 0.7978845608028654
    for part in range(5):
        z2 = taps(xcat, w1, part * 2 * ROW, 2 * ROW, 1)
        for q in range(2):
            r = part * 2 + q
            z = z2[q * ROW : (q + 1) * ROW]
            mask = col_mask
            if r == 0:
                mask = col_mask * flags[0]
            if r == 9:
                mask = col_mask * flags[1]
            zz = z * z
            t = jnp.tanh(root * z * (1.0 + 0.044715 * zz))
            half = 0.5 * (1.0 + t)
            slope = half + 0.5 * z * (1.0 - t * t) * (root * (1.0 + 3 * 0.044715 * zz))
            a1 = z * half * mask
            as_[8 + r * ROW : 8 + (r + 1) * ROW, :] = a1
            a1_out[r * ROW : (r + 1) * ROW, :] = a1.astype(BF)
            gp[r * ROW : (r + 1) * ROW, :] = (slope * mask).astype(BF)
    for b in range(3):
        acat[:, b * CP : (b + 1) * CP] = as_[7 + b : 7 + b + N10, :].astype(BF)
    for part in range(4):
        at = part * 2 * ROW
        h2 = hs[8 + 2 * ROW + at : 8 + 4 * ROW + at, :] + taps(acat, w2, at, 2 * ROW, 1)
        as_[at : at + 2 * ROW, :] = h2
    for r in range(8):
        h2c[r * 128 : r * 128 + 128, :] = as_[r * ROW + 2 : r * ROW + 130, :].astype(BF)
    field = dot(small[64:80, :], h2c[...], NT)
    tiles = [field[0:8, r * 128 : r * 128 + 128] for r in range(8)]
    top = tiles[0]
    for r in range(1, 8):
        top = jnp.maximum(jnp.abs(top), jnp.abs(tiles[r]))
    largest = jnp.maximum(jnp.max(jnp.abs(top)), 1e-30)
    up = 32000.0 / largest
    down = largest * (1.0 / 32000.0)
    for r in range(8):
        whole = jnp.round(tiles[r] * up).astype(I32)
        fq[r * 8 : r * 8 + 3, :] = pack_pair(whole[0:3], whole[3:6])
    pf[...] = jnp.zeros_like(pf)
    lane = lax.broadcasted_iota(I32, (8, 128), 1)

    def owners(ob, carry):
        rows = pl.ds(pl.multiple_of(ob * 8, 8), 8)
        live = lane < cnt[rows, 0:1]
        sums = [jnp.zeros((8, 128), F32)] * 6
        for k in range(4):
            index = cells[k, rows, :]
            low, high = index & 127, index >> 7
            weight = jnp.where(live, wts[k, rows, :] * down, 0.0)
            got = [jnp.zeros((8, 128), I32)] * 3
            for r in range(8):
                here = high == r
                got = [jnp.where(here, pick(fq, r * 8 + v, low), got[v]) for v in range(3)]
            for v in range(3):
                x, y = unpack_pair(got[v])
                sums[v] = sums[v] + weight * x
                sums[v + 3] = sums[v + 3] + weight * y
        for v in range(6):
            pf[pl.ds(ob * 64 + v, 8, stride=8), :] = sums[v]
        return carry

    lax.fori_loop(0, 16, owners, 0)
    out[...] = pf[...].astype(BF)


def turn_kernel(flags, a1, ftm, swap1, swap2, small, a1t, h0t, wide, thin, pa, pt):
    wide[...] = a1[...].astype(F32)
    west, east = ordered(flags[5], swap1[...].astype(F32), swap2[...].astype(F32))
    for r in range(12):
        at = r * ROW
        thin[at : at + 2, :] = west[2 * r : 2 * r + 2]
        thin[at + 2 : at + 130, :] = ftm[r * 128 : r * 128 + 128, :].astype(F32)
        thin[at + 130 : at + 132, :] = east[2 * r : 2 * r + 2]
    ones = lax.broadcasted_iota(I32, (CP, CP), 0) == lax.broadcasted_iota(I32, (CP, CP), 1)
    same = jnp.where(ones, 1.0, 0.0).astype(BF)
    win_t = dot(same[0:C, :], small[0:64, :], NT).astype(BF)
    for b in range(3):
        for r in range(10):
            at = slice(r * 128, r * 128 + 128)
            pa[at, :] = wide[r * ROW + 1 + b : r * ROW + 129 + b, :].astype(BF)
            pt[at, :] = thin[(r + 1) * ROW + 1 + b : (r + 1) * ROW + 129 + b, :].astype(BF)
        a1t[b * C : (b + 1) * C, :] = dot(same[0:C, :], pa[...], NT).astype(BF)
        h0t[b * C : (b + 1) * C, :] = dot(win_t, pt[...], NT).astype(BF)


def spread_row(row):
    return jnp.broadcast_to(row, (16, 128)).astype(BF)


def iotas(count):
    base = lax.broadcasted_iota(I32, (16, 128), 0)
    return [(base + 16 * m).astype(F32).astype(BF) for m in range(count)]


def overlapped(count, build, multiply):
    build(0, 0)

    def step(i, carry):
        build(2 * i + 1, 1)
        multiply(0)
        build(jnp.minimum(2 * i + 2, count - 1), 0)
        multiply(1)
        return carry

    lax.fori_loop(0, count // 2, step, 0)


def owner_kernel(recv, obs, target, pred, loss, out, l0, l1, r0, r1, total, rq, gf):
    steps = iotas(8)
    none = jnp.zeros((16, 128), BF)
    one = jnp.ones((16, 128), BF)
    lefts, rights = (l0, l1), (r0, r1)

    def collect(tb, slot):
        left, right = lefts[slot], rights[slot]
        block = recv[pl.ds(pl.multiple_of(tb * 64, 64), 64), :].astype(F32)
        index = obs[pl.ds(pl.multiple_of(tb * 8, 8), 8), :]
        low = (index & 127).astype(F32)
        high = (index >> 7).astype(F32)
        for i in range(8):
            at = slice(i * 128, i * 128 + 128)
            here = spread_row(high[i : i + 1]) == steps[0]
            for v in range(6):
                value = spread_row(block[i * 8 + v : i * 8 + v + 1])
                left[v * 16 : v * 16 + 16, at] = jnp.where(here, value, none)
            mine = spread_row(low[i : i + 1])
            for m in range(8):
                right[m * 16 : m * 16 + 16, at] = jnp.where(mine == steps[m], one, none)

    def multiply(slot):
        total[...] += dot(lefts[slot][...], rights[slot][...], NT)

    total[...] = jnp.zeros_like(total)
    overlapped(16, collect, multiply)
    scale = 1.0 / (6 * 2048)
    squares = jnp.zeros((6, 128), F32)
    resids = []
    for h in range(16):
        at = slice(h * 128, h * 128 + 128)
        mine = total[pl.ds(h, 6, stride=16), :]
        pred[:, at] = mine
        resid = mine - target[:, at]
        squares = squares + resid * resid
        resids.append(resid * scale)
    loss[...] = jnp.full((16, 128), jnp.sum(squares) * (0.5 * scale), F32)
    top = jnp.abs(resids[0])
    for h in range(1, 16):
        top = jnp.maximum(top, jnp.abs(resids[h]))
    largest = jnp.maximum(jnp.max(top), 1e-30)
    up = 32000.0 / largest
    down = largest * (1.0 / 32000.0)
    for h in range(16):
        whole = jnp.round(resids[h] * up).astype(I32)
        rq[h * 8 : h * 8 + 3, :] = pack_pair(whole[0:3], whole[3:6])
    gf[...] = jnp.zeros_like(gf)

    def choose(tb, carry):
        index = obs[pl.ds(pl.multiple_of(tb * 8, 8), 8), :]
        low, high = index & 127, index >> 7
        got = [jnp.zeros((8, 128), I32)] * 3
        for h in range(16):
            here = high == h
            got = [jnp.where(here, pick(rq, h * 8 + v, low), got[v]) for v in range(3)]
        for v in range(3):
            x, y = unpack_pair(got[v])
            gf[pl.ds(tb * 64 + v, 8, stride=8), :] = x * down
            gf[pl.ds(tb * 64 + v + 3, 8, stride=8), :] = y * down
        return carry

    lax.fori_loop(0, 16, choose, 0)
    out[...] = gf[...].astype(BF)


def spread_kernel(
    flags, grad, cells, wts, cnt, out, out1, out2, l0, l1, r0, r1, total
):
    lefts, rights = (l0, l1), (r0, r1)
    steps = iotas(4)
    none = jnp.zeros((16, 128), BF)
    total[...] = jnp.zeros_like(total)
    lane = lax.broadcasted_iota(I32, (8, 128), 1)

    def owners(ob, slot):
        left, right = lefts[slot], rights[slot]
        rows = pl.ds(pl.multiple_of(ob * 8, 8), 8)
        live = lane < cnt[rows, 0:1]
        block = grad[pl.ds(pl.multiple_of(ob * 64, 64), 64), :].astype(F32)
        index = [cells[k, rows, :] for k in range(4)]
        low = [(i & 63).astype(F32) for i in index]
        high = [(i >> 6).astype(F32) for i in index]
        weight = [jnp.where(live, wts[k, rows, :], 0.0) for k in range(4)]
        for i in range(8):
            values = [spread_row(block[i * 8 + v : i * 8 + v + 1]) for v in range(6)]
            for k in range(4):
                at = slice((i * 4 + k) * 128, (i * 4 + k) * 128 + 128)
                here = spread_row(high[k][i : i + 1]) == steps[0]
                for v in range(6):
                    left[v * 16 : v * 16 + 16, at] = jnp.where(here, values[v], none)
                mine = spread_row(low[k][i : i + 1])
                amount = spread_row(weight[k][i : i + 1])
                for m in range(4):
                    right[m * 16 : m * 16 + 16, at] = jnp.where(mine == steps[m], amount, none)

    def multiply(slot):
        total[...] += dot(lefts[slot][...], rights[slot][...], NT)

    overlapped(16, owners, multiply)
    out[...] = jnp.zeros_like(out)
    for r in range(8):
        even = total[pl.ds(2 * r, 6, stride=16), :]
        odd = total[pl.ds(2 * r + 1, 6, stride=16), :]
        out[r * 8 : r * 8 + 6, :] = jnp.concatenate([even, odd], 1)
    out1[...], out2[...] = ordered(flags[4], out[0:16, :], out[48:64, :])


def backward_kernel(
    flags, gf, et, swap1, swap2, fm, a1t, h0t, gp, h2c, c2, c1, small, loss, pay, gfields, es, bw,
    gs, g2cat, zs, gzcat, gc, w2, w1,
):
    zero8 = jnp.zeros((8, CP), F32)
    gs[0:8, :] = zero8
    gs[N12 + 8 : N12 + 16, :] = zero8
    zs[0:8, :] = zero8
    zs[N10 + 8 : N10 + 16, :] = zero8
    stack_weights(w2, c2, -1)
    stack_weights(w1, c1, -1)
    core = (flags[4] > 0).astype(I32)
    base_s = pl.multiple_of(core * HALF, 16)
    base_f = pl.multiple_of((1 - core) * HALF, 16)

    def put(base, at, value):
        pay[pl.ds(pl.multiple_of(base + at, 16), value.shape[0]), :] = value.astype(BF)

    def put_taps(base, turned):
        for a in range(3):
            y = dot(turned[:, a * 128 : a * 128 + 1024], gc[...])
            for b in range(3):
                tap = a * 3 + b
                mine = y[b * C : (b + 1) * C]
                put(base, tap * C, mine[:, 0:128])
                rest = mine[:, 128:256]
                put(base, REST + tap * 96, rest[0:96] + pltpu.roll(rest[96:192], 64, 1))

    es[...] = jnp.zeros_like(es)
    es[2:130, 0:96] = et[...]
    es[0:2, 0:96], es[130:132, 0:96] = ordered(flags[5], swap1[...], swap2[...])
    bw[...] = jnp.zeros_like(bw)
    for r in range(12):
        at, block = (r // 2) * 16, small[64 + 16 * (r % 2) : 80 + 16 * (r % 2), :]
        bw[at : at + 16, r * CP : (r + 1) * CP] = block
        bw[128 + at : 144 + at, r * CP : (r + 1) * CP] = block
    x = es[...]
    x_hi = x.astype(BF)
    x_lo = (x - x_hi.astype(F32)).astype(BF)
    both = jnp.concatenate([x_hi, x_lo], 1)
    for r in range(12):
        gs[8 + r * ROW : 8 + (r + 1) * ROW, :] = dot(both, bw[:, r * CP : (r + 1) * CP])
    for b in range(3):
        g2cat[:, b * CP : (b + 1) * CP] = gs[9 - b : 9 - b + N12, :].astype(BF)
    for r in range(8):
        at = 8 + (r + 2) * ROW + 2
        gc[r * 128 : r * 128 + 128, :] = gs[at : at + 128, :].astype(BF)
    put_taps(base_s, a1t)
    for part in range(5):
        at = part * 2 * ROW
        g = taps(g2cat, w2, at, 2 * ROW, -1)
        zs[8 + at : 8 + at + 2 * ROW, :] = g * gp[at : at + 2 * ROW, :].astype(F32)
    for b in range(3):
        gzcat[:, b * CP : (b + 1) * CP] = zs[9 - b : 9 - b + N10, :].astype(BF)
    for r in range(8):
        at = 8 + (r + 1) * ROW + 2
        gc[r * 128 : r * 128 + 128, :] = zs[at : at + 128, :].astype(BF)
    put_taps(base_f, h0t)
    for part in range(4):
        at = 8 + 2 * ROW + part * 2 * ROW
        gs[at : at + 2 * ROW, :] = gs[at : at + 2 * ROW, :] + taps(
            gzcat, w1, part * 2 * ROW, 2 * ROW, -1
        )
    for r in range(8):
        at = 8 + (r + 2) * ROW + 2
        gc[r * 128 : r * 128 + 128, :] = gs[at : at + 128, :].astype(BF)
    g_in = dot(fm[...], gc[...])
    g_fields = dot(small[0:64, :], gc[...], NT)
    for r in range(8):
        gfields[pl.ds(r, 64, stride=8), :] = g_fields[:, r * 128 : r * 128 + 128]
    line = jnp.concatenate([gf[r * 8 : r * 8 + 8, :] for r in range(8)], 1)
    line_hi = line.astype(BF).astype(F32)
    line2 = jnp.concatenate([line_hi, line - line_hi], 0).astype(BF)
    g_out = dot(line2, h2c[...])
    g_out = g_out[0:8] + g_out[8:16]
    put(base_s, EXTRA, g_in[:, 0:128])
    rest = g_in[:, 128:256]
    put(base_s, EXTRA + 64, rest[0:32] + pltpu.roll(rest[32:64], 64, 1))
    put(base_s, EXTRA + 96, jnp.zeros((HALF - EXTRA - 96, 128), F32))
    put(base_f, EXTRA, jnp.concatenate([g_out[:, 0:128], g_out[:, 128:256]], 0))
    put(base_f, EXTRA + 16, loss[...])
    put(base_f, EXTRA + 32, jnp.zeros((HALF - EXTRA - 32, 128), F32))


def unpack_kernel(flags, mine, other, second, first, g_in, g_out, loss):
    def unpack(source, kernel):
        for tap in range(9):
            a, b = tap // 3, tap % 3
            kernel[a, b, :, 0:128] = source[tap * C : (tap + 1) * C, :].astype(F32)
            rest = source[REST + tap * 96 : REST + tap * 96 + 96, :].astype(F32)
            kernel[a, b, 0:96, 128:C] = rest[:, 0:64]
            kernel[a, b, 96:C, 128:C] = pltpu.roll(rest, 64, 1)[:, 0:64]

    def both(s, f):
        unpack(s, second)
        unpack(f, first)
        g_in[:, 0:128] = s[EXTRA : EXTRA + 64, :].astype(F32)
        rest = s[EXTRA + 64 : EXTRA + 96, :].astype(F32)
        g_in[0:32, 128:C] = rest[:, 0:64]
        g_in[32:64, 128:C] = pltpu.roll(rest, 64, 1)[:, 0:64]
        extra = f[EXTRA : EXTRA + 32, :].astype(F32)
        g_out[:, 0:128] = extra[0:8]
        g_out[:, 128:256] = extra[8:16]
        loss[...] = extra[16:24]

    @pl.when(flags[4] == 0)
    def _():
        both(mine, other)

    @pl.when(flags[4] > 0)
    def _():
        both(other, mine)


def swaps(one, two, axis):
    count = lax.axis_size(axis)
    pairs = [[(i, i + 1) for i in range(start, count - 1, 2)] for start in range(2)]
    return tuple(
        lax.ppermute(x, axis, p + [(j, i) for i, j in p]) for x, p in zip((one, two), pairs)
    )


def exchange(rows, groups=None):
    return lax.all_to_all(
        rows, AXES, split_axis=0, concat_axis=0, tiled=True, axis_index_groups=groups
    )


def call(kernel, out_shapes, scratch, *operands, smem=0, vmem=60, flops=0):
    specs = [pl.BlockSpec(memory_space=pltpu.SMEM)] * smem + [
        pl.BlockSpec(memory_space=pltpu.VMEM)
    ] * (len(operands) - smem)
    return pl.pallas_call(
        kernel,
        out_shape=[jax.ShapeDtypeStruct(s, d) for s, d in out_shapes],
        in_specs=specs,
        out_specs=[pl.BlockSpec(memory_space=pltpu.VMEM)] * len(out_shapes),
        scratch_shapes=[pltpu.VMEM(s, d) for s, d in scratch],
        compiler_params=pltpu.CompilerParams(vmem_limit_bytes=vmem * 1024 * 1024),
        cost_estimate=pl.CostEstimate(flops=flops, bytes_accessed=4_000_000, transcendentals=0),
    )(*operands)


def on_device(
    fields,
    w_in,
    conv_first,
    conv_second,
    w_out,
    slot_cells,
    slot_weights,
    slot_count,
    recv_obs,
    targets,
):
    ns, ew = lax.axis_index("ns"), lax.axis_index("ew")
    n_ns, n_ew = lax.axis_size("ns"), lax.axis_size("ew")
    flags = jnp.stack(
        [ns > 0, ns < n_ns - 1, ew > 0, ew < n_ew - 1, (ns & 1) > 0, (ew & 1) > 0]
    ).astype(F32)
    cells = slot_cells.reshape(4, 128, CAP)
    wts = slot_weights.reshape(4, 128, CAP)
    cnt = slot_count.reshape(128, 1)
    obs = recv_obs.reshape(128, CAP)
    turned = w_out.T
    small = jnp.concatenate(
        [w_in, jnp.pad(turned, ((0, 10), (0, 0))), jnp.pad(turned, ((8, 2), (0, 0)))], 0
    )
    small = jnp.pad(small, ((0, 0), (0, CP - C)))

    last, first = fields[:, 6:8].reshape(128, 128), fields[:, 0:2].reshape(128, 128)
    one, two = swaps(*ordered(ns & 1, first, last), "ns")
    ftm, fm, one, two = call(
        fields_kernel,
        [((12 * 128, 64), BF), ((64, 1024), BF), ((32, 64), BF), ((32, 64), BF)],
        [((512, 128), F32), ((128, 128), F32), ((128, 128), F32), ((32, 64), F32), ((32, 64), F32)],
        flags, fields.reshape(512, 128), one, two,
        smem=1, vmem=8,
    )
    west, east = swaps(one, two, "ew")
    sent, a1, gp, h2c = call(
        forward_kernel,
        [((1024, 128), BF), ((N10, CP), BF), ((N10, CP), BF), ((1024, CP), BF)],
        [
            ((N12 + 16, CP), F32), ((N12, 3 * CP), BF), ((N10 + 16, CP), F32),
            ((N10, 3 * CP), BF), ((3, 3 * CP, CP), BF), ((3, 3 * CP, CP), BF),
            ((64, 128), I32), ((1024, 128), F32),
        ],
        flags, ftm, west, east, small, conv_first, conv_second, cells, wts, cnt,
        smem=1, vmem=28, flops=2 * 10**9,
    )
    received = exchange(sent)
    a1t, h0t = call(
        turn_kernel,
        [((3 * C, 1280), BF), ((3 * C, 1280), BF)],
        [((N10, CP), F32), ((N12, 64), F32), ((1280, CP), BF), ((1280, 64), BF)],
        flags, a1, ftm, west, east, small,
        smem=1, vmem=16, flops=10**9,
    )
    pred, loss, back = call(
        owner_kernel,
        [((6, 2048), F32), ((16, 128), F32), ((1024, 128), BF)],
        [
            ((96, 1024), BF), ((96, 1024), BF), ((128, 1024), BF), ((128, 1024), BF),
            ((96, 128), F32), ((128, 128), I32), ((1024, 128), F32),
        ],
        received, obs, targets,
        vmem=8, flops=10**9,
    )
    grads = exchange(back)
    g_field, one, two = call(
        spread_kernel,
        [((64, 128), F32), ((16, 128), F32), ((16, 128), F32)],
        [
            ((96, 4096), BF), ((96, 4096), BF), ((64, 4096), BF), ((64, 4096), BF),
            ((96, 64), F32),
        ],
        flags, grads, cells, wts, cnt,
        smem=1, vmem=12, flops=10**9,
    )
    one, two = swaps(one, two, "ns")
    et, one, two = call(
        turn_field_kernel,
        [((128, 96), F32), ((2, 96), F32), ((2, 96), F32)],
        [],
        flags, g_field, one, two,
        smem=1, vmem=4,
    )
    one, two = swaps(one, two, "ew")
    pay, g_fields = call(
        backward_kernel,
        [((2 * HALF, 128), BF), ((512, 128), F32)],
        [
            ((ROW, 128), F32), ((CP, 12 * CP), BF), ((N12 + 16, CP), F32), ((N12, 3 * CP), BF),
            ((N10 + 16, CP), F32), ((N10, 3 * CP), BF), ((1024, CP), BF),
            ((3, CP, 3 * CP), BF), ((3, CP, 3 * CP), BF),
        ],
        flags, g_field, et, one, two, fm, a1t, h0t, gp, h2c, conv_second, conv_first, small, loss,
        smem=1, vmem=28, flops=2 * 10**9,
    )
    pairs = [(n, n ^ 1) for n in range(n_ns)]
    groups = [[n * n_ew + e for n in range(c, n_ns, 2) for e in range(n_ew)] for c in range(2)]
    theirs = lax.ppermute(pay[HALF:], "ns", pairs)
    summed = (pay[:HALF].astype(F32) + theirs.astype(F32)).astype(BF).reshape(64, PIECE, 128)
    share = jnp.sum(exchange(summed, groups).astype(F32), axis=0).astype(BF)
    mine = exchange(jnp.broadcast_to(share[None], (64, PIECE, 128)), groups).reshape(HALF, 128)
    other = lax.ppermute(mine, "ns", pairs)
    grad_second, grad_first, grad_in, g_out, total = call(
        unpack_kernel,
        [((3, 3, C, C), F32), ((3, 3, C, C), F32), ((64, C), F32), ((8, CP), F32), ((8, 128), F32)],
        [],
        flags, mine, other,
        smem=1, vmem=16,
    )
    return (
        pred,
        total[0, 0],
        grad_first,
        grad_second,
        grad_in,
        g_out[:6, :C].T,
        g_fields.reshape(64, TH, TW),
    )


def solution(mesh):
    in_specs = (
        P(None, "ns", "ew"),
        P(),
        P(),
        P(),
        P(),
        P(("ns", "ew"), None, None),
        P(("ns", "ew"), None, None),
        P(("ns", "ew"), None),
        P(("ns", "ew"), None),
        P(None, ("ns", "ew")),
    )
    out_specs = (P(None, ("ns", "ew")), P(), P(), P(), P(), P(), P(None, "ns", "ew"))
    return jax.shard_map(
        on_device, mesh=mesh, in_specs=in_specs, out_specs=out_specs, check_vma=False
    )
```

```python
import jax
import jax.numpy as jnp
from jax import lax
from jax.experimental import pallas as pl
from jax.experimental.pallas import tpu as pltpu
from jax.sharding import PartitionSpec as P

BF = jnp.bfloat16
F32 = jnp.float32
I32 = jnp.int32
CAP = 128
TH, TW = 8, 128
C = 192
ROW = 144
N12, N10, N8 = 12 * ROW, 10 * ROW, 8 * ROW
CP = 256
AXES = ("ns", "ew")
PIECE = 48
HALF = 64 * PIECE
REST = 1728
EXTRA = 2592
LONG = 2 * 10**10
NT = (((1,), (1,)), ((), ()))
TN = (((0,), (0,)), ((), ()))


def dot(x, y, dims=(((1,), (0,)), ((), ()))):
    return lax.dot_general(x, y, dims, preferred_element_type=F32)


def taps(cat, weight, first, count, order):
    total = None
    for a in range(3):
        start = (a if order > 0 else 2 - a) * ROW + first
        rows = cat[start : start + count, :]
        term = dot(rows, weight[a]) if order > 0 else dot(rows, weight[a], NT)
        total = term if total is None else total + term
    return total


def stack_weights(out, kernel, order):
    out[...] = jnp.zeros_like(out)
    for a in range(3):
        for b in range(3):
            if order > 0:
                out[a, b * CP : b * CP + C, 0:C] = kernel[a, b]
            else:
                out[a, 0:C, b * CP : b * CP + C] = kernel[a, b]


def pick(table, row, index):
    return jnp.take_along_axis(
        jnp.broadcast_to(table[row : row + 1, :], (8, 128)),
        index,
        axis=1,
        mode="promise_in_bounds",
    )


def pack_pair(x, y):
    return x * 65536 + (y + 32768)


def unpack_pair(word):
    return (word >> 16).astype(F32), ((word & 65535) - 32768).astype(F32)


def ordered(odd, x, y):
    return jnp.where(odd > 0, x, y), jnp.where(odd > 0, y, x)


def own_kernel(f8, fto, fm, wo, eo, s8):
    s8[...] = f8[...].astype(F32)
    for r in range(8):
        block = s8[pl.ds(r, 64, stride=8), :]
        fm[:, r * 128 : r * 128 + 128] = block.astype(BF)
        turned = block.T
        fto[r * 128 : r * 128 + 128, :] = turned.astype(BF)
        wo[2 * r : 2 * r + 2, :] = turned[0:2]
        eo[2 * r : 2 * r + 2, :] = turned[126:128]


def rim_kernel(flags, swap1, swap2, wo, eo, ftr, out1, out2, sn, ss, sw, se):
    sn[...], ss[...] = ordered(flags[4], swap1[...].astype(F32), swap2[...].astype(F32))
    sw[...] = jnp.zeros_like(sw)
    se[...] = jnp.zeros_like(se)
    sw[4:20, :] = wo[...]
    se[4:20, :] = eo[...]
    for i in range(4):
        block = (sn if i < 2 else ss)[pl.ds(i % 2, 64, stride=2), :]
        r = i if i < 2 else i + 8
        turned = block.T
        ftr[i * 128 : i * 128 + 128, :] = turned.astype(BF)
        sw[2 * r : 2 * r + 2, :] = turned[0:2]
        se[2 * r : 2 * r + 2, :] = turned[126:128]
    one, two = ordered(flags[5], sw[...], se[...])
    out1[...] = one.astype(BF)
    out2[...] = two.astype(BF)


def row_of(own, rim, r):
    if 2 <= r < 10:
        return own[(r - 2) * 128 : (r - 1) * 128]
    i = r if r < 2 else r - 8
    return rim[i * 128 : i * 128 + 128]


def turn_field_kernel(flags, gf, swap1, swap2, et, out1, out2):
    north, south = ordered(flags[4], swap1[...], swap2[...])
    turned = jnp.concatenate([north, gf[...], south], 0).T
    et[...] = turned
    out1[...], out2[...] = ordered(flags[5], turned[0:2], turned[126:128])


def forward_kernel(
    flags, fto, ftr, swap1, swap2, small, c1, c2, cells, wts, cnt, out, a1_out, gp, h2c, hs, xcat,
    as_, acat, w1, w2, fq, pf,
):
    zero8 = jnp.zeros((8, CP), F32)
    hs[0:8, :] = zero8
    hs[N12 + 8 : N12 + 16, :] = zero8
    as_[0:8, :] = zero8
    as_[N10 + 8 : N10 + 16, :] = zero8
    stack_weights(w1, c1, 1)
    stack_weights(w2, c2, 1)
    own, rim = dot(fto[...], small[0:64, :]), dot(ftr[...], small[0:64, :])
    west, east = ordered(
        flags[5], dot(swap1[...], small[0:64, :]), dot(swap2[...], small[0:64, :])
    )
    for r in range(12):
        at = 8 + r * ROW
        hs[at + 128 : at + ROW, :] = jnp.zeros((ROW - 128, CP), F32)
        hs[at : at + 2, :] = west[2 * r : 2 * r + 2]
        hs[at + 2 : at + 130, :] = row_of(own, rim, r)
        hs[at + 130 : at + 132, :] = east[2 * r : 2 * r + 2]
    for b in range(3):
        xcat[:, b * CP : (b + 1) * CP] = hs[7 + b : 7 + b + N12, :].astype(BF)
    col = lax.broadcasted_iota(I32, (ROW, CP), 0)
    col_mask = jnp.where(col == 1, flags[2], jnp.where(col == 130, flags[3], 1.0))
    root = 0.7978845608028654
    for part in range(5):
        z2 = taps(xcat, w1, part * 2 * ROW, 2 * ROW, 1)
        for q in range(2):
            r = part * 2 + q
            z = z2[q * ROW : (q + 1) * ROW]
            mask = col_mask
            if r == 0:
                mask = col_mask * flags[0]
            if r == 9:
                mask = col_mask * flags[1]
            zz = z * z
            t = jnp.tanh(root * z * (1.0 + 0.044715 * zz))
            half = 0.5 * (1.0 + t)
            slope = half + 0.5 * z * (1.0 - t * t) * (root * (1.0 + 3 * 0.044715 * zz))
            a1 = z * half * mask
            as_[8 + r * ROW : 8 + (r + 1) * ROW, :] = a1
            a1_out[r * ROW : (r + 1) * ROW, :] = a1.astype(BF)
            gp[r * ROW : (r + 1) * ROW, :] = (slope * mask).astype(BF)
    for b in range(3):
        acat[:, b * CP : (b + 1) * CP] = as_[7 + b : 7 + b + N10, :].astype(BF)
    for part in range(4):
        at = part * 2 * ROW
        h2 = hs[8 + 2 * ROW + at : 8 + 4 * ROW + at, :] + taps(acat, w2, at, 2 * ROW, 1)
        as_[at : at + 2 * ROW, :] = h2
    for r in range(8):
        h2c[r * 128 : r * 128 + 128, :] = as_[r * ROW + 2 : r * ROW + 130, :].astype(BF)
    field = dot(small[64:80, :], h2c[...], NT)
    tiles = [field[0:8, r * 128 : r * 128 + 128] for r in range(8)]
    top = tiles[0]
    for r in range(1, 8):
        top = jnp.maximum(jnp.abs(top), jnp.abs(tiles[r]))
    largest = jnp.maximum(jnp.max(jnp.abs(top)), 1e-30)
    up = 32000.0 / largest
    down = largest * (1.0 / 32000.0)
    for r in range(8):
        whole = jnp.round(tiles[r] * up).astype(I32)
        fq[r * 8 : r * 8 + 3, :] = pack_pair(whole[0:3], whole[3:6])
    pf[...] = jnp.zeros_like(pf)
    lane = lax.broadcasted_iota(I32, (8, 128), 1)

    def owners(ob, carry):
        rows = pl.ds(pl.multiple_of(ob * 8, 8), 8)
        live = lane < cnt[rows, 0:1]
        sums = [jnp.zeros((8, 128), F32)] * 6
        for k in range(4):
            index = cells[k, rows, :]
            low, high = index & 127, index >> 7
            weight = jnp.where(live, wts[k, rows, :] * down, 0.0)
            got = [jnp.zeros((8, 128), I32)] * 3
            for r in range(8):
                here = high == r
                got = [jnp.where(here, pick(fq, r * 8 + v, low), got[v]) for v in range(3)]
            for v in range(3):
                x, y = unpack_pair(got[v])
                sums[v] = sums[v] + weight * x
                sums[v + 3] = sums[v + 3] + weight * y
        for v in range(6):
            pf[pl.ds(ob * 64 + v, 8, stride=8), :] = sums[v]
        return carry

    lax.fori_loop(0, 16, owners, 0)
    out[...] = pf[...].astype(BF)


def turn_kernel(flags, a1, fto, ftr, swap1, swap2, small, a1t, h0t, wide, thin, pa, pt):
    wide[...] = a1[...].astype(F32)
    west, east = ordered(flags[5], swap1[...].astype(F32), swap2[...].astype(F32))
    for r in range(12):
        at = r * ROW
        thin[at : at + 2, :] = west[2 * r : 2 * r + 2]
        thin[at + 2 : at + 130, :] = row_of(fto, ftr, r).astype(F32)
        thin[at + 130 : at + 132, :] = east[2 * r : 2 * r + 2]
    ones = lax.broadcasted_iota(I32, (CP, CP), 0) == lax.broadcasted_iota(I32, (CP, CP), 1)
    same = jnp.where(ones, 1.0, 0.0).astype(BF)
    win_t = dot(same[0:C, :], small[0:64, :], NT).astype(BF)
    for b in range(3):
        for r in range(10):
            at = slice(r * 128, r * 128 + 128)
            pa[at, :] = wide[r * ROW + 1 + b : r * ROW + 129 + b, :].astype(BF)
            pt[at, :] = thin[(r + 1) * ROW + 1 + b : (r + 1) * ROW + 129 + b, :].astype(BF)
        a1t[b * C : (b + 1) * C, :] = dot(same[0:C, :], pa[...], NT).astype(BF)
        h0t[b * C : (b + 1) * C, :] = dot(win_t, pt[...], NT).astype(BF)


def spread_row(row):
    return jnp.broadcast_to(row, (16, 128)).astype(BF)


def iotas(count):
    base = lax.broadcasted_iota(I32, (16, 128), 0)
    return [(base + 16 * m).astype(F32).astype(BF) for m in range(count)]


def overlapped(count, build, multiply):
    build(0, 0)

    def step(i, carry):
        build(2 * i + 1, 1)
        multiply(0)
        build(jnp.minimum(2 * i + 2, count - 1), 0)
        multiply(1)
        return carry

    lax.fori_loop(0, count // 2, step, 0)


def owner_kernel(recv, obs, target, pred, loss, out, l0, l1, r0, r1, total, rq, gf):
    steps = iotas(8)
    none = jnp.zeros((16, 128), BF)
    one = jnp.ones((16, 128), BF)
    lefts, rights = (l0, l1), (r0, r1)

    def collect(tb, slot):
        left, right = lefts[slot], rights[slot]
        block = recv[pl.ds(pl.multiple_of(tb * 64, 64), 64), :].astype(F32)
        index = obs[pl.ds(pl.multiple_of(tb * 8, 8), 8), :]
        low = (index & 127).astype(F32)
        high = (index >> 7).astype(F32)
        for i in range(8):
            at = slice(i * 128, i * 128 + 128)
            here = spread_row(high[i : i + 1]) == steps[0]
            for v in range(6):
                value = spread_row(block[i * 8 + v : i * 8 + v + 1])
                left[v * 16 : v * 16 + 16, at] = jnp.where(here, value, none)
            mine = spread_row(low[i : i + 1])
            for m in range(8):
                right[m * 16 : m * 16 + 16, at] = jnp.where(mine == steps[m], one, none)

    def multiply(slot):
        total[...] += dot(lefts[slot][...], rights[slot][...], NT)

    total[...] = jnp.zeros_like(total)
    overlapped(16, collect, multiply)
    scale = 1.0 / (6 * 2048)
    squares = jnp.zeros((6, 128), F32)
    resids = []
    for h in range(16):
        at = slice(h * 128, h * 128 + 128)
        mine = total[pl.ds(h, 6, stride=16), :]
        pred[:, at] = mine
        resid = mine - target[:, at]
        squares = squares + resid * resid
        resids.append(resid * scale)
    loss[...] = jnp.full((16, 128), jnp.sum(squares) * (0.5 * scale), F32)
    top = jnp.abs(resids[0])
    for h in range(1, 16):
        top = jnp.maximum(top, jnp.abs(resids[h]))
    largest = jnp.maximum(jnp.max(top), 1e-30)
    up = 32000.0 / largest
    down = largest * (1.0 / 32000.0)
    for h in range(16):
        whole = jnp.round(resids[h] * up).astype(I32)
        rq[h * 8 : h * 8 + 3, :] = pack_pair(whole[0:3], whole[3:6])
    gf[...] = jnp.zeros_like(gf)

    def choose(tb, carry):
        index = obs[pl.ds(pl.multiple_of(tb * 8, 8), 8), :]
        low, high = index & 127, index >> 7
        got = [jnp.zeros((8, 128), I32)] * 3
        for h in range(16):
            here = high == h
            got = [jnp.where(here, pick(rq, h * 8 + v, low), got[v]) for v in range(3)]
        for v in range(3):
            x, y = unpack_pair(got[v])
            gf[pl.ds(tb * 64 + v, 8, stride=8), :] = x * down
            gf[pl.ds(tb * 64 + v + 3, 8, stride=8), :] = y * down
        return carry

    lax.fori_loop(0, 16, choose, 0)
    out[...] = gf[...].astype(BF)


def spread_kernel(
    flags, grad, cells, wts, cnt, out, out1, out2, l0, l1, r0, r1, total
):
    lefts, rights = (l0, l1), (r0, r1)
    steps = iotas(4)
    none = jnp.zeros((16, 128), BF)
    total[...] = jnp.zeros_like(total)
    lane = lax.broadcasted_iota(I32, (8, 128), 1)

    def owners(ob, slot):
        left, right = lefts[slot], rights[slot]
        rows = pl.ds(pl.multiple_of(ob * 8, 8), 8)
        live = lane < cnt[rows, 0:1]
        block = grad[pl.ds(pl.multiple_of(ob * 64, 64), 64), :].astype(F32)
        index = [cells[k, rows, :] for k in range(4)]
        low = [(i & 63).astype(F32) for i in index]
        high = [(i >> 6).astype(F32) for i in index]
        weight = [jnp.where(live, wts[k, rows, :], 0.0) for k in range(4)]
        for i in range(8):
            values = [spread_row(block[i * 8 + v : i * 8 + v + 1]) for v in range(6)]
            for k in range(4):
                at = slice((i * 4 + k) * 128, (i * 4 + k) * 128 + 128)
                here = spread_row(high[k][i : i + 1]) == steps[0]
                for v in range(6):
                    left[v * 16 : v * 16 + 16, at] = jnp.where(here, values[v], none)
                mine = spread_row(low[k][i : i + 1])
                amount = spread_row(weight[k][i : i + 1])
                for m in range(4):
                    right[m * 16 : m * 16 + 16, at] = jnp.where(mine == steps[m], amount, none)

    def multiply(slot):
        total[...] += dot(lefts[slot][...], rights[slot][...], NT)

    overlapped(16, owners, multiply)
    out[...] = jnp.zeros_like(out)
    for r in range(8):
        even = total[pl.ds(2 * r, 6, stride=16), :]
        odd = total[pl.ds(2 * r + 1, 6, stride=16), :]
        out[r * 8 : r * 8 + 6, :] = jnp.concatenate([even, odd], 1)
    out1[...], out2[...] = ordered(flags[4], out[0:16, :], out[48:64, :])


def backward_kernel(
    flags, gf, et, swap1, swap2, fm, a1t, h0t, gp, h2c, c2, c1, small, loss, pay, gfields, es, bw,
    gs, g2cat, zs, gzcat, gc, w2, w1,
):
    zero8 = jnp.zeros((8, CP), F32)
    gs[0:8, :] = zero8
    gs[N12 + 8 : N12 + 16, :] = zero8
    zs[0:8, :] = zero8
    zs[N10 + 8 : N10 + 16, :] = zero8
    stack_weights(w2, c2, -1)
    stack_weights(w1, c1, -1)
    core = (flags[4] > 0).astype(I32)
    base_s = pl.multiple_of(core * HALF, 16)
    base_f = pl.multiple_of((1 - core) * HALF, 16)

    def put(base, at, value):
        pay[pl.ds(pl.multiple_of(base + at, 16), value.shape[0]), :] = value.astype(BF)

    def put_taps(base, turned):
        for a in range(3):
            y = dot(turned[:, a * 128 : a * 128 + 1024], gc[...])
            for b in range(3):
                tap = a * 3 + b
                mine = y[b * C : (b + 1) * C]
                put(base, tap * C, mine[:, 0:128])
                rest = mine[:, 128:256]
                put(base, REST + tap * 96, rest[0:96] + pltpu.roll(rest[96:192], 64, 1))

    es[...] = jnp.zeros_like(es)
    es[2:130, 0:96] = et[...]
    es[0:2, 0:96], es[130:132, 0:96] = ordered(flags[5], swap1[...], swap2[...])
    bw[...] = jnp.zeros_like(bw)
    for r in range(12):
        at, block = (r // 2) * 16, small[64 + 16 * (r % 2) : 80 + 16 * (r % 2), :]
        bw[at : at + 16, r * CP : (r + 1) * CP] = block
        bw[128 + at : 144 + at, r * CP : (r + 1) * CP] = block
    x = es[...]
    x_hi = x.astype(BF)
    x_lo = (x - x_hi.astype(F32)).astype(BF)
    both = jnp.concatenate([x_hi, x_lo], 1)
    for r in range(12):
        gs[8 + r * ROW : 8 + (r + 1) * ROW, :] = dot(both, bw[:, r * CP : (r + 1) * CP])
    for b in range(3):
        g2cat[:, b * CP : (b + 1) * CP] = gs[9 - b : 9 - b + N12, :].astype(BF)
    for r in range(8):
        at = 8 + (r + 2) * ROW + 2
        gc[r * 128 : r * 128 + 128, :] = gs[at : at + 128, :].astype(BF)
    put_taps(base_s, a1t)
    for part in range(5):
        at = part * 2 * ROW
        g = taps(g2cat, w2, at, 2 * ROW, -1)
        zs[8 + at : 8 + at + 2 * ROW, :] = g * gp[at : at + 2 * ROW, :].astype(F32)
    for b in range(3):
        gzcat[:, b * CP : (b + 1) * CP] = zs[9 - b : 9 - b + N10, :].astype(BF)
    for r in range(8):
        at = 8 + (r + 1) * ROW + 2
        gc[r * 128 : r * 128 + 128, :] = zs[at : at + 128, :].astype(BF)
    put_taps(base_f, h0t)
    for part in range(4):
        at = 8 + 2 * ROW + part * 2 * ROW
        gs[at : at + 2 * ROW, :] = gs[at : at + 2 * ROW, :] + taps(
            gzcat, w1, part * 2 * ROW, 2 * ROW, -1
        )
    for r in range(8):
        at = 8 + (r + 2) * ROW + 2
        gc[r * 128 : r * 128 + 128, :] = gs[at : at + 128, :].astype(BF)
    g_in = dot(fm[...], gc[...])
    g_fields = dot(small[0:64, :], gc[...], NT)
    for r in range(8):
        gfields[pl.ds(r, 64, stride=8), :] = g_fields[:, r * 128 : r * 128 + 128]
    line = jnp.concatenate([gf[r * 8 : r * 8 + 8, :] for r in range(8)], 1)
    line_hi = line.astype(BF).astype(F32)
    line2 = jnp.concatenate([line_hi, line - line_hi], 0).astype(BF)
    g_out = dot(line2, h2c[...])
    g_out = g_out[0:8] + g_out[8:16]
    put(base_s, EXTRA, g_in[:, 0:128])
    rest = g_in[:, 128:256]
    put(base_s, EXTRA + 64, rest[0:32] + pltpu.roll(rest[32:64], 64, 1))
    put(base_s, EXTRA + 96, jnp.zeros((HALF - EXTRA - 96, 128), F32))
    put(base_f, EXTRA, jnp.concatenate([g_out[:, 0:128], g_out[:, 128:256]], 0))
    put(base_f, EXTRA + 16, loss[...])
    put(base_f, EXTRA + 32, jnp.zeros((HALF - EXTRA - 32, 128), F32))


def unpack_kernel(flags, mine, other, second, first, g_in, g_out, loss):
    def unpack(source, kernel):
        for tap in range(9):
            a, b = tap // 3, tap % 3
            kernel[a, b, :, 0:128] = source[tap * C : (tap + 1) * C, :].astype(F32)
            rest = source[REST + tap * 96 : REST + tap * 96 + 96, :].astype(F32)
            kernel[a, b, 0:96, 128:C] = rest[:, 0:64]
            kernel[a, b, 96:C, 128:C] = pltpu.roll(rest, 64, 1)[:, 0:64]

    def both(s, f):
        unpack(s, second)
        unpack(f, first)
        g_in[:, 0:128] = s[EXTRA : EXTRA + 64, :].astype(F32)
        rest = s[EXTRA + 64 : EXTRA + 96, :].astype(F32)
        g_in[0:32, 128:C] = rest[:, 0:64]
        g_in[32:64, 128:C] = pltpu.roll(rest, 64, 1)[:, 0:64]
        extra = f[EXTRA : EXTRA + 32, :].astype(F32)
        g_out[:, 0:128] = extra[0:6]
        g_out[:, 128:C] = extra[8:14, 0:64]
        loss[0, 0] = jnp.max(extra[16:24])

    @pl.when(flags[4] == 0)
    def _():
        both(mine, other)

    @pl.when(flags[4] > 0)
    def _():
        both(other, mine)


def swaps(one, two, axis):
    count = lax.axis_size(axis)
    pairs = [[(i, i + 1) for i in range(start, count - 1, 2)] for start in range(2)]
    return tuple(
        lax.ppermute(x, axis, p + [(j, i) for i, j in p]) for x, p in zip((one, two), pairs)
    )


def exchange(rows, groups=None):
    return lax.all_to_all(
        rows, AXES, split_axis=0, concat_axis=0, tiled=True, axis_index_groups=groups
    )


def call(kernel, out_shapes, scratch, *operands, smem=0, smem_out=0, vmem=60, flops=0):
    vm, sm = pl.BlockSpec(memory_space=pltpu.VMEM), pl.BlockSpec(memory_space=pltpu.SMEM)
    return pl.pallas_call(
        kernel,
        out_shape=[jax.ShapeDtypeStruct(s, d) for s, d in out_shapes],
        in_specs=[sm] * smem + [vm] * (len(operands) - smem),
        out_specs=[vm] * (len(out_shapes) - smem_out) + [sm] * smem_out,
        scratch_shapes=[pltpu.VMEM(s, d) for s, d in scratch],
        compiler_params=pltpu.CompilerParams(vmem_limit_bytes=vmem * 1024 * 1024),
        cost_estimate=pl.CostEstimate(flops=flops, bytes_accessed=4_000_000, transcendentals=0),
    )(*operands)


def on_device(
    fields,
    w_in,
    conv_first,
    conv_second,
    w_out,
    slot_cells,
    slot_weights,
    slot_count,
    recv_obs,
    targets,
):
    ns, ew = lax.axis_index("ns"), lax.axis_index("ew")
    n_ns, n_ew = lax.axis_size("ns"), lax.axis_size("ew")
    flags = jnp.stack(
        [ns > 0, ns < n_ns - 1, ew > 0, ew < n_ew - 1, (ns & 1) > 0, (ew & 1) > 0]
    ).astype(F32)
    cells = slot_cells.reshape(4, 128, CAP)
    wts = slot_weights.reshape(4, 128, CAP)
    cnt = slot_count.reshape(128, 1)
    obs = recv_obs.reshape(128, CAP)
    turned = w_out.T
    small = jnp.concatenate(
        [w_in, jnp.pad(turned, ((0, 10), (0, 0))), jnp.pad(turned, ((8, 2), (0, 0)))], 0
    )
    small = jnp.pad(small, ((0, 0), (0, CP - C)))

    last, first = fields[:, 6:8].reshape(128, 128), fields[:, 0:2].reshape(128, 128)
    one, two = swaps(*ordered(ns & 1, first, last), "ns")
    fto, fm, own_west, own_east = call(
        own_kernel,
        [((1024, 64), BF), ((64, 1024), BF), ((16, 64), F32), ((16, 64), F32)],
        [((512, 128), F32)],
        fields.reshape(512, 128),
        vmem=8, flops=LONG,
    )
    ftr, one, two = call(
        rim_kernel,
        [((512, 64), BF), ((32, 64), BF), ((32, 64), BF)],
        [((128, 128), F32), ((128, 128), F32), ((32, 64), F32), ((32, 64), F32)],
        flags, one, two, own_west, own_east,
        smem=1, vmem=8, flops=LONG,
    )
    west, east = swaps(one, two, "ew")
    sent, a1, gp, h2c = call(
        forward_kernel,
        [((1024, 128), BF), ((N10, CP), BF), ((N10, CP), BF), ((1024, CP), BF)],
        [
            ((N12 + 16, CP), F32), ((N12, 3 * CP), BF), ((N10 + 16, CP), F32),
            ((N10, 3 * CP), BF), ((3, 3 * CP, CP), BF), ((3, 3 * CP, CP), BF),
            ((64, 128), I32), ((1024, 128), F32),
        ],
        flags, fto, ftr, west, east, small, conv_first, conv_second, cells, wts, cnt,
        smem=1, vmem=28, flops=2 * 10**9,
    )
    received = exchange(sent)
    a1t, h0t = call(
        turn_kernel,
        [((3 * C, 1280), BF), ((3 * C, 1280), BF)],
        [((N10, CP), F32), ((N12, 64), F32), ((1280, CP), BF), ((1280, 64), BF)],
        flags, a1, fto, ftr, west, east, small,
        smem=1, vmem=16, flops=10**9,
    )
    pred, loss, back = call(
        owner_kernel,
        [((6, 2048), F32), ((16, 128), F32), ((1024, 128), BF)],
        [
            ((96, 1024), BF), ((96, 1024), BF), ((128, 1024), BF), ((128, 1024), BF),
            ((96, 128), F32), ((128, 128), I32), ((1024, 128), F32),
        ],
        received, obs, targets,
        vmem=8, flops=10**9,
    )
    grads = exchange(back)
    g_field, one, two = call(
        spread_kernel,
        [((64, 128), F32), ((16, 128), F32), ((16, 128), F32)],
        [
            ((96, 4096), BF), ((96, 4096), BF), ((64, 4096), BF), ((64, 4096), BF),
            ((96, 64), F32),
        ],
        flags, grads, cells, wts, cnt,
        smem=1, vmem=12, flops=10**9,
    )
    one, two = swaps(one, two, "ns")
    et, one, two = call(
        turn_field_kernel,
        [((128, 96), F32), ((2, 96), F32), ((2, 96), F32)],
        [],
        flags, g_field, one, two,
        smem=1, vmem=4, flops=LONG,
    )
    one, two = swaps(one, two, "ew")
    pay, g_fields = call(
        backward_kernel,
        [((2 * HALF, 128), BF), ((512, 128), F32)],
        [
            ((ROW, 128), F32), ((CP, 12 * CP), BF), ((N12 + 16, CP), F32), ((N12, 3 * CP), BF),
            ((N10 + 16, CP), F32), ((N10, 3 * CP), BF), ((1024, CP), BF),
            ((3, CP, 3 * CP), BF), ((3, CP, 3 * CP), BF),
        ],
        flags, g_field, et, one, two, fm, a1t, h0t, gp, h2c, conv_second, conv_first, small, loss,
        smem=1, vmem=28, flops=2 * 10**9,
    )
    pairs = [(n, n ^ 1) for n in range(n_ns)]
    groups = [[n * n_ew + e for n in range(c, n_ns, 2) for e in range(n_ew)] for c in range(2)]
    theirs = lax.ppermute(pay[HALF:], "ns", pairs)
    summed = (pay[:HALF].astype(F32) + theirs.astype(F32)).astype(BF).reshape(64, PIECE, 128)
    share = jnp.sum(exchange(summed, groups).astype(F32), axis=0).astype(BF)
    mine = exchange(jnp.broadcast_to(share[None], (64, PIECE, 128)), groups).reshape(HALF, 128)
    other = lax.ppermute(mine, "ns", pairs)
    grad_second, grad_first, grad_in, g_out, total = call(
        unpack_kernel,
        [((3, 3, C, C), F32), ((3, 3, C, C), F32), ((64, C), F32), ((6, C), F32), ((1, 1), F32)],
        [],
        flags, mine, other,
        smem=1, smem_out=1, vmem=16,
    )
    return (
        pred,
        total[0, 0],
        grad_first,
        grad_second,
        grad_in,
        g_out.T,
        g_fields.reshape(64, TH, TW),
    )


def solution(mesh):
    in_specs = (
        P(None, "ns", "ew"),
        P(),
        P(),
        P(),
        P(),
        P(("ns", "ew"), None, None),
        P(("ns", "ew"), None, None),
        P(("ns", "ew"), None),
        P(("ns", "ew"), None),
        P(None, ("ns", "ew")),
    )
    out_specs = (P(None, ("ns", "ew")), P(), P(), P(), P(), P(), P(None, "ns", "ew"))
    return jax.shard_map(
        on_device, mesh=mesh, in_specs=in_specs, out_specs=out_specs, check_vma=False
    )
```

```python
import jax
import jax.numpy as jnp
from jax import lax
from jax.experimental import pallas as pl
from jax.experimental.pallas import tpu as pltpu
from jax.sharding import PartitionSpec as P

BF = jnp.bfloat16
F32 = jnp.float32
I32 = jnp.int32
CAP = 128
TH, TW = 8, 128
C = 192
ROW = 144
N12, N10, N8 = 12 * ROW, 10 * ROW, 8 * ROW
CP = 256
AXES = ("ns", "ew")
PIECE = 48
HALF = 64 * PIECE
REST = 1728
EXTRA = 2592
LONG = 2 * 10**10
NT = (((1,), (1,)), ((), ()))
TN = (((0,), (0,)), ((), ()))


def dot(x, y, dims=(((1,), (0,)), ((), ()))):
    return lax.dot_general(x, y, dims, preferred_element_type=F32)


def taps(cat, weight, first, count, order):
    total = None
    for a in range(3):
        start = (a if order > 0 else 2 - a) * ROW + first
        rows = cat[start : start + count, :]
        term = dot(rows, weight[a]) if order > 0 else dot(rows, weight[a], NT)
        total = term if total is None else total + term
    return total


def stack_weights(out, kernel, order):
    out[...] = jnp.zeros_like(out)
    for a in range(3):
        for b in range(3):
            if order > 0:
                out[a, b * CP : b * CP + C, 0:C] = kernel[a, b]
            else:
                out[a, 0:C, b * CP : b * CP + C] = kernel[a, b]


def pick(table, row, index):
    return jnp.take_along_axis(
        jnp.broadcast_to(table[row : row + 1, :], (8, 128)),
        index,
        axis=1,
        mode="promise_in_bounds",
    )


def pack_pair(x, y):
    return x * 65536 + (y + 32768)


def unpack_pair(word):
    return (word >> 16).astype(F32), ((word & 65535) - 32768).astype(F32)


def ordered(odd, x, y):
    return jnp.where(odd > 0, x, y), jnp.where(odd > 0, y, x)


def own_kernel(f8, fto, fm, wo, eo, s8):
    s8[...] = f8[...].astype(F32)
    for r in range(8):
        block = s8[pl.ds(r, 64, stride=8), :]
        fm[:, r * 128 : r * 128 + 128] = block.astype(BF)
        turned = block.T
        fto[r * 128 : r * 128 + 128, :] = turned.astype(BF)
        wo[2 * r : 2 * r + 2, :] = turned[0:2]
        eo[2 * r : 2 * r + 2, :] = turned[126:128]


def rim_kernel(flags, swap1, swap2, wo, eo, ftr, out1, out2, sn, ss, sw, se):
    sn[...], ss[...] = ordered(flags[4], swap1[...].astype(F32), swap2[...].astype(F32))
    sw[...] = jnp.zeros_like(sw)
    se[...] = jnp.zeros_like(se)
    sw[4:20, :] = wo[...]
    se[4:20, :] = eo[...]
    for i in range(4):
        block = (sn if i < 2 else ss)[pl.ds(i % 2, 64, stride=2), :]
        r = i if i < 2 else i + 8
        turned = block.T
        ftr[i * 128 : i * 128 + 128, :] = turned.astype(BF)
        sw[2 * r : 2 * r + 2, :] = turned[0:2]
        se[2 * r : 2 * r + 2, :] = turned[126:128]
    one, two = ordered(flags[5], sw[...], se[...])
    out1[...] = one.astype(BF)
    out2[...] = two.astype(BF)


def row_of(own, rim, r):
    if 2 <= r < 10:
        return own[(r - 2) * 128 : (r - 1) * 128]
    i = r if r < 2 else r - 8
    return rim[i * 128 : i * 128 + 128]


def turn_field_kernel(flags, gf, swap1, swap2, et, out1, out2):
    north, south = ordered(flags[4], swap1[...], swap2[...])
    turned = jnp.concatenate([north, gf[...], south], 0).T
    et[...] = turned
    out1[...], out2[...] = ordered(flags[5], turned[0:2], turned[126:128])


def forward_kernel(
    flags, fto, ftr, swap1, swap2, small, c1, c2, cells, wts, cnt, out, a1_out, gp, h2c, hs, xcat,
    as_, acat, w1, w2, fq, pf,
):
    zero8 = jnp.zeros((8, CP), F32)
    hs[0:8, :] = zero8
    hs[N12 + 8 : N12 + 16, :] = zero8
    as_[0:8, :] = zero8
    as_[N10 + 8 : N10 + 16, :] = zero8
    stack_weights(w1, c1, 1)
    stack_weights(w2, c2, 1)
    own, rim = dot(fto[...], small[0:64, :]), dot(ftr[...], small[0:64, :])
    west, east = ordered(
        flags[5], dot(swap1[...], small[0:64, :]), dot(swap2[...], small[0:64, :])
    )
    for r in range(12):
        at = 8 + r * ROW
        hs[at + 128 : at + ROW, :] = jnp.zeros((ROW - 128, CP), F32)
        hs[at : at + 2, :] = west[2 * r : 2 * r + 2]
        hs[at + 2 : at + 130, :] = row_of(own, rim, r)
        hs[at + 130 : at + 132, :] = east[2 * r : 2 * r + 2]
    for b in range(3):
        xcat[:, b * CP : (b + 1) * CP] = hs[7 + b : 7 + b + N12, :].astype(BF)
    col = lax.broadcasted_iota(I32, (ROW, CP), 0)
    col_mask = jnp.where(col == 1, flags[2], jnp.where(col == 130, flags[3], 1.0))
    root = 0.7978845608028654
    for part in range(5):
        z2 = taps(xcat, w1, part * 2 * ROW, 2 * ROW, 1)
        for q in range(2):
            r = part * 2 + q
            z = z2[q * ROW : (q + 1) * ROW]
            mask = col_mask
            if r == 0:
                mask = col_mask * flags[0]
            if r == 9:
                mask = col_mask * flags[1]
            zz = z * z
            t = jnp.tanh(root * z * (1.0 + 0.044715 * zz))
            half = 0.5 * (1.0 + t)
            slope = half + 0.5 * z * (1.0 - t * t) * (root * (1.0 + 3 * 0.044715 * zz))
            a1 = z * half * mask
            as_[8 + r * ROW : 8 + (r + 1) * ROW, :] = a1
            a1_out[r * ROW : (r + 1) * ROW, :] = a1.astype(BF)
            gp[r * ROW : (r + 1) * ROW, :] = (slope * mask).astype(BF)
    for b in range(3):
        acat[:, b * CP : (b + 1) * CP] = as_[7 + b : 7 + b + N10, :].astype(BF)
    for part in range(4):
        at = part * 2 * ROW
        h2 = hs[8 + 2 * ROW + at : 8 + 4 * ROW + at, :] + taps(acat, w2, at, 2 * ROW, 1)
        as_[at : at + 2 * ROW, :] = h2
    for r in range(8):
        h2c[r * 128 : r * 128 + 128, :] = as_[r * ROW + 2 : r * ROW + 130, :].astype(BF)
    field = dot(small[64:80, :], h2c[...], NT)
    tiles = [field[0:8, r * 128 : r * 128 + 128] for r in range(8)]
    top = tiles[0]
    for r in range(1, 8):
        top = jnp.maximum(jnp.abs(top), jnp.abs(tiles[r]))
    largest = jnp.maximum(jnp.max(jnp.abs(top)), 1e-30)
    up = 32000.0 / largest
    down = largest * (1.0 / 32000.0)
    for r in range(8):
        whole = jnp.round(tiles[r] * up).astype(I32)
        fq[r * 8 : r * 8 + 3, :] = pack_pair(whole[0:3], whole[3:6])
    pf[...] = jnp.zeros_like(pf)
    lane = lax.broadcasted_iota(I32, (8, 128), 1)

    def owners(ob, carry):
        rows = pl.ds(pl.multiple_of(ob * 8, 8), 8)
        live = lane < cnt[rows, 0:1]
        sums = [jnp.zeros((8, 128), F32)] * 6
        for k in range(4):
            index = cells[k, rows, :]
            low, high = index & 127, index >> 7
            weight = jnp.where(live, wts[k, rows, :] * down, 0.0)
            got = [jnp.zeros((8, 128), I32)] * 3
            for r in range(8):
                here = high == r
                got = [jnp.where(here, pick(fq, r * 8 + v, low), got[v]) for v in range(3)]
            for v in range(3):
                x, y = unpack_pair(got[v])
                sums[v] = sums[v] + weight * x
                sums[v + 3] = sums[v + 3] + weight * y
        for v in range(6):
            pf[pl.ds(ob * 64 + v, 8, stride=8), :] = sums[v]
        return carry

    lax.fori_loop(0, 16, owners, 0, unroll=4)
    out[...] = pf[...].astype(BF)


def turn_kernel(flags, a1, fto, ftr, swap1, swap2, small, a1t, h0t, wide, thin, pa, pt):
    wide[...] = a1[...].astype(F32)
    west, east = ordered(flags[5], swap1[...].astype(F32), swap2[...].astype(F32))
    for r in range(12):
        at = r * ROW
        thin[at : at + 2, :] = west[2 * r : 2 * r + 2]
        thin[at + 2 : at + 130, :] = row_of(fto, ftr, r).astype(F32)
        thin[at + 130 : at + 132, :] = east[2 * r : 2 * r + 2]
    ones = lax.broadcasted_iota(I32, (CP, CP), 0) == lax.broadcasted_iota(I32, (CP, CP), 1)
    same = jnp.where(ones, 1.0, 0.0).astype(BF)
    win_t = dot(same[0:C, :], small[0:64, :], NT).astype(BF)
    for b in range(3):
        for r in range(10):
            at = slice(r * 128, r * 128 + 128)
            pa[at, :] = wide[r * ROW + 1 + b : r * ROW + 129 + b, :].astype(BF)
            pt[at, :] = thin[(r + 1) * ROW + 1 + b : (r + 1) * ROW + 129 + b, :].astype(BF)
        a1t[b * C : (b + 1) * C, :] = dot(same[0:C, :], pa[...], NT).astype(BF)
        h0t[b * C : (b + 1) * C, :] = dot(win_t, pt[...], NT).astype(BF)


def spread_row(row):
    return jnp.broadcast_to(row, (16, 128)).astype(BF)


def iotas(count):
    base = lax.broadcasted_iota(I32, (16, 128), 0)
    return [(base + 16 * m).astype(F32).astype(BF) for m in range(count)]


def overlapped(count, build, multiply):
    build(0, 0)

    def step(i, carry):
        build(2 * i + 1, 1)
        multiply(0)
        build(jnp.minimum(2 * i + 2, count - 1), 0)
        multiply(1)
        return carry

    lax.fori_loop(0, count // 2, step, 0, unroll=2)


def owner_kernel(recv, obs, target, pred, loss, out, l0, l1, r0, r1, total, rq, gf):
    steps = iotas(8)
    none = jnp.zeros((16, 128), BF)
    one = jnp.ones((16, 128), BF)
    lefts, rights = (l0, l1), (r0, r1)

    def collect(tb, slot):
        left, right = lefts[slot], rights[slot]
        block = recv[pl.ds(pl.multiple_of(tb * 64, 64), 64), :].astype(F32)
        index = obs[pl.ds(pl.multiple_of(tb * 8, 8), 8), :]
        low = (index & 127).astype(F32)
        high = (index >> 7).astype(F32)
        for i in range(8):
            at = slice(i * 128, i * 128 + 128)
            here = spread_row(high[i : i + 1]) == steps[0]
            for v in range(6):
                value = spread_row(block[i * 8 + v : i * 8 + v + 1])
                left[v * 16 : v * 16 + 16, at] = jnp.where(here, value, none)
            mine = spread_row(low[i : i + 1])
            for m in range(8):
                right[m * 16 : m * 16 + 16, at] = jnp.where(mine == steps[m], one, none)

    def multiply(slot):
        total[...] += dot(lefts[slot][...], rights[slot][...], NT)

    total[...] = jnp.zeros_like(total)
    overlapped(16, collect, multiply)
    scale = 1.0 / (6 * 2048)
    squares = jnp.zeros((6, 128), F32)
    resids = []
    for h in range(16):
        at = slice(h * 128, h * 128 + 128)
        mine = total[pl.ds(h, 6, stride=16), :]
        pred[:, at] = mine
        resid = mine - target[:, at]
        squares = squares + resid * resid
        resids.append(resid * scale)
    loss[...] = jnp.full((16, 128), jnp.sum(squares) * (0.5 * scale), F32)
    top = jnp.abs(resids[0])
    for h in range(1, 16):
        top = jnp.maximum(top, jnp.abs(resids[h]))
    largest = jnp.maximum(jnp.max(top), 1e-30)
    up = 32000.0 / largest
    down = largest * (1.0 / 32000.0)
    for h in range(16):
        whole = jnp.round(resids[h] * up).astype(I32)
        rq[h * 8 : h * 8 + 3, :] = pack_pair(whole[0:3], whole[3:6])
    gf[...] = jnp.zeros_like(gf)

    def choose(tb, carry):
        index = obs[pl.ds(pl.multiple_of(tb * 8, 8), 8), :]
        low, high = index & 127, index >> 7
        got = [jnp.zeros((8, 128), I32)] * 3
        for h in range(16):
            here = high == h
            got = [jnp.where(here, pick(rq, h * 8 + v, low), got[v]) for v in range(3)]
        for v in range(3):
            x, y = unpack_pair(got[v])
            gf[pl.ds(tb * 64 + v, 8, stride=8), :] = x * down
            gf[pl.ds(tb * 64 + v + 3, 8, stride=8), :] = y * down
        return carry

    lax.fori_loop(0, 16, choose, 0, unroll=4)
    out[...] = gf[...].astype(BF)


def spread_kernel(
    flags, grad, cells, wts, cnt, out, out1, out2, l0, l1, r0, r1, total
):
    lefts, rights = (l0, l1), (r0, r1)
    steps = iotas(4)
    none = jnp.zeros((16, 128), BF)
    total[...] = jnp.zeros_like(total)
    lane = lax.broadcasted_iota(I32, (8, 128), 1)

    def owners(ob, slot):
        left, right = lefts[slot], rights[slot]
        rows = pl.ds(pl.multiple_of(ob * 8, 8), 8)
        live = lane < cnt[rows, 0:1]
        block = grad[pl.ds(pl.multiple_of(ob * 64, 64), 64), :].astype(F32)
        index = [cells[k, rows, :] for k in range(4)]
        low = [(i & 63).astype(F32) for i in index]
        high = [(i >> 6).astype(F32) for i in index]
        weight = [jnp.where(live, wts[k, rows, :], 0.0) for k in range(4)]
        for i in range(8):
            values = [spread_row(block[i * 8 + v : i * 8 + v + 1]) for v in range(6)]
            for k in range(4):
                at = slice((i * 4 + k) * 128, (i * 4 + k) * 128 + 128)
                here = spread_row(high[k][i : i + 1]) == steps[0]
                for v in range(6):
                    left[v * 16 : v * 16 + 16, at] = jnp.where(here, values[v], none)
                mine = spread_row(low[k][i : i + 1])
                amount = spread_row(weight[k][i : i + 1])
                for m in range(4):
                    right[m * 16 : m * 16 + 16, at] = jnp.where(mine == steps[m], amount, none)

    def multiply(slot):
        total[...] += dot(lefts[slot][...], rights[slot][...], NT)

    overlapped(16, owners, multiply)
    out[...] = jnp.zeros_like(out)
    for r in range(8):
        even = total[pl.ds(2 * r, 6, stride=16), :]
        odd = total[pl.ds(2 * r + 1, 6, stride=16), :]
        out[r * 8 : r * 8 + 6, :] = jnp.concatenate([even, odd], 1)
    out1[...], out2[...] = ordered(flags[4], out[0:16, :], out[48:64, :])


def backward_kernel(
    flags, gf, et, swap1, swap2, fm, a1t, h0t, gp, h2c, c2, c1, small, loss, pay, gfields, es, bw,
    gs, g2cat, zs, gzcat, gc, w2, w1,
):
    zero8 = jnp.zeros((8, CP), F32)
    gs[0:8, :] = zero8
    gs[N12 + 8 : N12 + 16, :] = zero8
    zs[0:8, :] = zero8
    zs[N10 + 8 : N10 + 16, :] = zero8
    stack_weights(w2, c2, -1)
    stack_weights(w1, c1, -1)
    core = (flags[4] > 0).astype(I32)
    base_s = pl.multiple_of(core * HALF, 16)
    base_f = pl.multiple_of((1 - core) * HALF, 16)

    def put(base, at, value):
        pay[pl.ds(pl.multiple_of(base + at, 16), value.shape[0]), :] = value.astype(BF)

    def put_taps(base, turned):
        for a in range(3):
            y = dot(turned[:, a * 128 : a * 128 + 1024], gc[...])
            for b in range(3):
                tap = a * 3 + b
                mine = y[b * C : (b + 1) * C]
                put(base, tap * C, mine[:, 0:128])
                rest = mine[:, 128:256]
                put(base, REST + tap * 96, rest[0:96] + pltpu.roll(rest[96:192], 64, 1))

    es[...] = jnp.zeros_like(es)
    es[2:130, 0:96] = et[...]
    es[0:2, 0:96], es[130:132, 0:96] = ordered(flags[5], swap1[...], swap2[...])
    bw[...] = jnp.zeros_like(bw)
    for r in range(12):
        at, block = (r // 2) * 16, small[64 + 16 * (r % 2) : 80 + 16 * (r % 2), :]
        bw[at : at + 16, r * CP : (r + 1) * CP] = block
        bw[128 + at : 144 + at, r * CP : (r + 1) * CP] = block
    x = es[...]
    x_hi = x.astype(BF)
    x_lo = (x - x_hi.astype(F32)).astype(BF)
    both = jnp.concatenate([x_hi, x_lo], 1)
    for r in range(12):
        gs[8 + r * ROW : 8 + (r + 1) * ROW, :] = dot(both, bw[:, r * CP : (r + 1) * CP])
    for b in range(3):
        g2cat[:, b * CP : (b + 1) * CP] = gs[9 - b : 9 - b + N12, :].astype(BF)
    for r in range(8):
        at = 8 + (r + 2) * ROW + 2
        gc[r * 128 : r * 128 + 128, :] = gs[at : at + 128, :].astype(BF)
    put_taps(base_s, a1t)
    for part in range(5):
        at = part * 2 * ROW
        g = taps(g2cat, w2, at, 2 * ROW, -1)
        zs[8 + at : 8 + at + 2 * ROW, :] = g * gp[at : at + 2 * ROW, :].astype(F32)
    for b in range(3):
        gzcat[:, b * CP : (b + 1) * CP] = zs[9 - b : 9 - b + N10, :].astype(BF)
    for r in range(8):
        at = 8 + (r + 1) * ROW + 2
        gc[r * 128 : r * 128 + 128, :] = zs[at : at + 128, :].astype(BF)
    put_taps(base_f, h0t)
    for part in range(4):
        at = 8 + 2 * ROW + part * 2 * ROW
        gs[at : at + 2 * ROW, :] = gs[at : at + 2 * ROW, :] + taps(
            gzcat, w1, part * 2 * ROW, 2 * ROW, -1
        )
    for r in range(8):
        at = 8 + (r + 2) * ROW + 2
        gc[r * 128 : r * 128 + 128, :] = gs[at : at + 128, :].astype(BF)
    g_in = dot(fm[...], gc[...])
    g_fields = dot(small[0:64, :], gc[...], NT)
    for r in range(8):
        gfields[pl.ds(r, 64, stride=8), :] = g_fields[:, r * 128 : r * 128 + 128]
    line = jnp.concatenate([gf[r * 8 : r * 8 + 8, :] for r in range(8)], 1)
    line_hi = line.astype(BF).astype(F32)
    line2 = jnp.concatenate([line_hi, line - line_hi], 0).astype(BF)
    g_out = dot(line2, h2c[...])
    g_out = g_out[0:8] + g_out[8:16]
    put(base_s, EXTRA, g_in[:, 0:128])
    rest = g_in[:, 128:256]
    put(base_s, EXTRA + 64, rest[0:32] + pltpu.roll(rest[32:64], 64, 1))
    put(base_s, EXTRA + 96, jnp.zeros((HALF - EXTRA - 96, 128), F32))
    put(base_f, EXTRA, jnp.concatenate([g_out[:, 0:128], g_out[:, 128:256]], 0))
    put(base_f, EXTRA + 16, loss[...])
    put(base_f, EXTRA + 32, jnp.zeros((HALF - EXTRA - 32, 128), F32))


def unpack_kernel(flags, mine, other, second, first, g_in, g_out, loss, sv, fv, sems):
    def unpack(source, kernel, out, at):
        copies = []
        for tap in range(9):
            a, b = tap // 3, tap % 3
            kernel[a, b, :, 0:128] = source[tap * C : (tap + 1) * C, :].astype(F32)
            rest = source[REST + tap * 96 : REST + tap * 96 + 96, :].astype(F32)
            kernel[a, b, 0:96, 128:C] = rest[:, 0:64]
            kernel[a, b, 96:C, 128:C] = pltpu.roll(rest, 64, 1)[:, 0:64]
            if b == 2:
                copies.append(pltpu.make_async_copy(kernel.at[a], out.at[a], sems.at[at + a]))
                copies[-1].start()
        return copies

    def both(s, f):
        copies = unpack(s, sv, second, 0) + unpack(f, fv, first, 3)
        g_in[:, 0:128] = s[EXTRA : EXTRA + 64, :].astype(F32)
        rest = s[EXTRA + 64 : EXTRA + 96, :].astype(F32)
        g_in[0:32, 128:C] = rest[:, 0:64]
        g_in[32:64, 128:C] = pltpu.roll(rest, 64, 1)[:, 0:64]
        extra = f[EXTRA : EXTRA + 32, :].astype(F32)
        g_out[:, 0:128] = extra[0:6]
        g_out[:, 128:C] = extra[8:14, 0:64]
        loss[0, 0] = jnp.max(extra[16:24])
        for copy in copies:
            copy.wait()

    @pl.when(flags[4] == 0)
    def _():
        both(mine, other)

    @pl.when(flags[4] > 0)
    def _():
        both(other, mine)


def swaps(one, two, axis):
    count = lax.axis_size(axis)
    pairs = [[(i, i + 1) for i in range(start, count - 1, 2)] for start in range(2)]
    return tuple(
        lax.ppermute(x, axis, p + [(j, i) for i, j in p]) for x, p in zip((one, two), pairs)
    )


def exchange(rows, groups=None):
    return lax.all_to_all(
        rows, AXES, split_axis=0, concat_axis=0, tiled=True, axis_index_groups=groups
    )


def call(kernel, out_shapes, scratch, *operands, smem=0, any_out=0, smem_out=0, vmem=60, flops=0):
    vm, sm = pl.BlockSpec(memory_space=pltpu.VMEM), pl.BlockSpec(memory_space=pltpu.SMEM)
    return pl.pallas_call(
        kernel,
        out_shape=[jax.ShapeDtypeStruct(s, d) for s, d in out_shapes],
        in_specs=[sm] * smem + [vm] * (len(operands) - smem),
        out_specs=[pl.BlockSpec(memory_space=pl.ANY)] * any_out
        + [vm] * (len(out_shapes) - any_out - smem_out)
        + [sm] * smem_out,
        scratch_shapes=[pltpu.VMEM(*s) if isinstance(s, tuple) else s for s in scratch],
        compiler_params=pltpu.CompilerParams(vmem_limit_bytes=vmem * 1024 * 1024),
        cost_estimate=pl.CostEstimate(flops=flops, bytes_accessed=4_000_000, transcendentals=0),
    )(*operands)


def on_device(
    fields,
    w_in,
    conv_first,
    conv_second,
    w_out,
    slot_cells,
    slot_weights,
    slot_count,
    recv_obs,
    targets,
):
    ns, ew = lax.axis_index("ns"), lax.axis_index("ew")
    n_ns, n_ew = lax.axis_size("ns"), lax.axis_size("ew")
    flags = jnp.stack(
        [ns > 0, ns < n_ns - 1, ew > 0, ew < n_ew - 1, (ns & 1) > 0, (ew & 1) > 0]
    ).astype(F32)
    cells = slot_cells.reshape(4, 128, CAP)
    wts = slot_weights.reshape(4, 128, CAP)
    cnt = slot_count.reshape(128, 1)
    obs = recv_obs.reshape(128, CAP)
    turned = w_out.T
    small = jnp.concatenate(
        [w_in, jnp.pad(turned, ((0, 10), (0, 0))), jnp.pad(turned, ((8, 2), (0, 0)))], 0
    )
    small = jnp.pad(small, ((0, 0), (0, CP - C)))

    last, first = fields[:, 6:8].reshape(128, 128), fields[:, 0:2].reshape(128, 128)
    one, two = swaps(*ordered(ns & 1, first, last), "ns")
    fto, fm, own_west, own_east = call(
        own_kernel,
        [((1024, 64), BF), ((64, 1024), BF), ((16, 64), F32), ((16, 64), F32)],
        [((512, 128), F32)],
        fields.reshape(512, 128),
        vmem=8, flops=LONG,
    )
    ftr, one, two = call(
        rim_kernel,
        [((512, 64), BF), ((32, 64), BF), ((32, 64), BF)],
        [((128, 128), F32), ((128, 128), F32), ((32, 64), F32), ((32, 64), F32)],
        flags, one, two, own_west, own_east,
        smem=1, vmem=8, flops=LONG,
    )
    west, east = swaps(one, two, "ew")
    sent, a1, gp, h2c = call(
        forward_kernel,
        [((1024, 128), BF), ((N10, CP), BF), ((N10, CP), BF), ((1024, CP), BF)],
        [
            ((N12 + 16, CP), F32), ((N12, 3 * CP), BF), ((N10 + 16, CP), F32),
            ((N10, 3 * CP), BF), ((3, 3 * CP, CP), BF), ((3, 3 * CP, CP), BF),
            ((64, 128), I32), ((1024, 128), F32),
        ],
        flags, fto, ftr, west, east, small, conv_first, conv_second, cells, wts, cnt,
        smem=1, vmem=28, flops=2 * 10**9,
    )
    received = exchange(sent)
    a1t, h0t = call(
        turn_kernel,
        [((3 * C, 1280), BF), ((3 * C, 1280), BF)],
        [((N10, CP), F32), ((N12, 64), F32), ((1280, CP), BF), ((1280, 64), BF)],
        flags, a1, fto, ftr, west, east, small,
        smem=1, vmem=16, flops=10**9,
    )
    pred, loss, back = call(
        owner_kernel,
        [((6, 2048), F32), ((16, 128), F32), ((1024, 128), BF)],
        [
            ((96, 1024), BF), ((96, 1024), BF), ((128, 1024), BF), ((128, 1024), BF),
            ((96, 128), F32), ((128, 128), I32), ((1024, 128), F32),
        ],
        received, obs, targets,
        vmem=8, flops=10**9,
    )
    grads = exchange(back)
    g_field, one, two = call(
        spread_kernel,
        [((64, 128), F32), ((16, 128), F32), ((16, 128), F32)],
        [
            ((96, 4096), BF), ((96, 4096), BF), ((64, 4096), BF), ((64, 4096), BF),
            ((96, 64), F32),
        ],
        flags, grads, cells, wts, cnt,
        smem=1, vmem=12, flops=10**9,
    )
    one, two = swaps(one, two, "ns")
    et, one, two = call(
        turn_field_kernel,
        [((128, 96), F32), ((2, 96), F32), ((2, 96), F32)],
        [],
        flags, g_field, one, two,
        smem=1, vmem=4, flops=LONG,
    )
    one, two = swaps(one, two, "ew")
    pay, g_fields = call(
        backward_kernel,
        [((2 * HALF, 128), BF), ((512, 128), F32)],
        [
            ((ROW, 128), F32), ((CP, 12 * CP), BF), ((N12 + 16, CP), F32), ((N12, 3 * CP), BF),
            ((N10 + 16, CP), F32), ((N10, 3 * CP), BF), ((1024, CP), BF),
            ((3, CP, 3 * CP), BF), ((3, CP, 3 * CP), BF),
        ],
        flags, g_field, et, one, two, fm, a1t, h0t, gp, h2c, conv_second, conv_first, small, loss,
        smem=1, vmem=28, flops=2 * 10**9,
    )
    pairs = [(n, n ^ 1) for n in range(n_ns)]
    groups = [[n * n_ew + e for n in range(c, n_ns, 2) for e in range(n_ew)] for c in range(2)]
    theirs = lax.ppermute(pay[HALF:], "ns", pairs)
    summed = (pay[:HALF].astype(F32) + theirs.astype(F32)).astype(BF).reshape(64, PIECE, 128)
    share = jnp.sum(exchange(summed, groups).astype(F32), axis=0).astype(BF)
    mine = exchange(jnp.broadcast_to(share[None], (64, PIECE, 128)), groups).reshape(HALF, 128)
    other = lax.ppermute(mine, "ns", pairs)
    grad_second, grad_first, grad_in, g_out, total = call(
        unpack_kernel,
        [((3, 3, C, C), F32), ((3, 3, C, C), F32), ((64, C), F32), ((6, C), F32), ((1, 1), F32)],
        [((3, 3, C, C), F32), ((3, 3, C, C), F32), pltpu.SemaphoreType.DMA((6,))],
        flags, mine, other,
        smem=1, any_out=2, smem_out=1, vmem=16,
    )
    return (
        pred,
        total[0, 0],
        grad_first,
        grad_second,
        grad_in,
        g_out.T,
        g_fields.reshape(64, TH, TW),
    )


def solution(mesh):
    in_specs = (
        P(None, "ns", "ew"),
        P(),
        P(),
        P(),
        P(),
        P(("ns", "ew"), None, None),
        P(("ns", "ew"), None, None),
        P(("ns", "ew"), None),
        P(("ns", "ew"), None),
        P(None, ("ns", "ew")),
    )
    out_specs = (P(None, ("ns", "ew")), P(), P(), P(), P(), P(), P(None, "ns", "ew"))
    return jax.shard_map(
        on_device, mesh=mesh, in_specs=in_specs, out_specs=out_specs, check_vma=False
    )
```

```python
import jax
import jax.numpy as jnp
from jax import lax
from jax.experimental import pallas as pl
from jax.experimental.pallas import tpu as pltpu
from jax.sharding import PartitionSpec as P

BF = jnp.bfloat16
F32 = jnp.float32
I32 = jnp.int32
CAP = 128
TH, TW = 8, 128
C = 192
ROW = 144
N12, N10, N8 = 12 * ROW, 10 * ROW, 8 * ROW
CP = 256
AXES = ("ns", "ew")
PIECE = 48
HALF = 64 * PIECE
REST = 1728
EXTRA = 2592
LONG = 2 * 10**10
NT = (((1,), (1,)), ((), ()))
TN = (((0,), (0,)), ((), ()))


def dot(x, y, dims=(((1,), (0,)), ((), ()))):
    return lax.dot_general(x, y, dims, preferred_element_type=F32)


def taps(cat, weight, first, count, order):
    total = None
    for a in range(3):
        start = (a if order > 0 else 2 - a) * ROW + first
        rows = cat[start : start + count, :]
        term = dot(rows, weight[a]) if order > 0 else dot(rows, weight[a], NT)
        total = term if total is None else total + term
    return total


def stack_weights(out, kernel, order):
    out[...] = jnp.zeros_like(out)
    for a in range(3):
        for b in range(3):
            if order > 0:
                out[a, b * CP : b * CP + C, 0:C] = kernel[a, b]
            else:
                out[a, 0:C, b * CP : b * CP + C] = kernel[a, b]


def pick(table, row, index):
    return jnp.take_along_axis(
        jnp.broadcast_to(table[row : row + 1, :], (8, 128)),
        index,
        axis=1,
        mode="promise_in_bounds",
    )


def pack_pair(x, y):
    return x * 65536 + (y + 32768)


def unpack_pair(word):
    return (word >> 16).astype(F32), ((word & 65535) - 32768).astype(F32)


def ordered(odd, x, y):
    return jnp.where(odd > 0, x, y), jnp.where(odd > 0, y, x)


def own_kernel(f8, fto, fm, wo, eo, s8):
    s8[...] = f8[...].astype(F32)
    for r in range(8):
        block = s8[pl.ds(r, 64, stride=8), :]
        fm[:, r * 128 : r * 128 + 128] = block.astype(BF)
        turned = block.T
        fto[r * 128 : r * 128 + 128, :] = turned.astype(BF)
        wo[2 * r : 2 * r + 2, :] = turned[0:2]
        eo[2 * r : 2 * r + 2, :] = turned[126:128]


def rim_kernel(flags, swap1, swap2, wo, eo, ftr, out1, out2, sn, ss, sw, se):
    sn[...], ss[...] = ordered(flags[4], swap1[...].astype(F32), swap2[...].astype(F32))
    sw[...] = jnp.zeros_like(sw)
    se[...] = jnp.zeros_like(se)
    sw[4:20, :] = wo[...]
    se[4:20, :] = eo[...]
    for i in range(4):
        block = (sn if i < 2 else ss)[pl.ds(i % 2, 64, stride=2), :]
        r = i if i < 2 else i + 8
        turned = block.T
        ftr[i * 128 : i * 128 + 128, :] = turned.astype(BF)
        sw[2 * r : 2 * r + 2, :] = turned[0:2]
        se[2 * r : 2 * r + 2, :] = turned[126:128]
    one, two = ordered(flags[5], sw[...], se[...])
    out1[...] = one.astype(BF)
    out2[...] = two.astype(BF)


def row_of(own, rim, r):
    if 2 <= r < 10:
        return own[(r - 2) * 128 : (r - 1) * 128]
    i = r if r < 2 else r - 8
    return rim[i * 128 : i * 128 + 128]


def turn_field_kernel(flags, gf, swap1, swap2, et, out1, out2):
    north, south = ordered(flags[4], swap1[...], swap2[...])
    turned = jnp.concatenate([north, gf[...], south], 0).T
    et[...] = turned
    out1[...], out2[...] = ordered(flags[5], turned[0:2], turned[126:128])


def forward_kernel(
    flags, fto, ftr, swap1, swap2, small, c1, c2, cells, wts, cnt, out, a1_out, gp, h2c, hs, xcat,
    as_, acat, w1, w2, fq, pf,
):
    zero8 = jnp.zeros((8, CP), F32)
    hs[0:8, :] = zero8
    hs[N12 + 8 : N12 + 16, :] = zero8
    as_[0:8, :] = zero8
    as_[N10 + 8 : N10 + 16, :] = zero8
    stack_weights(w1, c1, 1)
    stack_weights(w2, c2, 1)
    own, rim = dot(fto[...], small[0:64, :]), dot(ftr[...], small[0:64, :])
    west, east = ordered(
        flags[5], dot(swap1[...], small[0:64, :]), dot(swap2[...], small[0:64, :])
    )
    for r in range(12):
        at = 8 + r * ROW
        hs[at + 128 : at + ROW, :] = jnp.zeros((ROW - 128, CP), F32)
        hs[at : at + 2, :] = west[2 * r : 2 * r + 2]
        hs[at + 2 : at + 130, :] = row_of(own, rim, r)
        hs[at + 130 : at + 132, :] = east[2 * r : 2 * r + 2]
    for b in range(3):
        xcat[:, b * CP : (b + 1) * CP] = hs[7 + b : 7 + b + N12, :].astype(BF)
    col = lax.broadcasted_iota(I32, (ROW, CP), 0)
    col_mask = jnp.where(col == 1, flags[2], jnp.where(col == 130, flags[3], 1.0))
    root = 0.7978845608028654
    for part in range(5):
        z2 = taps(xcat, w1, part * 2 * ROW, 2 * ROW, 1)
        for q in range(2):
            r = part * 2 + q
            z = z2[q * ROW : (q + 1) * ROW]
            mask = col_mask
            if r == 0:
                mask = col_mask * flags[0]
            if r == 9:
                mask = col_mask * flags[1]
            zz = z * z
            t = jnp.tanh(root * z * (1.0 + 0.044715 * zz))
            half = 0.5 * (1.0 + t)
            slope = half + 0.5 * z * (1.0 - t * t) * (root * (1.0 + 3 * 0.044715 * zz))
            a1 = z * half * mask
            as_[8 + r * ROW : 8 + (r + 1) * ROW, :] = a1
            a1_out[r * ROW : (r + 1) * ROW, :] = a1.astype(BF)
            gp[r * ROW : (r + 1) * ROW, :] = (slope * mask).astype(BF)
    for b in range(3):
        acat[:, b * CP : (b + 1) * CP] = as_[7 + b : 7 + b + N10, :].astype(BF)
    for part in range(4):
        at = part * 2 * ROW
        h2 = hs[8 + 2 * ROW + at : 8 + 4 * ROW + at, :] + taps(acat, w2, at, 2 * ROW, 1)
        as_[at : at + 2 * ROW, :] = h2
    for r in range(8):
        h2c[r * 128 : r * 128 + 128, :] = as_[r * ROW + 2 : r * ROW + 130, :].astype(BF)
    field = dot(small[64:80, :], h2c[...], NT)
    tiles = [field[0:8, r * 128 : r * 128 + 128] for r in range(8)]
    top = tiles[0]
    for r in range(1, 8):
        top = jnp.maximum(jnp.abs(top), jnp.abs(tiles[r]))
    largest = jnp.maximum(jnp.max(jnp.abs(top)), 1e-30)
    up = 32000.0 / largest
    down = largest * (1.0 / 32000.0)
    for r in range(8):
        whole = jnp.round(tiles[r] * up).astype(I32)
        fq[r * 8 : r * 8 + 3, :] = pack_pair(whole[0:3], whole[3:6])
    pf[...] = jnp.zeros_like(pf)
    lane = lax.broadcasted_iota(I32, (8, 128), 1)

    def owners(ob, carry):
        rows = pl.ds(pl.multiple_of(ob * 8, 8), 8)
        live = lane < cnt[rows, 0:1]
        sums = [jnp.zeros((8, 128), F32)] * 6
        for k in range(4):
            index = cells[k, rows, :]
            low, high = index & 127, index >> 7
            weight = jnp.where(live, wts[k, rows, :] * down, 0.0)
            got = [jnp.zeros((8, 128), I32)] * 3
            for r in range(8):
                here = high == r
                got = [jnp.where(here, pick(fq, r * 8 + v, low), got[v]) for v in range(3)]
            for v in range(3):
                x, y = unpack_pair(got[v])
                sums[v] = sums[v] + weight * x
                sums[v + 3] = sums[v + 3] + weight * y
        for v in range(6):
            pf[pl.ds(ob * 64 + v, 8, stride=8), :] = sums[v]
        return carry

    lax.fori_loop(0, 16, owners, 0, unroll=8)
    out[...] = pf[...].astype(BF)


def turn_kernel(flags, a1, fto, ftr, swap1, swap2, small, a1t, h0t, wide, thin, pa, pt):
    wide[...] = a1[...].astype(F32)
    west, east = ordered(flags[5], swap1[...].astype(F32), swap2[...].astype(F32))
    for r in range(12):
        at = r * ROW
        thin[at : at + 2, :] = west[2 * r : 2 * r + 2]
        thin[at + 2 : at + 130, :] = row_of(fto, ftr, r).astype(F32)
        thin[at + 130 : at + 132, :] = east[2 * r : 2 * r + 2]
    ones = lax.broadcasted_iota(I32, (CP, CP), 0) == lax.broadcasted_iota(I32, (CP, CP), 1)
    same = jnp.where(ones, 1.0, 0.0).astype(BF)
    win_t = dot(same[0:C, :], small[0:64, :], NT).astype(BF)
    for b in range(3):
        for r in range(10):
            at = slice(r * 128, r * 128 + 128)
            pa[at, :] = wide[r * ROW + 1 + b : r * ROW + 129 + b, :].astype(BF)
            pt[at, :] = thin[(r + 1) * ROW + 1 + b : (r + 1) * ROW + 129 + b, :].astype(BF)
        a1t[b * C : (b + 1) * C, :] = dot(same[0:C, :], pa[...], NT).astype(BF)
        h0t[b * C : (b + 1) * C, :] = dot(win_t, pt[...], NT).astype(BF)


def spread_row(row):
    return jnp.broadcast_to(row, (16, 128)).astype(BF)


def iotas(count):
    base = lax.broadcasted_iota(I32, (16, 128), 0)
    return [(base + 16 * m).astype(F32).astype(BF) for m in range(count)]


def overlapped(count, build, multiply):
    build(0, 0)

    def step(i, carry):
        build(2 * i + 1, 1)
        multiply(0)
        build(jnp.minimum(2 * i + 2, count - 1), 0)
        multiply(1)
        return carry

    lax.fori_loop(0, count // 2, step, 0)


def owner_kernel(recv, obs, target, pred, loss, out, l0, l1, r0, r1, total, rq, gf):
    steps = iotas(8)
    none = jnp.zeros((16, 128), BF)
    one = jnp.ones((16, 128), BF)
    lefts, rights = (l0, l1), (r0, r1)

    def collect(group, slot):
        for q in range(4):
            collect_eight(group * 4 + q, q * 1024, lefts[slot], rights[slot])

    def collect_eight(tb, start, left, right):
        block = recv[pl.ds(pl.multiple_of(tb * 64, 64), 64), :].astype(F32)
        index = obs[pl.ds(pl.multiple_of(tb * 8, 8), 8), :]
        low = (index & 127).astype(F32)
        high = (index >> 7).astype(F32)
        for i in range(8):
            at = slice(start + i * 128, start + i * 128 + 128)
            here = spread_row(high[i : i + 1]) == steps[0]
            for v in range(6):
                value = spread_row(block[i * 8 + v : i * 8 + v + 1])
                left[v * 16 : v * 16 + 16, at] = jnp.where(here, value, none)
            mine = spread_row(low[i : i + 1])
            for m in range(8):
                right[m * 16 : m * 16 + 16, at] = jnp.where(mine == steps[m], one, none)

    def multiply(slot):
        total[...] += dot(lefts[slot][...], rights[slot][...], NT)

    total[...] = jnp.zeros_like(total)
    overlapped(4, collect, multiply)
    scale = 1.0 / (6 * 2048)
    squares = jnp.zeros((6, 128), F32)
    resids = []
    for h in range(16):
        at = slice(h * 128, h * 128 + 128)
        mine = total[pl.ds(h, 6, stride=16), :]
        pred[:, at] = mine
        resid = mine - target[:, at]
        squares = squares + resid * resid
        resids.append(resid * scale)
    loss[...] = jnp.full((16, 128), jnp.sum(squares) * (0.5 * scale), F32)
    top = jnp.abs(resids[0])
    for h in range(1, 16):
        top = jnp.maximum(top, jnp.abs(resids[h]))
    largest = jnp.maximum(jnp.max(top), 1e-30)
    up = 32000.0 / largest
    down = largest * (1.0 / 32000.0)
    for h in range(16):
        whole = jnp.round(resids[h] * up).astype(I32)
        rq[h * 8 : h * 8 + 3, :] = pack_pair(whole[0:3], whole[3:6])
    gf[...] = jnp.zeros_like(gf)

    def choose(tb, carry):
        index = obs[pl.ds(pl.multiple_of(tb * 8, 8), 8), :]
        low, high = index & 127, index >> 7
        got = [jnp.zeros((8, 128), I32)] * 3
        for h in range(16):
            here = high == h
            got = [jnp.where(here, pick(rq, h * 8 + v, low), got[v]) for v in range(3)]
        for v in range(3):
            x, y = unpack_pair(got[v])
            gf[pl.ds(tb * 64 + v, 8, stride=8), :] = x * down
            gf[pl.ds(tb * 64 + v + 3, 8, stride=8), :] = y * down
        return carry

    lax.fori_loop(0, 16, choose, 0, unroll=8)
    out[...] = gf[...].astype(BF)


def spread_kernel(
    flags, grad, cells, wts, cnt, out, out1, out2, l0, l1, r0, r1, total
):
    lefts, rights = (l0, l1), (r0, r1)
    steps = iotas(4)
    none = jnp.zeros((16, 128), BF)
    total[...] = jnp.zeros_like(total)
    lane = lax.broadcasted_iota(I32, (8, 128), 1)

    def owners(group, slot):
        for q in range(2):
            owners_eight(group * 2 + q, q * 4096, lefts[slot], rights[slot])

    def owners_eight(ob, start, left, right):
        rows = pl.ds(pl.multiple_of(ob * 8, 8), 8)
        live = lane < cnt[rows, 0:1]
        block = grad[pl.ds(pl.multiple_of(ob * 64, 64), 64), :].astype(F32)
        index = [cells[k, rows, :] for k in range(4)]
        low = [(i & 63).astype(F32) for i in index]
        high = [(i >> 6).astype(F32) for i in index]
        weight = [jnp.where(live, wts[k, rows, :], 0.0) for k in range(4)]
        for i in range(8):
            values = [spread_row(block[i * 8 + v : i * 8 + v + 1]) for v in range(6)]
            for k in range(4):
                at = slice(start + (i * 4 + k) * 128, start + (i * 4 + k) * 128 + 128)
                here = spread_row(high[k][i : i + 1]) == steps[0]
                for v in range(6):
                    left[v * 16 : v * 16 + 16, at] = jnp.where(here, values[v], none)
                mine = spread_row(low[k][i : i + 1])
                amount = spread_row(weight[k][i : i + 1])
                for m in range(4):
                    right[m * 16 : m * 16 + 16, at] = jnp.where(mine == steps[m], amount, none)

    def multiply(slot):
        total[...] += dot(lefts[slot][...], rights[slot][...], NT)

    overlapped(8, owners, multiply)
    out[...] = jnp.zeros_like(out)
    for r in range(8):
        even = total[pl.ds(2 * r, 6, stride=16), :]
        odd = total[pl.ds(2 * r + 1, 6, stride=16), :]
        out[r * 8 : r * 8 + 6, :] = jnp.concatenate([even, odd], 1)
    out1[...], out2[...] = ordered(flags[4], out[0:16, :], out[48:64, :])


def backward_kernel(
    flags, gf, et, swap1, swap2, fm, a1t, h0t, gp, h2c, c2, c1, small, loss, pay, gfields, es, bw,
    gs, g2cat, zs, gzcat, gc, w2, w1,
):
    zero8 = jnp.zeros((8, CP), F32)
    gs[0:8, :] = zero8
    gs[N12 + 8 : N12 + 16, :] = zero8
    zs[0:8, :] = zero8
    zs[N10 + 8 : N10 + 16, :] = zero8
    stack_weights(w2, c2, -1)
    stack_weights(w1, c1, -1)
    core = (flags[4] > 0).astype(I32)
    base_s = pl.multiple_of(core * HALF, 16)
    base_f = pl.multiple_of((1 - core) * HALF, 16)

    def put(base, at, value):
        pay[pl.ds(pl.multiple_of(base + at, 16), value.shape[0]), :] = value.astype(BF)

    def put_taps(base, turned):
        for a in range(3):
            y = dot(turned[:, a * 128 : a * 128 + 1024], gc[...])
            for b in range(3):
                tap = a * 3 + b
                mine = y[b * C : (b + 1) * C]
                put(base, tap * C, mine[:, 0:128])
                rest = mine[:, 128:256]
                put(base, REST + tap * 96, rest[0:96] + pltpu.roll(rest[96:192], 64, 1))

    es[...] = jnp.zeros_like(es)
    es[2:130, 0:96] = et[...]
    es[0:2, 0:96], es[130:132, 0:96] = ordered(flags[5], swap1[...], swap2[...])
    bw[...] = jnp.zeros_like(bw)
    for r in range(12):
        at, block = (r // 2) * 16, small[64 + 16 * (r % 2) : 80 + 16 * (r % 2), :]
        bw[at : at + 16, r * CP : (r + 1) * CP] = block
        bw[128 + at : 144 + at, r * CP : (r + 1) * CP] = block
    x = es[...]
    x_hi = x.astype(BF)
    x_lo = (x - x_hi.astype(F32)).astype(BF)
    both = jnp.concatenate([x_hi, x_lo], 1)
    for r in range(12):
        gs[8 + r * ROW : 8 + (r + 1) * ROW, :] = dot(both, bw[:, r * CP : (r + 1) * CP])
    for b in range(3):
        g2cat[:, b * CP : (b + 1) * CP] = gs[9 - b : 9 - b + N12, :].astype(BF)
    for r in range(8):
        at = 8 + (r + 2) * ROW + 2
        gc[r * 128 : r * 128 + 128, :] = gs[at : at + 128, :].astype(BF)
    put_taps(base_s, a1t)
    for part in range(5):
        at = part * 2 * ROW
        g = taps(g2cat, w2, at, 2 * ROW, -1)
        zs[8 + at : 8 + at + 2 * ROW, :] = g * gp[at : at + 2 * ROW, :].astype(F32)
    for b in range(3):
        gzcat[:, b * CP : (b + 1) * CP] = zs[9 - b : 9 - b + N10, :].astype(BF)
    for r in range(8):
        at = 8 + (r + 1) * ROW + 2
        gc[r * 128 : r * 128 + 128, :] = zs[at : at + 128, :].astype(BF)
    put_taps(base_f, h0t)
    for part in range(4):
        at = 8 + 2 * ROW + part * 2 * ROW
        gs[at : at + 2 * ROW, :] = gs[at : at + 2 * ROW, :] + taps(
            gzcat, w1, part * 2 * ROW, 2 * ROW, -1
        )
    for r in range(8):
        at = 8 + (r + 2) * ROW + 2
        gc[r * 128 : r * 128 + 128, :] = gs[at : at + 128, :].astype(BF)
    g_in = dot(fm[...], gc[...])
    g_fields = dot(small[0:64, :], gc[...], NT)
    for r in range(8):
        gfields[pl.ds(r, 64, stride=8), :] = g_fields[:, r * 128 : r * 128 + 128]
    line = jnp.concatenate([gf[r * 8 : r * 8 + 8, :] for r in range(8)], 1)
    line_hi = line.astype(BF).astype(F32)
    line2 = jnp.concatenate([line_hi, line - line_hi], 0).astype(BF)
    g_out = dot(line2, h2c[...])
    g_out = g_out[0:8] + g_out[8:16]
    put(base_s, EXTRA, g_in[:, 0:128])
    rest = g_in[:, 128:256]
    put(base_s, EXTRA + 64, rest[0:32] + pltpu.roll(rest[32:64], 64, 1))
    put(base_s, EXTRA + 96, jnp.zeros((HALF - EXTRA - 96, 128), F32))
    put(base_f, EXTRA, jnp.concatenate([g_out[:, 0:128], g_out[:, 128:256]], 0))
    put(base_f, EXTRA + 16, loss[...])
    put(base_f, EXTRA + 32, jnp.zeros((HALF - EXTRA - 32, 128), F32))


def unpack_kernel(flags, mine, other, second, first, g_in, g_out, loss):
    def unpack(source, kernel):
        for tap in range(9):
            a, b = tap // 3, tap % 3
            kernel[a, b, :, 0:128] = source[tap * C : (tap + 1) * C, :].astype(F32)
            rest = source[REST + tap * 96 : REST + tap * 96 + 96, :].astype(F32)
            kernel[a, b, 0:96, 128:C] = rest[:, 0:64]
            kernel[a, b, 96:C, 128:C] = pltpu.roll(rest, 64, 1)[:, 0:64]

    def both(s, f):
        unpack(s, second)
        unpack(f, first)
        g_in[:, 0:128] = s[EXTRA : EXTRA + 64, :].astype(F32)
        rest = s[EXTRA + 64 : EXTRA + 96, :].astype(F32)
        g_in[0:32, 128:C] = rest[:, 0:64]
        g_in[32:64, 128:C] = pltpu.roll(rest, 64, 1)[:, 0:64]
        extra = f[EXTRA : EXTRA + 32, :].astype(F32)
        g_out[:, 0:128] = extra[0:6]
        g_out[:, 128:C] = extra[8:14, 0:64]
        loss[0, 0] = jnp.max(extra[16:24])

    @pl.when(flags[4] == 0)
    def _():
        both(mine, other)

    @pl.when(flags[4] > 0)
    def _():
        both(other, mine)


def swaps(one, two, axis):
    count = lax.axis_size(axis)
    pairs = [[(i, i + 1) for i in range(start, count - 1, 2)] for start in range(2)]
    return tuple(
        lax.ppermute(x, axis, p + [(j, i) for i, j in p]) for x, p in zip((one, two), pairs)
    )


def exchange(rows, groups=None):
    return lax.all_to_all(
        rows, AXES, split_axis=0, concat_axis=0, tiled=True, axis_index_groups=groups
    )


def call(kernel, out_shapes, scratch, *operands, smem=0, smem_out=0, vmem=60, flops=0):
    vm, sm = pl.BlockSpec(memory_space=pltpu.VMEM), pl.BlockSpec(memory_space=pltpu.SMEM)
    return pl.pallas_call(
        kernel,
        out_shape=[jax.ShapeDtypeStruct(s, d) for s, d in out_shapes],
        in_specs=[sm] * smem + [vm] * (len(operands) - smem),
        out_specs=[vm] * (len(out_shapes) - smem_out) + [sm] * smem_out,
        scratch_shapes=[pltpu.VMEM(s, d) for s, d in scratch],
        compiler_params=pltpu.CompilerParams(vmem_limit_bytes=vmem * 1024 * 1024),
        cost_estimate=pl.CostEstimate(flops=flops, bytes_accessed=4_000_000, transcendentals=0),
    )(*operands)


def on_device(
    fields,
    w_in,
    conv_first,
    conv_second,
    w_out,
    slot_cells,
    slot_weights,
    slot_count,
    recv_obs,
    targets,
):
    ns, ew = lax.axis_index("ns"), lax.axis_index("ew")
    n_ns, n_ew = lax.axis_size("ns"), lax.axis_size("ew")
    flags = jnp.stack(
        [ns > 0, ns < n_ns - 1, ew > 0, ew < n_ew - 1, (ns & 1) > 0, (ew & 1) > 0]
    ).astype(F32)
    cells = slot_cells.reshape(4, 128, CAP)
    wts = slot_weights.reshape(4, 128, CAP)
    cnt = slot_count.reshape(128, 1)
    obs = recv_obs.reshape(128, CAP)
    turned = w_out.T
    small = jnp.concatenate(
        [w_in, jnp.pad(turned, ((0, 10), (0, 0))), jnp.pad(turned, ((8, 2), (0, 0)))], 0
    )
    small = jnp.pad(small, ((0, 0), (0, CP - C)))

    last, first = fields[:, 6:8].reshape(128, 128), fields[:, 0:2].reshape(128, 128)
    one, two = swaps(*ordered(ns & 1, first, last), "ns")
    fto, fm, own_west, own_east = call(
        own_kernel,
        [((1024, 64), BF), ((64, 1024), BF), ((16, 64), F32), ((16, 64), F32)],
        [((512, 128), F32)],
        fields.reshape(512, 128),
        vmem=8, flops=LONG,
    )
    ftr, one, two = call(
        rim_kernel,
        [((512, 64), BF), ((32, 64), BF), ((32, 64), BF)],
        [((128, 128), F32), ((128, 128), F32), ((32, 64), F32), ((32, 64), F32)],
        flags, one, two, own_west, own_east,
        smem=1, vmem=8, flops=LONG,
    )
    west, east = swaps(one, two, "ew")
    sent, a1, gp, h2c = call(
        forward_kernel,
        [((1024, 128), BF), ((N10, CP), BF), ((N10, CP), BF), ((1024, CP), BF)],
        [
            ((N12 + 16, CP), F32), ((N12, 3 * CP), BF), ((N10 + 16, CP), F32),
            ((N10, 3 * CP), BF), ((3, 3 * CP, CP), BF), ((3, 3 * CP, CP), BF),
            ((64, 128), I32), ((1024, 128), F32),
        ],
        flags, fto, ftr, west, east, small, conv_first, conv_second, cells, wts, cnt,
        smem=1, vmem=28, flops=2 * 10**9,
    )
    received = exchange(sent)
    a1t, h0t = call(
        turn_kernel,
        [((3 * C, 1280), BF), ((3 * C, 1280), BF)],
        [((N10, CP), F32), ((N12, 64), F32), ((1280, CP), BF), ((1280, 64), BF)],
        flags, a1, fto, ftr, west, east, small,
        smem=1, vmem=16, flops=10**9,
    )
    pred, loss, back = call(
        owner_kernel,
        [((6, 2048), F32), ((16, 128), F32), ((1024, 128), BF)],
        [
            ((96, 4096), BF), ((96, 4096), BF), ((128, 4096), BF), ((128, 4096), BF),
            ((96, 128), F32), ((128, 128), I32), ((1024, 128), F32),
        ],
        received, obs, targets,
        vmem=12, flops=10**9,
    )
    grads = exchange(back)
    g_field, one, two = call(
        spread_kernel,
        [((64, 128), F32), ((16, 128), F32), ((16, 128), F32)],
        [
            ((96, 8192), BF), ((96, 8192), BF), ((64, 8192), BF), ((64, 8192), BF),
            ((96, 64), F32),
        ],
        flags, grads, cells, wts, cnt,
        smem=1, vmem=16, flops=10**9,
    )
    one, two = swaps(one, two, "ns")
    et, one, two = call(
        turn_field_kernel,
        [((128, 96), F32), ((2, 96), F32), ((2, 96), F32)],
        [],
        flags, g_field, one, two,
        smem=1, vmem=4, flops=LONG,
    )
    one, two = swaps(one, two, "ew")
    pay, g_fields = call(
        backward_kernel,
        [((2 * HALF, 128), BF), ((512, 128), F32)],
        [
            ((ROW, 128), F32), ((CP, 12 * CP), BF), ((N12 + 16, CP), F32), ((N12, 3 * CP), BF),
            ((N10 + 16, CP), F32), ((N10, 3 * CP), BF), ((1024, CP), BF),
            ((3, CP, 3 * CP), BF), ((3, CP, 3 * CP), BF),
        ],
        flags, g_field, et, one, two, fm, a1t, h0t, gp, h2c, conv_second, conv_first, small, loss,
        smem=1, vmem=28, flops=2 * 10**9,
    )
    pairs = [(n, n ^ 1) for n in range(n_ns)]
    groups = [[n * n_ew + e for n in range(c, n_ns, 2) for e in range(n_ew)] for c in range(2)]
    theirs = lax.ppermute(pay[HALF:], "ns", pairs)
    summed = (pay[:HALF].astype(F32) + theirs.astype(F32)).astype(BF).reshape(64, PIECE, 128)
    share = jnp.sum(exchange(summed, groups).astype(F32), axis=0).astype(BF)
    mine = exchange(jnp.broadcast_to(share[None], (64, PIECE, 128)), groups).reshape(HALF, 128)
    other = lax.ppermute(mine, "ns", pairs)
    grad_second, grad_first, grad_in, g_out, total = call(
        unpack_kernel,
        [((3, 3, C, C), F32), ((3, 3, C, C), F32), ((64, C), F32), ((6, C), F32), ((1, 1), F32)],
        [],
        flags, mine, other,
        smem=1, smem_out=1, vmem=16,
    )
    return (
        pred,
        total[0, 0],
        grad_first,
        grad_second,
        grad_in,
        g_out.T,
        g_fields.reshape(64, TH, TW),
    )


def solution(mesh):
    in_specs = (
        P(None, "ns", "ew"),
        P(),
        P(),
        P(),
        P(),
        P(("ns", "ew"), None, None),
        P(("ns", "ew"), None, None),
        P(("ns", "ew"), None),
        P(("ns", "ew"), None),
        P(None, ("ns", "ew")),
    )
    out_specs = (P(None, ("ns", "ew")), P(), P(), P(), P(), P(), P(None, "ns", "ew"))
    return jax.shard_map(
        on_device, mesh=mesh, in_specs=in_specs, out_specs=out_specs, check_vma=False
    )
```

```python
import jax
import jax.numpy as jnp
from jax import lax
from jax.experimental import pallas as pl
from jax.experimental.pallas import tpu as pltpu
from jax.sharding import PartitionSpec as P

BF = jnp.bfloat16
F32 = jnp.float32
I32 = jnp.int32
CAP = 128
TH, TW = 8, 128
C = 192
ROW = 144
N12, N10, N8 = 12 * ROW, 10 * ROW, 8 * ROW
CP = 256
AXES = ("ns", "ew")
PIECE = 48
HALF = 64 * PIECE
REST = 1728
EXTRA = 2592
LONG = 2 * 10**10
NT = (((1,), (1,)), ((), ()))
TN = (((0,), (0,)), ((), ()))


def dot(x, y, dims=(((1,), (0,)), ((), ()))):
    return lax.dot_general(x, y, dims, preferred_element_type=F32)


def taps(cat, weight, first, count, order):
    total = None
    for a in range(3):
        start = (a if order > 0 else 2 - a) * ROW + first
        rows = cat[start : start + count, :]
        term = dot(rows, weight[a]) if order > 0 else dot(rows, weight[a], NT)
        total = term if total is None else total + term
    return total


def stack_weights(out, kernel, order):
    out[...] = jnp.zeros_like(out)
    for a in range(3):
        for b in range(3):
            if order > 0:
                out[a, b * CP : b * CP + C, 0:C] = kernel[a, b]
            else:
                out[a, 0:C, b * CP : b * CP + C] = kernel[a, b]


def pick(table, row, index):
    return jnp.take_along_axis(
        jnp.broadcast_to(table[row : row + 1, :], (8, 128)),
        index,
        axis=1,
        mode="promise_in_bounds",
    )


def pack_pair(x, y):
    return x * 65536 + (y + 32768)


def unpack_pair(word):
    return (word >> 16).astype(F32), ((word & 65535) - 32768).astype(F32)


def ordered(odd, x, y):
    return jnp.where(odd > 0, x, y), jnp.where(odd > 0, y, x)


def own_kernel(f8, fto, fm, wo, eo, s8):
    s8[...] = f8[...].astype(F32)
    for r in range(8):
        block = s8[pl.ds(r, 64, stride=8), :]
        fm[:, r * 128 : r * 128 + 128] = block.astype(BF)
        turned = block.T
        fto[r * 128 : r * 128 + 128, :] = turned.astype(BF)
        wo[2 * r : 2 * r + 2, :] = turned[0:2]
        eo[2 * r : 2 * r + 2, :] = turned[126:128]


def rim_kernel(flags, swap1, swap2, wo, eo, ftr, out1, out2, sn, ss, sw, se):
    sn[...], ss[...] = ordered(flags[4], swap1[...].astype(F32), swap2[...].astype(F32))
    sw[...] = jnp.zeros_like(sw)
    se[...] = jnp.zeros_like(se)
    sw[4:20, :] = wo[...]
    se[4:20, :] = eo[...]
    for i in range(4):
        block = (sn if i < 2 else ss)[pl.ds(i % 2, 64, stride=2), :]
        r = i if i < 2 else i + 8
        turned = block.T
        ftr[i * 128 : i * 128 + 128, :] = turned.astype(BF)
        sw[2 * r : 2 * r + 2, :] = turned[0:2]
        se[2 * r : 2 * r + 2, :] = turned[126:128]
    one, two = ordered(flags[5], sw[...], se[...])
    out1[...] = one.astype(BF)
    out2[...] = two.astype(BF)


def row_of(own, rim, r):
    if 2 <= r < 10:
        return own[(r - 2) * 128 : (r - 1) * 128]
    i = r if r < 2 else r - 8
    return rim[i * 128 : i * 128 + 128]


def turn_field_kernel(flags, gf, swap1, swap2, et, out1, out2):
    north, south = ordered(flags[4], swap1[...], swap2[...])
    turned = jnp.concatenate([north, gf[...], south], 0).T
    et[...] = turned
    out1[...], out2[...] = ordered(flags[5], turned[0:2], turned[126:128])


def forward_kernel(
    flags, fto, ftr, swap1, swap2, small, c1, c2, cells, wts, cnt, out, a1_out, gp, h2c, hs, xcat,
    as_, acat, w1, w2, fq, pf,
):
    zero8 = jnp.zeros((8, CP), F32)
    hs[0:8, :] = zero8
    hs[N12 + 8 : N12 + 16, :] = zero8
    as_[0:8, :] = zero8
    as_[N10 + 8 : N10 + 16, :] = zero8
    stack_weights(w1, c1, 1)
    stack_weights(w2, c2, 1)
    own, rim = dot(fto[...], small[0:64, :]), dot(ftr[...], small[0:64, :])
    west, east = ordered(
        flags[5], dot(swap1[...], small[0:64, :]), dot(swap2[...], small[0:64, :])
    )
    for r in range(12):
        at = 8 + r * ROW
        hs[at + 128 : at + ROW, :] = jnp.zeros((ROW - 128, CP), F32)
        hs[at : at + 2, :] = west[2 * r : 2 * r + 2]
        hs[at + 2 : at + 130, :] = row_of(own, rim, r)
        hs[at + 130 : at + 132, :] = east[2 * r : 2 * r + 2]
    for b in range(3):
        xcat[:, b * CP : (b + 1) * CP] = hs[7 + b : 7 + b + N12, :].astype(BF)
    col = lax.broadcasted_iota(I32, (ROW, CP), 0)
    col_mask = jnp.where(col == 1, flags[2], jnp.where(col == 130, flags[3], 1.0))
    root = 0.7978845608028654
    for part in range(5):
        z2 = taps(xcat, w1, part * 2 * ROW, 2 * ROW, 1)
        for q in range(2):
            r = part * 2 + q
            z = z2[q * ROW : (q + 1) * ROW]
            mask = col_mask
            if r == 0:
                mask = col_mask * flags[0]
            if r == 9:
                mask = col_mask * flags[1]
            zz = z * z
            t = jnp.tanh(root * z * (1.0 + 0.044715 * zz))
            half = 0.5 * (1.0 + t)
            slope = half + 0.5 * z * (1.0 - t * t) * (root * (1.0 + 3 * 0.044715 * zz))
            a1 = z * half * mask
            as_[8 + r * ROW : 8 + (r + 1) * ROW, :] = a1
            a1_out[r * ROW : (r + 1) * ROW, :] = a1.astype(BF)
            gp[r * ROW : (r + 1) * ROW, :] = (slope * mask).astype(BF)
    for b in range(3):
        acat[:, b * CP : (b + 1) * CP] = as_[7 + b : 7 + b + N10, :].astype(BF)
    for part in range(4):
        at = part * 2 * ROW
        h2 = hs[8 + 2 * ROW + at : 8 + 4 * ROW + at, :] + taps(acat, w2, at, 2 * ROW, 1)
        as_[at : at + 2 * ROW, :] = h2
    for r in range(8):
        h2c[r * 128 : r * 128 + 128, :] = as_[r * ROW + 2 : r * ROW + 130, :].astype(BF)
    field = dot(small[64:80, :], h2c[...], NT)
    tiles = [field[0:8, r * 128 : r * 128 + 128] for r in range(8)]
    top = tiles[0]
    for r in range(1, 8):
        top = jnp.maximum(jnp.abs(top), jnp.abs(tiles[r]))
    largest = jnp.maximum(jnp.max(jnp.abs(top)), 1e-30)
    up = 32000.0 / largest
    down = largest * (1.0 / 32000.0)
    for r in range(8):
        whole = jnp.round(tiles[r] * up).astype(I32)
        fq[r * 8 : r * 8 + 3, :] = pack_pair(whole[0:3], whole[3:6])
    pf[...] = jnp.zeros_like(pf)
    lane = lax.broadcasted_iota(I32, (8, 128), 1)

    def owners(ob, carry):
        rows = pl.ds(pl.multiple_of(ob * 8, 8), 8)
        live = lane < cnt[rows, 0:1]
        sums = [jnp.zeros((8, 128), F32)] * 6
        for k in range(4):
            index = cells[k, rows, :]
            low, high = index & 127, index >> 7
            weight = jnp.where(live, wts[k, rows, :] * down, 0.0)
            got = [jnp.zeros((8, 128), I32)] * 3
            for r in range(8):
                here = high == r
                got = [jnp.where(here, pick(fq, r * 8 + v, low), got[v]) for v in range(3)]
            for v in range(3):
                x, y = unpack_pair(got[v])
                sums[v] = sums[v] + weight * x
                sums[v + 3] = sums[v + 3] + weight * y
        for v in range(6):
            pf[pl.ds(ob * 64 + v, 8, stride=8), :] = sums[v]
        return carry

    lax.fori_loop(0, 16, owners, 0, unroll=8)
    out[...] = pf[...].astype(BF)


def turn_kernel(flags, a1, fto, ftr, swap1, swap2, small, a1t, h0t, wide, thin, pa, pt):
    wide[...] = a1[...].astype(F32)
    west, east = ordered(flags[5], swap1[...].astype(F32), swap2[...].astype(F32))
    for r in range(12):
        at = r * ROW
        thin[at : at + 2, :] = west[2 * r : 2 * r + 2]
        thin[at + 2 : at + 130, :] = row_of(fto, ftr, r).astype(F32)
        thin[at + 130 : at + 132, :] = east[2 * r : 2 * r + 2]
    ones = lax.broadcasted_iota(I32, (CP, CP), 0) == lax.broadcasted_iota(I32, (CP, CP), 1)
    same = jnp.where(ones, 1.0, 0.0).astype(BF)
    win_t = dot(same[0:C, :], small[0:64, :], NT).astype(BF)
    for b in range(3):
        for r in range(10):
            at = slice(r * 128, r * 128 + 128)
            pa[at, :] = wide[r * ROW + 1 + b : r * ROW + 129 + b, :].astype(BF)
            pt[at, :] = thin[(r + 1) * ROW + 1 + b : (r + 1) * ROW + 129 + b, :].astype(BF)
        a1t[b * C : (b + 1) * C, :] = dot(same[0:C, :], pa[...], NT).astype(BF)
        h0t[b * C : (b + 1) * C, :] = dot(win_t, pt[...], NT).astype(BF)


def spread_row(row):
    return jnp.broadcast_to(row, (16, 128)).astype(BF)


def iotas(count):
    base = lax.broadcasted_iota(I32, (16, 128), 0)
    return [(base + 16 * m).astype(F32).astype(BF) for m in range(count)]


def overlapped(count, build, multiply):
    build(0, 0)

    def step(i, carry):
        build(2 * i + 1, 1)
        multiply(0)
        build(jnp.minimum(2 * i + 2, count - 1), 0)
        multiply(1)
        return carry

    lax.fori_loop(0, count // 2, step, 0)


def owner_kernel(recv, obs, target, pred, loss, out, l0, l1, r0, r1, total, rq, gf):
    steps = iotas(8)
    none = jnp.zeros((16, 128), BF)
    one = jnp.ones((16, 128), BF)
    lefts, rights = (l0, l1), (r0, r1)

    def collect(group, slot):
        for q in range(4):
            collect_eight(group * 4 + q, q * 1024, lefts[slot], rights[slot])

    def collect_eight(tb, start, left, right):
        block = recv[pl.ds(pl.multiple_of(tb * 64, 64), 64), :].astype(F32)
        index = obs[pl.ds(pl.multiple_of(tb * 8, 8), 8), :]
        low = (index & 127).astype(F32)
        high = (index >> 7).astype(F32)
        for i in range(8):
            at = slice(start + i * 128, start + i * 128 + 128)
            here = spread_row(high[i : i + 1]) == steps[0]
            for v in range(6):
                value = spread_row(block[i * 8 + v : i * 8 + v + 1])
                left[v * 16 : v * 16 + 16, at] = jnp.where(here, value, none)
            mine = spread_row(low[i : i + 1])
            for m in range(8):
                right[m * 16 : m * 16 + 16, at] = jnp.where(mine == steps[m], one, none)

    def multiply(slot):
        total[...] += dot(lefts[slot][...], rights[slot][...], NT)

    total[...] = jnp.zeros_like(total)
    overlapped(4, collect, multiply)
    scale = 1.0 / (6 * 2048)
    squares = jnp.zeros((6, 128), F32)
    resids = []
    for h in range(16):
        at = slice(h * 128, h * 128 + 128)
        mine = total[pl.ds(h, 6, stride=16), :]
        pred[:, at] = mine
        resid = mine - target[:, at]
        squares = squares + resid * resid
        resids.append(resid * scale)
    loss[...] = jnp.full((16, 128), jnp.sum(squares) * (0.5 * scale), F32)
    top = jnp.abs(resids[0])
    for h in range(1, 16):
        top = jnp.maximum(top, jnp.abs(resids[h]))
    largest = jnp.maximum(jnp.max(top), 1e-30)
    up = 32000.0 / largest
    down = largest * (1.0 / 32000.0)
    for h in range(16):
        whole = jnp.round(resids[h] * up).astype(I32)
        rq[h * 8 : h * 8 + 3, :] = pack_pair(whole[0:3], whole[3:6])
    gf[...] = jnp.zeros_like(gf)

    def choose(tb, carry):
        index = obs[pl.ds(pl.multiple_of(tb * 8, 8), 8), :]
        low, high = index & 127, index >> 7
        got = [jnp.zeros((8, 128), I32)] * 3
        for h in range(16):
            here = high == h
            got = [jnp.where(here, pick(rq, h * 8 + v, low), got[v]) for v in range(3)]
        for v in range(3):
            x, y = unpack_pair(got[v])
            gf[pl.ds(tb * 64 + v, 8, stride=8), :] = x * down
            gf[pl.ds(tb * 64 + v + 3, 8, stride=8), :] = y * down
        return carry

    lax.fori_loop(0, 16, choose, 0, unroll=8)
    out[...] = gf[...].astype(BF)


def spread_kernel(
    flags, grad, cells, wts, cnt, out, out1, out2, l0, l1, r0, r1, total
):
    lefts, rights = (l0, l1), (r0, r1)
    steps = iotas(4)
    none = jnp.zeros((16, 128), BF)
    total[...] = jnp.zeros_like(total)
    lane = lax.broadcasted_iota(I32, (8, 128), 1)

    def owners(group, slot):
        for q in range(4):
            owners_eight(group * 4 + q, q * 4096, lefts[slot], rights[slot])

    def owners_eight(ob, start, left, right):
        rows = pl.ds(pl.multiple_of(ob * 8, 8), 8)
        live = lane < cnt[rows, 0:1]
        block = grad[pl.ds(pl.multiple_of(ob * 64, 64), 64), :].astype(F32)
        index = [cells[k, rows, :] for k in range(4)]
        low = [(i & 63).astype(F32) for i in index]
        high = [(i >> 6).astype(F32) for i in index]
        weight = [jnp.where(live, wts[k, rows, :], 0.0) for k in range(4)]
        for i in range(8):
            values = [spread_row(block[i * 8 + v : i * 8 + v + 1]) for v in range(6)]
            for k in range(4):
                at = slice(start + (i * 4 + k) * 128, start + (i * 4 + k) * 128 + 128)
                here = spread_row(high[k][i : i + 1]) == steps[0]
                for v in range(6):
                    left[v * 16 : v * 16 + 16, at] = jnp.where(here, values[v], none)
                mine = spread_row(low[k][i : i + 1])
                amount = spread_row(weight[k][i : i + 1])
                for m in range(4):
                    right[m * 16 : m * 16 + 16, at] = jnp.where(mine == steps[m], amount, none)

    def multiply(slot):
        total[...] += dot(lefts[slot][...], rights[slot][...], NT)

    overlapped(4, owners, multiply)
    out[...] = jnp.zeros_like(out)
    for r in range(8):
        even = total[pl.ds(2 * r, 6, stride=16), :]
        odd = total[pl.ds(2 * r + 1, 6, stride=16), :]
        out[r * 8 : r * 8 + 6, :] = jnp.concatenate([even, odd], 1)
    out1[...], out2[...] = ordered(flags[4], out[0:16, :], out[48:64, :])


def backward_kernel(
    flags, gf, et, swap1, swap2, fm, a1t, h0t, gp, h2c, c2, c1, small, loss, pay, gfields, es, bw,
    gs, g2cat, zs, gzcat, gc, w2, w1,
):
    zero8 = jnp.zeros((8, CP), F32)
    gs[0:8, :] = zero8
    gs[N12 + 8 : N12 + 16, :] = zero8
    zs[0:8, :] = zero8
    zs[N10 + 8 : N10 + 16, :] = zero8
    stack_weights(w2, c2, -1)
    stack_weights(w1, c1, -1)
    core = (flags[4] > 0).astype(I32)
    base_s = pl.multiple_of(core * HALF, 16)
    base_f = pl.multiple_of((1 - core) * HALF, 16)

    def put(base, at, value):
        pay[pl.ds(pl.multiple_of(base + at, 16), value.shape[0]), :] = value.astype(BF)

    def put_taps(base, turned):
        for a in range(3):
            y = dot(turned[:, a * 128 : a * 128 + 1024], gc[...])
            for b in range(3):
                tap = a * 3 + b
                mine = y[b * C : (b + 1) * C]
                put(base, tap * C, mine[:, 0:128])
                rest = mine[:, 128:256]
                put(base, REST + tap * 96, rest[0:96] + pltpu.roll(rest[96:192], 64, 1))

    es[...] = jnp.zeros_like(es)
    es[2:130, 0:96] = et[...]
    es[0:2, 0:96], es[130:132, 0:96] = ordered(flags[5], swap1[...], swap2[...])
    bw[...] = jnp.zeros_like(bw)
    for r in range(12):
        at, block = (r // 2) * 16, small[64 + 16 * (r % 2) : 80 + 16 * (r % 2), :]
        bw[at : at + 16, r * CP : (r + 1) * CP] = block
        bw[128 + at : 144 + at, r * CP : (r + 1) * CP] = block
    x = es[...]
    x_hi = x.astype(BF)
    x_lo = (x - x_hi.astype(F32)).astype(BF)
    both = jnp.concatenate([x_hi, x_lo], 1)
    for r in range(12):
        gs[8 + r * ROW : 8 + (r + 1) * ROW, :] = dot(both, bw[:, r * CP : (r + 1) * CP])
    for b in range(3):
        g2cat[:, b * CP : (b + 1) * CP] = gs[9 - b : 9 - b + N12, :].astype(BF)
    for r in range(8):
        at = 8 + (r + 2) * ROW + 2
        gc[r * 128 : r * 128 + 128, :] = gs[at : at + 128, :].astype(BF)
    put_taps(base_s, a1t)
    for part in range(5):
        at = part * 2 * ROW
        g = taps(g2cat, w2, at, 2 * ROW, -1)
        zs[8 + at : 8 + at + 2 * ROW, :] = g * gp[at : at + 2 * ROW, :].astype(F32)
    for b in range(3):
        gzcat[:, b * CP : (b + 1) * CP] = zs[9 - b : 9 - b + N10, :].astype(BF)
    for r in range(8):
        at = 8 + (r + 1) * ROW + 2
        gc[r * 128 : r * 128 + 128, :] = zs[at : at + 128, :].astype(BF)
    put_taps(base_f, h0t)
    for part in range(4):
        at = 8 + 2 * ROW + part * 2 * ROW
        gs[at : at + 2 * ROW, :] = gs[at : at + 2 * ROW, :] + taps(
            gzcat, w1, part * 2 * ROW, 2 * ROW, -1
        )
    for r in range(8):
        at = 8 + (r + 2) * ROW + 2
        gc[r * 128 : r * 128 + 128, :] = gs[at : at + 128, :].astype(BF)
    g_in = dot(fm[...], gc[...])
    g_fields = dot(small[0:64, :], gc[...], NT)
    for r in range(8):
        gfields[pl.ds(r, 64, stride=8), :] = g_fields[:, r * 128 : r * 128 + 128]
    line = jnp.concatenate([gf[r * 8 : r * 8 + 8, :] for r in range(8)], 1)
    line_hi = line.astype(BF).astype(F32)
    line2 = jnp.concatenate([line_hi, line - line_hi], 0).astype(BF)
    g_out = dot(line2, h2c[...])
    g_out = g_out[0:8] + g_out[8:16]
    put(base_s, EXTRA, g_in[:, 0:128])
    rest = g_in[:, 128:256]
    put(base_s, EXTRA + 64, rest[0:32] + pltpu.roll(rest[32:64], 64, 1))
    put(base_s, EXTRA + 96, jnp.zeros((HALF - EXTRA - 96, 128), F32))
    put(base_f, EXTRA, jnp.concatenate([g_out[:, 0:128], g_out[:, 128:256]], 0))
    put(base_f, EXTRA + 16, loss[...])
    put(base_f, EXTRA + 32, jnp.zeros((HALF - EXTRA - 32, 128), F32))


def unpack_kernel(flags, mine, other, second, first, g_in, g_out, loss):
    def unpack(source, kernel):
        for tap in range(9):
            a, b = tap // 3, tap % 3
            kernel[a, b, :, 0:128] = source[tap * C : (tap + 1) * C, :].astype(F32)
            rest = source[REST + tap * 96 : REST + tap * 96 + 96, :].astype(F32)
            kernel[a, b, 0:96, 128:C] = rest[:, 0:64]
            kernel[a, b, 96:C, 128:C] = pltpu.roll(rest, 64, 1)[:, 0:64]

    def both(s, f):
        unpack(s, second)
        unpack(f, first)
        g_in[:, 0:128] = s[EXTRA : EXTRA + 64, :].astype(F32)
        rest = s[EXTRA + 64 : EXTRA + 96, :].astype(F32)
        g_in[0:32, 128:C] = rest[:, 0:64]
        g_in[32:64, 128:C] = pltpu.roll(rest, 64, 1)[:, 0:64]
        extra = f[EXTRA : EXTRA + 32, :].astype(F32)
        g_out[:, 0:128] = extra[0:6]
        g_out[:, 128:C] = extra[8:14, 0:64]
        loss[0, 0] = jnp.max(extra[16:24])

    @pl.when(flags[4] == 0)
    def _():
        both(mine, other)

    @pl.when(flags[4] > 0)
    def _():
        both(other, mine)


def swaps(one, two, axis):
    count = lax.axis_size(axis)
    pairs = [[(i, i + 1) for i in range(start, count - 1, 2)] for start in range(2)]
    return tuple(
        lax.ppermute(x, axis, p + [(j, i) for i, j in p]) for x, p in zip((one, two), pairs)
    )


def exchange(rows, groups=None):
    return lax.all_to_all(
        rows, AXES, split_axis=0, concat_axis=0, tiled=True, axis_index_groups=groups
    )


def call(kernel, out_shapes, scratch, *operands, smem=0, smem_out=0, vmem=60, flops=0):
    vm, sm = pl.BlockSpec(memory_space=pltpu.VMEM), pl.BlockSpec(memory_space=pltpu.SMEM)
    return pl.pallas_call(
        kernel,
        out_shape=[jax.ShapeDtypeStruct(s, d) for s, d in out_shapes],
        in_specs=[sm] * smem + [vm] * (len(operands) - smem),
        out_specs=[vm] * (len(out_shapes) - smem_out) + [sm] * smem_out,
        scratch_shapes=[pltpu.VMEM(s, d) for s, d in scratch],
        compiler_params=pltpu.CompilerParams(vmem_limit_bytes=vmem * 1024 * 1024),
        cost_estimate=pl.CostEstimate(flops=flops, bytes_accessed=4_000_000, transcendentals=0),
    )(*operands)


def on_device(
    fields,
    w_in,
    conv_first,
    conv_second,
    w_out,
    slot_cells,
    slot_weights,
    slot_count,
    recv_obs,
    targets,
):
    ns, ew = lax.axis_index("ns"), lax.axis_index("ew")
    n_ns, n_ew = lax.axis_size("ns"), lax.axis_size("ew")
    flags = jnp.stack(
        [ns > 0, ns < n_ns - 1, ew > 0, ew < n_ew - 1, (ns & 1) > 0, (ew & 1) > 0]
    ).astype(F32)
    cells = slot_cells.reshape(4, 128, CAP)
    wts = slot_weights.reshape(4, 128, CAP)
    cnt = slot_count.reshape(128, 1)
    obs = recv_obs.reshape(128, CAP)
    turned = w_out.T
    small = jnp.concatenate(
        [w_in, jnp.pad(turned, ((0, 10), (0, 0))), jnp.pad(turned, ((8, 2), (0, 0)))], 0
    )
    small = jnp.pad(small, ((0, 0), (0, CP - C)))

    last, first = fields[:, 6:8].reshape(128, 128), fields[:, 0:2].reshape(128, 128)
    one, two = swaps(*ordered(ns & 1, first, last), "ns")
    fto, fm, own_west, own_east = call(
        own_kernel,
        [((1024, 64), BF), ((64, 1024), BF), ((16, 64), F32), ((16, 64), F32)],
        [((512, 128), F32)],
        fields.reshape(512, 128),
        vmem=8, flops=LONG,
    )
    ftr, one, two = call(
        rim_kernel,
        [((512, 64), BF), ((32, 64), BF), ((32, 64), BF)],
        [((128, 128), F32), ((128, 128), F32), ((32, 64), F32), ((32, 64), F32)],
        flags, one, two, own_west, own_east,
        smem=1, vmem=8, flops=LONG,
    )
    west, east = swaps(one, two, "ew")
    sent, a1, gp, h2c = call(
        forward_kernel,
        [((1024, 128), BF), ((N10, CP), BF), ((N10, CP), BF), ((1024, CP), BF)],
        [
            ((N12 + 16, CP), F32), ((N12, 3 * CP), BF), ((N10 + 16, CP), F32),
            ((N10, 3 * CP), BF), ((3, 3 * CP, CP), BF), ((3, 3 * CP, CP), BF),
            ((64, 128), I32), ((1024, 128), F32),
        ],
        flags, fto, ftr, west, east, small, conv_first, conv_second, cells, wts, cnt,
        smem=1, vmem=28, flops=2 * 10**9,
    )
    received = exchange(sent)
    a1t, h0t = call(
        turn_kernel,
        [((3 * C, 1280), BF), ((3 * C, 1280), BF)],
        [((N10, CP), F32), ((N12, 64), F32), ((1280, CP), BF), ((1280, 64), BF)],
        flags, a1, fto, ftr, west, east, small,
        smem=1, vmem=16, flops=10**9,
    )
    pred, loss, back = call(
        owner_kernel,
        [((6, 2048), F32), ((16, 128), F32), ((1024, 128), BF)],
        [
            ((96, 4096), BF), ((96, 4096), BF), ((128, 4096), BF), ((128, 4096), BF),
            ((96, 128), F32), ((128, 128), I32), ((1024, 128), F32),
        ],
        received, obs, targets,
        vmem=12, flops=10**9,
    )
    grads = exchange(back)
    g_field, one, two = call(
        spread_kernel,
        [((64, 128), F32), ((16, 128), F32), ((16, 128), F32)],
        [
            ((96, 16384), BF), ((96, 16384), BF), ((64, 16384), BF), ((64, 16384), BF),
            ((96, 64), F32),
        ],
        flags, grads, cells, wts, cnt,
        smem=1, vmem=20, flops=10**9,
    )
    one, two = swaps(one, two, "ns")
    et, one, two = call(
        turn_field_kernel,
        [((128, 96), F32), ((2, 96), F32), ((2, 96), F32)],
        [],
        flags, g_field, one, two,
        smem=1, vmem=4, flops=LONG,
    )
    one, two = swaps(one, two, "ew")
    pay, g_fields = call(
        backward_kernel,
        [((2 * HALF, 128), BF), ((512, 128), F32)],
        [
            ((ROW, 128), F32), ((CP, 12 * CP), BF), ((N12 + 16, CP), F32), ((N12, 3 * CP), BF),
            ((N10 + 16, CP), F32), ((N10, 3 * CP), BF), ((1024, CP), BF),
            ((3, CP, 3 * CP), BF), ((3, CP, 3 * CP), BF),
        ],
        flags, g_field, et, one, two, fm, a1t, h0t, gp, h2c, conv_second, conv_first, small, loss,
        smem=1, vmem=28, flops=2 * 10**9,
    )
    pairs = [(n, n ^ 1) for n in range(n_ns)]
    groups = [[n * n_ew + e for n in range(c, n_ns, 2) for e in range(n_ew)] for c in range(2)]
    theirs = lax.ppermute(pay[HALF:], "ns", pairs)
    summed = (pay[:HALF].astype(F32) + theirs.astype(F32)).astype(BF).reshape(64, PIECE, 128)
    share = jnp.sum(exchange(summed, groups).astype(F32), axis=0).astype(BF)
    mine = exchange(jnp.broadcast_to(share[None], (64, PIECE, 128)), groups).reshape(HALF, 128)
    other = lax.ppermute(mine, "ns", pairs)
    grad_second, grad_first, grad_in, g_out, total = call(
        unpack_kernel,
        [((3, 3, C, C), F32), ((3, 3, C, C), F32), ((64, C), F32), ((6, C), F32), ((1, 1), F32)],
        [],
        flags, mine, other,
        smem=1, smem_out=1, vmem=16,
    )
    return (
        pred,
        total[0, 0],
        grad_first,
        grad_second,
        grad_in,
        g_out.T,
        g_fields.reshape(64, TH, TW),
    )


def solution(mesh):
    in_specs = (
        P(None, "ns", "ew"),
        P(),
        P(),
        P(),
        P(),
        P(("ns", "ew"), None, None),
        P(("ns", "ew"), None, None),
        P(("ns", "ew"), None),
        P(("ns", "ew"), None),
        P(None, ("ns", "ew")),
    )
    out_specs = (P(None, ("ns", "ew")), P(), P(), P(), P(), P(), P(None, "ns", "ew"))
    return jax.shard_map(
        on_device, mesh=mesh, in_specs=in_specs, out_specs=out_specs, check_vma=False
    )
```
